128 devices in a mesh: ep: 32 (over x, y, core), tp: 4 (over z).
Axes of the slice: x: 4, y: 4, z: 4, core: 2. Of those that a mesh axis runs over, the one named last changes fastest.
Arguments:
- tokens: bfloat16 [6144, 2048], P('ep'), may hold values from -27 to 27
- expert_ids: int32 [6144, 6], P('ep'), may hold values from 0 to 63, as said below
- route_slots: int32 [6144, 6], P('ep'), may hold values from 0 to 35, as said below
- doc_ids: int32 [32, 192], P('ep'), may hold values from 0 to 11, never falling along the last dimension, each value on 1 to 144 neighbouring positions
- prenorm: bfloat16 [2048], P('ep'), may hold values from 0.5 to 1.5
- query_w: bfloat16 [2048, 3072], P('ep', 'tp'), may hold values from -0.125 to 0.125
- latent_w: bfloat16 [2048, 576], P('ep'), may hold values from -0.125 to 0.125
- latnorm: bfloat16 [512], P('ep'), may hold values from 0.5 to 1.5
- keyval_w: bfloat16 [512, 4096], P('ep', 'tp'), may hold values from -0.25 to 0.25
- output_w: bfloat16 [2048, 2048], P('tp', 'ep'), may hold values from -0.75 to 0.75
- midnorm: bfloat16 [2048], P('ep'), may hold values from 0.5 to 1.5
- router_w: bfloat16 [2048, 64], P('ep'), may hold values from -0.0625 to 0.0625
- shgate_w: bfloat16 [2048, 2816], P('ep', 'tp'), may hold values from -0.125 to 0.125
- shup_w: bfloat16 [2048, 2816], P('ep', 'tp'), may hold values from -0.125 to 0.125
- shdown_w: bfloat16 [2816, 2048], P('tp', 'ep'), may hold values from -0.109375 to 0.109375
- exgate_w: bfloat16 [64, 2048, 1408], P('ep', None, 'tp'), may hold values from -0.125 to 0.125
- exup_w: bfloat16 [64, 2048, 1408], P('ep', None, 'tp'), may hold values from -0.125 to 0.125
- exdown_w: bfloat16 [64, 1408, 2048], P('ep', 'tp'), may hold values from -0.15625 to 0.15625
- cotangent: bfloat16 [6144, 2048], P('ep'), may hold values from -6 to 6
Outputs:
- layer_out: bfloat16 [6144, 2048], P('ep')
- tokens_grad: bfloat16 [6144, 2048], P('ep')
- prenorm_grad: float32 [2048], P('ep')
- query_grad: float32 [2048, 3072], P('ep', 'tp')
- latent_grad: float32 [2048, 576], P('ep')
- latnorm_grad: float32 [512], P('ep')
- keyval_grad: float32 [512, 4096], P('ep', 'tp')
- output_grad: float32 [2048, 2048], P('tp', 'ep')
- midnorm_grad: float32 [2048], P('ep')
- router_grad: float32 [2048, 64], P('ep')
- shgate_grad: float32 [2048, 2816], P('ep', 'tp')
- shup_grad: float32 [2048, 2816], P('ep', 'tp')
- shdown_grad: float32 [2816, 2048], P('tp', 'ep')
- exgate_grad: float32 [64, 2048, 1408], P('ep', None, 'tp')
- exup_grad: float32 [64, 2048, 1408], P('ep', None, 'tp')
- exdown_grad: float32 [64, 1408, 2048], P('ep', 'tp')
The draws below stay inside these ranges and needn't reach their ends.
Inputs may be any that keep to these rules, and one draw needn't show every extreme that they name: `expert_ids`: the 6 experts of a token differ. Among the tokens of one aligned block of 192, at most 36 routes name one expert, and in every draw one expert is named by exactly 36 routes of every such block. `route_slots`: among the tokens of one aligned block of 192, the routes that name one expert have different slots.
All inputs are finite; a program needn't handle non-finite values.
Results may differ from the reference program's by a relative error of at most 0.03.
Values may be sent and summed in bfloat16 or wider, within the bound.
No kernel may reach another device: no remote copies, remote signals or barrier semaphores. Data moves between devices by JAX's collectives and lax.ppermute only.
A program may use at most 256 MiB of HBM per device.

```python
import math
import jax
import jax.numpy as jnp
import numpy as np
from jax import lax

D = 2048
H = 16
DN = 128
DR = 64
DV = 128
KVR = 512
FE = 1408
TOPK = 6
TOK_DEV = 192
FS = 2816
EXPERTS = 64
TOKENS = 6144
PACKS = 32
CAP = 36
N_TP = 4


def shuffled(key, row_count, length):
    noise_vals = jax.random.randint(key, (row_count, length), 0, 1 << 20)
    return jnp.argsort(noise_vals * length + jnp.arange(length, dtype=jnp.int32)[None, :], axis=1).astype(jnp.int32)


def route_table(key):
    blocks = TOKENS // TOK_DEV
    mean_load = TOK_DEV * TOPK // EXPERTS
    capacity = 2 * mean_load
    pair_key, heavy_key, label_key, slot_key, order_key = jax.random.split(key, 5)
    spread = jax.random.randint(pair_key, (blocks, EXPERTS // 2), 0, mean_load + 1)
    spread = spread.at[:, 0].set(mean_load)
    load_vals = jnp.stack([mean_load + spread, mean_load - spread], axis=2).reshape(blocks, EXPERTS)
    end_pos = jnp.cumsum(load_vals, axis=1)
    starts = end_pos - load_vals
    entry_pos = jnp.arange(TOK_DEV * TOPK, dtype=jnp.int32)
    run_index = jnp.sum((end_pos[:, None, :] <= entry_pos[None, :, None]).astype(jnp.int32), axis=2)
    within = entry_pos[None, :] - jnp.take_along_axis(starts, run_index, axis=1)
    heavy_expert = jax.random.randint(heavy_key, (), 0, EXPERTS)
    labels = shuffled(label_key, blocks, EXPERTS)
    first_label = labels[:, :1]
    labels = jnp.where(labels == heavy_expert, first_label, labels)
    labels = labels.at[:, 0].set(heavy_expert)
    expert_of = jnp.take_along_axis(labels, run_index, axis=1)
    slot_perm = shuffled(slot_key, blocks * EXPERTS, capacity).reshape(blocks, EXPERTS, capacity)
    slot_of = slot_perm[jnp.arange(blocks)[:, None], run_index, within]
    tok_perm = shuffled(order_key, blocks, TOK_DEV)
    expert_grid = expert_of.reshape(blocks, TOPK, TOK_DEV).transpose(0, 2, 1)
    slot_grid = slot_of.reshape(blocks, TOPK, TOK_DEV).transpose(0, 2, 1)
    expert_grid = jnp.take_along_axis(expert_grid, tok_perm[:, :, None], axis=1)
    slot_grid = jnp.take_along_axis(slot_grid, tok_perm[:, :, None], axis=1)
    return (expert_grid.reshape(TOKENS, TOPK).astype(jnp.int32), slot_grid.reshape(TOKENS, TOPK).astype(jnp.int32))


def draw_expert_ids(key, part):
    return route_table(key)[0]


def draw_route_slots(key, part):
    return route_table(key)[1]


def draw_tokens(key, part):
    key = jax.random.fold_in(key, 5)
    row_key, col_key, noise_key = jax.random.split(key, 3)
    row_scale = jnp.exp(jax.random.uniform(row_key, (TOKENS, 1), minval=math.log(0.3), maxval=math.log(3.0)))
    col_scale = jnp.exp(jax.random.uniform(col_key, (1, D), minval=math.log(0.3), maxval=math.log(3.0)))
    noise_vals = jax.random.normal(noise_key, (TOKENS, D))
    noise_vals = jnp.clip(noise_vals, -3.0, 3.0)
    return (noise_vals * row_scale * col_scale).astype(jnp.bfloat16)


def steps_of(own_key, shape, pieces, smallest, largest):
    level, own = 1.0, jax.random.fold_in(own_key, 6)
    for axis_at, shards_of in pieces:
        steps = jnp.exp(jax.random.uniform(jax.random.fold_in(own, axis_at), (shards_of,), jnp.float32, smallest / len(pieces), largest / len(pieces)))
        level = level * jnp.repeat(steps, shape[axis_at] // shards_of).reshape([-1 if axis == axis_at else 1 for axis in range(len(shape))])
    return level


def profile(number_of, total, most, lean):
    weights = [(1 << 20) // math.isqrt(rank ** lean) + 1 for rank in range(2, number_of + 1)]
    spare, counts = total - most - (number_of - 1), [1] * (number_of - 1)
    while spare > 0:
        free = [i for i in range(number_of - 1) if counts[i] < most]
        pool, budget = sum([weights[i] for i in free]), spare
        for i in free:
            more = min(most - counts[i], max(1, budget * weights[i] // pool), spare)
            counts[i] = counts[i] + more
            spare = spare - more
    return np.array([most] + counts)


def uneven(stream_key, count, total, most, slope):
    if count == 2:
        one = jax.random.randint(stream_key, (), max(1, total - most), min(most, total - 1) + 1)
        return jnp.stack([one, total - one])
    tallies = jnp.asarray(profile(count, total, most, slope), jnp.int32)
    couples = (count - 1) // 2
    giver, sink = tallies[1:1 + 2 * couples:2], tallies[2:2 + 2 * couples:2]
    margin = jnp.minimum(giver - 1, most - sink)
    passed = jax.random.randint(jax.random.fold_in(stream_key, 1), (couples,), 0, 1 << 20) % (margin + 1)
    tallies = tallies.at[1:1 + 2 * couples:2].set(giver - passed).at[2:2 + 2 * couples:2].set(sink + passed)
    return tallies[jax.random.permutation(jax.random.fold_in(stream_key, 2), count)]


def scatter_about(stream_key, dims, deviation, limit, shards=(), kind=jnp.bfloat16):
    gain = steps_of(stream_key, dims, shards, -0.22, 0.18) if shards else 1.0
    values = jax.random.normal(stream_key, dims, jnp.float32) * deviation * gain
    return jnp.minimum(jnp.maximum(values, -limit), limit).astype(kind)


def setup_inputs(seed: int = 0) -> dict:
    arg_keys = jax.random.split(jax.random.key(seed), 20)
    tokens = draw_tokens(jax.random.fold_in(arg_keys[19], 71), 0)
    expert_ids = draw_expert_ids(jax.random.fold_in(arg_keys[19], 71), 0)
    route_slots = draw_route_slots(jax.random.fold_in(arg_keys[19], 71), 0)
    doc_ids = jax.vmap(lambda own: jnp.searchsorted(jnp.cumsum(uneven(own, max(2, TOK_DEV // 16), TOK_DEV, 3 * TOK_DEV // 4, 2)), jnp.arange(TOK_DEV), side="right"))(jax.random.split(arg_keys[3], PACKS)).reshape((PACKS, TOK_DEV)).astype(jnp.int32)
    prenorm = jnp.clip(1.0 + 0.1 * jax.random.normal(arg_keys[4], (D,), jnp.float32), 0.5, 1.5).astype(jnp.bfloat16)
    query_w = scatter_about(arg_keys[5], (D, H * (DN + DR)), D ** -0.5, 0.125, ((0, 32), (1, 4)))
    latent_w = scatter_about(arg_keys[6], (D, KVR + DR), D ** -0.5, 0.125, ((0, 32),))
    latnorm = jnp.clip(1.0 + 0.1 * jax.random.normal(arg_keys[7], (KVR,), jnp.float32), 0.5, 1.5).astype(jnp.bfloat16)
    keyval_w = scatter_about(arg_keys[8], (KVR, H * (DN + DV)), KVR ** -0.5, 0.25, ((0, 32), (1, 4)))
    output_w = scatter_about(arg_keys[9], (H * DV, D), (H * DV // 32) ** -0.5, 0.75, ((0, 4), (1, 32)))
    midnorm = jnp.clip(1.0 + 0.1 * jax.random.normal(arg_keys[10], (D,), jnp.float32), 0.5, 1.5).astype(jnp.bfloat16)
    router_w = scatter_about(arg_keys[11], (D, EXPERTS), (4 * D) ** -0.5, 0.0625, ((0, 32),))
    shgate_w = scatter_about(arg_keys[12], (D, FS), D ** -0.5, 0.125, ((0, 32), (1, 4)))
    shup_w = scatter_about(arg_keys[13], (D, FS), D ** -0.5, 0.125, ((0, 32), (1, 4)))
    shdown_w = scatter_about(arg_keys[14], (FS, D), FS ** -0.5, 0.109375, ((0, 4), (1, 32)))
    exgate_w = scatter_about(arg_keys[15], (EXPERTS, D, FE), D ** -0.5, 0.125, ((0, 32), (2, 4)))
    exup_w = scatter_about(arg_keys[16], (EXPERTS, D, FE), D ** -0.5, 0.125, ((0, 32), (2, 4)))
    exdown_w = scatter_about(arg_keys[17], (EXPERTS, FE, D), FE ** -0.5, 0.15625, ((0, 32), (1, 4)))
    cotangent = scatter_about(arg_keys[18], (TOKENS, D), 1.0, 6.0, ((0, 32),))
    return {"tokens": tokens, "expert_ids": expert_ids, "route_slots": route_slots, "doc_ids": doc_ids, "prenorm": prenorm, "query_w": query_w, "latent_w": latent_w, "latnorm": latnorm, "keyval_w": keyval_w, "output_w": output_w, "midnorm": midnorm, "router_w": router_w, "shgate_w": shgate_w, "shup_w": shup_w, "shdown_w": shdown_w, "exgate_w": exgate_w, "exup_w": exup_w, "exdown_w": exdown_w, "cotangent": cotangent}


@jax.custom_vjp
def low(v):
    return lax.optimization_barrier(v.astype(jnp.bfloat16)).astype(jnp.float32)

@jax.custom_vjp
def low_back(v):
    return v

def low_keep(v):
    return (low(v), None)

def low_pass(kept, grad):
    return (grad,)

def back_keep(v):
    return (v, None)

def back_low(kept, grad):
    return (low(grad),)
low.defvjp(low_keep, low_pass)
low_back.defvjp(back_keep, back_low)
epsilon = 1e-06
route_scale = 2.446
rope_base = 50000.0
masked_fill = -1000000000.0
highest = lax.Precision.HIGHEST

def matmul(left_mat, right_mat):
    return jnp.dot(left_mat, right_mat, preferred_element_type=jnp.float32, precision=highest)

def silu(values):
    return values / (1.0 + jnp.exp(-values))

def rms_norm(values, gain_vec):
    return values * lax.rsqrt(lax.optimization_barrier(jnp.mean(values * values, -1, keepdims=True)) + epsilon) * gain_vec

def rope_tables(row_count):
    half_dim = DR // 2
    freq_vec = rope_base ** (-(jnp.arange(half_dim, dtype=jnp.float32) * (2.0 / DR)))
    angle_tab = jnp.arange(row_count, dtype=jnp.float32)[:, None] * freq_vec[None, :]
    return (jnp.cos(angle_tab), jnp.sin(angle_tab))

def rotate(values, cos_tab, sine_tab):
    half_dim = values.shape[-1] // 2
    first_half = values[..., :half_dim]
    second_half = values[..., half_dim:]
    return jnp.concatenate([first_half * cos_tab - second_half * sine_tab, second_half * cos_tab + first_half * sine_tab], -1)

def pack_attention(inputs):
    query_raw, rope_key, keyval, doc_row = inputs
    cos_tab, sine_tab = rope_tables(TOK_DEV)
    query_raw = query_raw.reshape(TOK_DEV, H, DN + DR)
    q_all = low(jnp.concatenate([query_raw[..., :DN], rotate(query_raw[..., DN:], cos_tab[:, None, :], sine_tab[:, None, :])], -1))
    key_rot = low(rotate(rope_key, cos_tab, sine_tab))
    keyval = keyval.reshape(TOK_DEV, H, DN + DV)
    key_all = jnp.concatenate([keyval[..., :DN], jnp.broadcast_to(key_rot[:, None, :], (TOK_DEV, H, DR))], -1)
    values = keyval[..., DN:]
    raw_scores = low_back(jnp.einsum('thd,shd->hts', q_all, key_all, precision=highest) * (DN + DR) ** (-0.5))
    position = jnp.arange(TOK_DEV)
    allowed = (doc_row[:, None] == doc_row[None, :]) & (position[:, None] >= position[None, :])
    masked = jnp.where(allowed[None], raw_scores, masked_fill)
    row_max = lax.optimization_barrier(jnp.max(masked, -1, keepdims=True))
    exp_scores = jnp.exp(masked - row_max)
    attn_probs = low(exp_scores / lax.optimization_barrier(jnp.sum(exp_scores, -1, keepdims=True)))
    attended = jnp.einsum('hts,shd->thd', attn_probs, values, precision=highest)
    return low_back(low(attended.reshape(TOK_DEV, H * DV)))

def layer(tokens, prenorm, query_w, latent_w, latnorm, keyval_w, output_w, midnorm, router_w, shgate_w, shup_w, shdown_w, exgate_w, exup_w, exdown_w, expert_ids, route_slots, doc_ids):
    pack_count = TOKENS // TOK_DEV
    normed = low(rms_norm(tokens, prenorm))
    query_raw = low_back(matmul(normed, query_w))
    latent_all = low_back(matmul(normed, latent_w))
    latent_n = low(rms_norm(latent_all[:, :KVR], latnorm))
    keyval = low_back(low(matmul(latent_n, keyval_w)))
    attended = lax.map(jax.checkpoint(pack_attention), (query_raw.reshape(pack_count, TOK_DEV, H * (DN + DR)), latent_all[:, KVR:].reshape(pack_count, TOK_DEV, DR), keyval.reshape(pack_count, TOK_DEV, H * (DN + DV)), doc_ids))
    attended = attended.reshape(TOKENS, H * DV)
    mid_resid = tokens + low_back(matmul(attended, output_w))
    normed2 = low(rms_norm(mid_resid, midnorm))
    logits = low_back(matmul(normed2, router_w))
    sel_vals = 1.0 / (1.0 + jnp.exp(-jnp.take_along_axis(logits, expert_ids, 1)))
    gate_vals = route_scale * sel_vals / lax.optimization_barrier(jnp.sum(sel_vals, -1, keepdims=True))
    sh_hidden = low(silu(low_back(matmul(normed2, shgate_w))) * low_back(matmul(normed2, shup_w)))
    shared_out = low_back(matmul(sh_hidden, shdown_w))
    route_id = jnp.arange(TOKENS * TOPK, dtype=jnp.int32)
    flat_place = expert_ids.reshape(-1) * (pack_count * CAP) + route_id // TOPK // TOK_DEV * CAP + route_slots.reshape(-1)
    inverse = jnp.full((EXPERTS * pack_count * CAP,), -1, jnp.int32).at[flat_place].set(route_id).reshape(EXPERTS, pack_count * CAP)
    lane_width = FE // N_TP

    def expert_block(inputs):
        index_table, gate_w, up_w, down_w = inputs
        filled = index_table >= 0
        row_block = jnp.where(filled[:, None], normed2[jnp.where(filled, index_table, 0) // TOPK], 0.0)
        row_block = low_back(row_block)
        total = jnp.zeros((row_block.shape[0], D), jnp.float32)
        for lane in range(N_TP):
            lane_rows = low_back(row_block)
            first = lane * lane_width
            gate_part = low_back(matmul(lane_rows, gate_w[:, first:first + lane_width]))
            up_part = low_back(matmul(lane_rows, up_w[:, first:first + lane_width]))
            hidden = low(silu(gate_part) * up_part)
            total = total + low(matmul(hidden, down_w[first:first + lane_width]))
        return low_back(low(total))
    outputs = lax.map(jax.checkpoint(expert_block), (inverse, exgate_w, exup_w, exdown_w))
    picked = outputs.reshape(EXPERTS * pack_count * CAP, D)[flat_place].reshape(TOKENS, TOPK, D)
    routed = lax.optimization_barrier(jnp.sum(picked * gate_vals[:, :, None], 1))
    return mid_resid + routed + shared_out

def reference(tokens, expert_ids, route_slots, doc_ids, prenorm, query_w, latent_w, latnorm, keyval_w, output_w, midnorm, router_w, shgate_w, shup_w, shdown_w, exgate_w, exup_w, exdown_w, cotangent):
    floats = [array_item.astype(jnp.float32) for array_item in (tokens, prenorm, query_w, latent_w, latnorm, keyval_w, output_w, midnorm, router_w, shgate_w, shup_w, shdown_w, exgate_w, exup_w, exdown_w)]

    def forward(*weights):
        return layer(*weights, expert_ids, route_slots, doc_ids)
    result, pullback = jax.vjp(forward, *floats)
    grad_list = pullback(cotangent.astype(jnp.float32))
    return (result.astype(jnp.bfloat16), grad_list[0].astype(jnp.bfloat16), grad_list[1], grad_list[2], grad_list[3], grad_list[4], grad_list[5], grad_list[6], grad_list[7], grad_list[8], grad_list[9], grad_list[10], grad_list[11], grad_list[12], grad_list[13], grad_list[14])
```

```python
import jax
import jax.numpy as jnp
from jax import lax
from jax.sharding import PartitionSpec as P

D = 2048
DN = 128
DR = 64
DV = 128
KVR = 512
TOPK = 6
EXP_DEV = 2
MAIN = 32

epsilon = 1e-06
route_scale = 2.446
rope_base = 50000.0
masked_fill = -1000000000.0

bf16 = jnp.bfloat16
f32 = jnp.float32


def matmul(left_mat, right_mat):
    return jnp.dot(left_mat, right_mat, preferred_element_type=f32)


def matmul_nt(left_mat, right_mat):
    return lax.dot_general(
        left_mat, right_mat, (((1,), (1,)), ((), ())), preferred_element_type=f32
    )


def matmul_tn(left_mat, right_mat):
    return lax.dot_general(
        left_mat, right_mat, (((0,), (0,)), ((), ())), preferred_element_type=f32
    )


def rms_scale(values):
    return lax.rsqrt(jnp.mean(values * values, -1, keepdims=True) + epsilon)


def rms_back(values, scale_vals, gain_vec, upstream):
    weighted = upstream * gain_vec
    inner_mean = jnp.mean(weighted * values, -1, keepdims=True)
    grad_in = scale_vals * weighted - values * scale_vals * scale_vals * scale_vals * inner_mean
    grad_gain = jnp.sum(upstream * values * scale_vals, 0)
    return (grad_in, grad_gain)


def rope_tables(row_count):
    half_dim = DR // 2
    freq_vec = rope_base ** (-(jnp.arange(half_dim, dtype=f32) * (2.0 / DR)))
    angle_tab = jnp.arange(row_count, dtype=f32)[:, None] * freq_vec[None, :]
    return (jnp.cos(angle_tab), jnp.sin(angle_tab))


def rotate(values, cos_tab, sine_tab):
    half_dim = values.shape[-1] // 2
    first_half = values[..., :half_dim]
    second_half = values[..., half_dim:]
    return jnp.concatenate(
        [
            first_half * cos_tab - second_half * sine_tab,
            second_half * cos_tab + first_half * sine_tab,
        ],
        -1,
    )


def shift(value, step):
    lanes = lax.axis_size("tp")
    return lax.ppermute(value, "tp", [(i, (i + step) % lanes) for i in range(lanes)])


def quarter_of(value, step):
    lanes = lax.axis_size("tp")
    width = value.shape[1] // lanes
    lane = lax.rem(lax.axis_index("tp") + step, lanes)
    return lax.dynamic_slice_in_dim(value, lane * width, width, 1)


def sum_to_quarter(partial):
    low = partial.astype(bf16)
    total = quarter_of(low, 0).astype(f32)
    for step in (1, 3, 2):
        total = total + shift(quarter_of(low, step), step).astype(f32)
    return total


def gather_quarters(piece):
    return lax.all_gather(piece, "tp", axis=1, tiled=True)


def sum_small(partial):
    total = partial.astype(f32)
    for step in (1, 3, 2):
        total = total + shift(partial, step).astype(f32)
    return total


def exchange(value):
    return lax.all_to_all(value, "ep", 0, 0, tiled=True)


def to_experts(value):
    blocks = value.shape[0]
    rest = value.shape[2:]
    return jnp.concatenate(
        [
            value[:, :MAIN].reshape(blocks * MAIN, *rest),
            value[:, MAIN:-MAIN].reshape(-1, *rest),
            value[:, -MAIN:].reshape(blocks * MAIN, *rest),
        ],
        0,
    )


def from_experts(value, blocks):
    rest = value.shape[1:]
    edge = blocks * MAIN
    return jnp.concatenate(
        [
            value[:edge].reshape(blocks, MAIN, *rest),
            value[edge:-edge].reshape(blocks, -1, *rest),
            value[-edge:].reshape(blocks, MAIN, *rest),
        ],
        1,
    )


def lanes_gather(piece):
    half = piece.shape[0] // 2
    width = piece.shape[1]
    lane = lax.axis_index("tp")
    lanes = lax.axis_size("tp")
    from_prev = shift(piece, 1)
    from_next = shift(piece, 3)
    far_top = shift(from_prev[:half], 1)
    far_bottom = shift(from_next[half:], 3)
    full = jnp.zeros((piece.shape[0], width * lanes), piece.dtype)
    for part, row, step in (
        (piece, 0, 0),
        (from_next, 0, 1),
        (from_prev, 0, 3),
        (far_top, 0, 2),
        (far_bottom, half, 2),
    ):
        place = lax.rem(lane + step, lanes) * width
        full = lax.dynamic_update_slice(full, part, (row, place))
    return full


def lanes_sum(parts):
    own, after, far, before = parts
    half = own.shape[0] // 2
    top = shift(far[:half], 1)
    bottom = shift(far[half:], 3)

    def plus(one, two):
        return (one.astype(f32) + two.astype(f32)).astype(bf16)

    from_prev = shift(jnp.concatenate([plus(after[:half], top), after[half:]], 0), 1)
    from_next = shift(jnp.concatenate([before[:half], plus(before[half:], bottom)], 0), 3)
    return (own.astype(f32) + from_prev.astype(f32) + from_next.astype(f32)).astype(bf16)


def per_device(
    tokens,
    expert_ids,
    route_slots,
    doc_ids,
    prenorm,
    query_w,
    latent_w,
    latnorm,
    keyval_w,
    output_w,
    midnorm,
    router_w,
    shgate_w,
    shup_w,
    shdown_w,
    exgate_w,
    exup_w,
    exdown_w,
    cotangent,
):
    owner_count = lax.axis_size("ep")
    experts = owner_count * EXP_DEV
    tok_count = tokens.shape[0]
    capacity = 2 * tok_count * TOPK // experts
    spill = capacity - MAIN
    width = EXP_DEV * capacity
    slot_rows = owner_count * width
    head_count = query_w.shape[1] // (DN + DR)
    score_scale = (DN + DR) ** (-0.5)
    shard = query_w.shape[0]
    q_cols = query_w.shape[1]
    lat_cols = latent_w.shape[1]
    kv_cols = keyval_w.shape[0] * keyval_w.shape[1] // shard
    out_cols = output_w.shape[0]
    sh_cols = shgate_w.shape[1]

    gains = jnp.stack(
        [prenorm, jnp.pad(latnorm, (0, shard - latnorm.shape[0])), midnorm], 1
    )
    gains = jnp.pad(gains, ((0, 0), (0, 128 - gains.shape[1])))
    first_pack = jnp.concatenate(
        [query_w, latent_w, router_w, keyval_w.reshape(shard, kv_cols), output_w.T, gains], 1
    )
    first_full = lax.all_gather(first_pack, "ep", axis=0, tiled=True)
    edges = [0]
    for cols in (q_cols, lat_cols, experts, kv_cols, out_cols, 128):
        edges.append(edges[-1] + cols)
    query_full = first_full[:, edges[0] : edges[1]]
    latent_full = first_full[:, edges[1] : edges[2]]
    router_full = first_full[:, edges[2] : edges[3]]
    keyval_full = first_full[:, edges[3] : edges[4]].reshape(KVR, keyval_w.shape[1])
    output_t = first_full[:, edges[4] : edges[5]]
    pre_gain = first_full[:, edges[5]]
    lat_gain = first_full[:, edges[5] + 1].reshape(owner_count, shard)[:, : latnorm.shape[0]]
    lat_gain = lat_gain.reshape(KVR)
    mid_gain = first_full[:, edges[5] + 2]

    local = expert_ids % EXP_DEV
    inside = jnp.where(
        route_slots < MAIN,
        local * (MAIN + EXP_DEV * spill) + route_slots,
        MAIN + local * spill + (route_slots - MAIN),
    )
    place = (expert_ids // EXP_DEV) * width + inside
    row_iota = lax.broadcasted_iota(jnp.int32, (slot_rows, tok_count), 0)
    matches = [row_iota == place[:, k][None, :] for k in range(TOPK)]
    pick = matches[0]
    for k in range(1, TOPK):
        pick = pick | matches[k]
    pick = pick.astype(bf16)
    token_iota = lax.broadcasted_iota(jnp.int32, (slot_rows, tok_count), 1)
    table = jnp.sum(jnp.where(pick > 0, token_iota + 1, 0), 1).astype(jnp.int32) - 1
    table = exchange(table.reshape(owner_count, width))

    upstream_all, first_full_ = lax.optimization_barrier((cotangent, first_full))
    dy_all = lax.all_gather(upstream_all, "ep", axis=0, tiled=True)
    dy_all = dy_all.reshape(owner_count, tok_count, D)
    second_pack = jnp.concatenate([shgate_w, shup_w, shdown_w.T], 1)
    second_pack, dy_all = lax.optimization_barrier((second_pack, dy_all))
    second_full = lax.all_gather(second_pack, "ep", axis=0, tiled=True)
    gateup_full = second_full[:, : 2 * sh_cols]
    shdown_t = second_full[:, 2 * sh_cols :]

    resid_in = tokens.astype(f32)
    pre_scale = rms_scale(resid_in)
    pre_weight = pre_gain.astype(f32)
    normed = (resid_in * pre_scale * pre_weight).astype(bf16)
    query_raw = matmul(normed, query_full).reshape(tok_count, head_count, DN + DR)
    latent_all = matmul(normed, latent_full)
    latent = latent_all[:, :KVR]
    lat_scale = rms_scale(latent)
    lat_weight = lat_gain.astype(f32)
    latent_n = (latent * lat_scale * lat_weight).astype(bf16)
    keyval = matmul(latent_n, keyval_full).astype(bf16).reshape(tok_count, head_count, DN + DV)
    cos_tab, sine_tab = rope_tables(tok_count)
    q_all = jnp.concatenate(
        [
            query_raw[..., :DN],
            rotate(query_raw[..., DN:], cos_tab[:, None, :], sine_tab[:, None, :]),
        ],
        -1,
    ).astype(bf16)
    key_rot = rotate(latent_all[:, KVR:], cos_tab, sine_tab).astype(bf16)
    key_all = jnp.concatenate(
        [keyval[..., :DN], jnp.broadcast_to(key_rot[:, None, :], (tok_count, head_count, DR))], -1
    )
    values = keyval[..., DN:]
    position = jnp.arange(tok_count)
    doc_row = doc_ids[0]
    allowed = ((doc_row[:, None] == doc_row[None, :]) & (position[:, None] >= position[None, :]))[
        None
    ]
    raw_scores = (
        jnp.einsum("thd,shd->hts", q_all, key_all, preferred_element_type=f32) * score_scale
    )
    masked = jnp.where(allowed, raw_scores, masked_fill)
    row_max = jnp.max(masked, -1, keepdims=True)
    exp_scores = jnp.exp(masked - row_max)
    softmax_sum = jnp.sum(exp_scores, -1, keepdims=True)
    probs = exp_scores / softmax_sum
    probs16 = probs.astype(bf16)
    attended = jnp.einsum("hts,shd->thd", probs16, values, preferred_element_type=f32)
    attended = attended.reshape(tok_count, head_count * DV).astype(bf16)
    attn_sum = gather_quarters(sum_to_quarter(matmul_nt(attended, output_t)).astype(bf16))
    mid_resid = resid_in + attn_sum.astype(f32)
    mid_scale = rms_scale(mid_resid)
    mid_weight = mid_gain.astype(f32)
    normed2 = (mid_resid * mid_scale * mid_weight).astype(bf16)

    sent = matmul(pick, quarter_of(normed2, 0)).astype(bf16)
    arrived = to_experts(exchange(sent.reshape(owner_count, width, -1)))
    rows = lanes_gather(arrived)

    logits = matmul(normed2, router_full)
    onehot = (
        expert_ids[:, :, None] == jnp.arange(experts, dtype=jnp.int32)[None, None, :]
    ).astype(f32)
    chosen = jnp.sum(onehot * logits[:, None, :], -1)
    sel_vals = 1.0 / (1.0 + jnp.exp(-chosen))
    sel_total = jnp.sum(sel_vals, -1, keepdims=True)
    gate_vals = route_scale * sel_vals / sel_total
    gate_rows = jnp.zeros((slot_rows, tok_count), f32)
    for k in range(TOPK):
        gate_rows = gate_rows + jnp.where(matches[k], gate_vals[:, k][None, :], 0.0)
    gate_rows = jnp.sum(gate_rows, 1).reshape(owner_count, width)
    gate_rows = to_experts(exchange(gate_rows))[:, None]

    upstream = cotangent.astype(f32)
    sh_both = matmul(normed2, gateup_full)
    sh_gate = sh_both[:, :sh_cols]
    sh_up = sh_both[:, sh_cols:]
    sh_sig = 1.0 / (1.0 + jnp.exp(-sh_gate))
    sh_hidden = (sh_gate * sh_sig * sh_up).astype(bf16)
    shared_q = sum_to_quarter(matmul_nt(sh_hidden, shdown_t))
    sh_dhidden = matmul(cotangent, shdown_t)
    sh_dgate = (sh_dhidden * sh_up * sh_sig * (1.0 + sh_gate * (1.0 - sh_sig))).astype(bf16)
    sh_dup = (sh_dhidden * sh_gate * sh_sig).astype(bf16)
    sh_dboth = jnp.concatenate([sh_dgate, sh_dup], 1)
    sh_dnormed_q = sum_to_quarter(matmul_nt(sh_dboth, gateup_full))
    second_grad = jnp.concatenate(
        [matmul_tn(normed2, sh_dboth).astype(bf16), matmul_tn(cotangent, sh_hidden).astype(bf16)],
        1,
    )
    second_sum = lax.psum_scatter(second_grad, "ep", scatter_dimension=0, tiled=True)

    pick_in = (
        table[:, :, None] == lax.broadcasted_iota(jnp.int32, (owner_count, width, tok_count), 2)
    ).astype(bf16)
    dy_rows = jnp.einsum("ist,itd->isd", pick_in, dy_all, preferred_element_type=f32)
    dy_rows = to_experts(dy_rows.astype(bf16))
    edge = owner_count * MAIN
    extra = slot_rows - 2 * edge
    span = edge + extra
    extra_iota = lax.broadcasted_iota(jnp.int32, (span, 1), 0)
    owned = (
        (extra_iota < edge) | ((extra_iota - edge) % (EXP_DEV * spill) < spill),
        (extra_iota >= extra) | (extra_iota % (EXP_DEV * spill) >= spill),
    )

    def join(first, second):
        return jnp.concatenate([first[:edge], first[edge:] + second[:extra], second[extra:]], 0)

    outs, drows, dgates = [], [], []
    exgate_grad, exup_grad, exdown_grad = [], [], []
    for e in range(EXP_DEV):
        at = slice(0, span) if e == 0 else slice(edge, slot_rows)
        e_rows, e_dy, e_gate = rows[at], dy_rows[at], gate_rows[at]
        ex_gate = matmul(e_rows, exgate_w[e])
        ex_up = matmul(e_rows, exup_w[e])
        ex_sig = 1.0 / (1.0 + jnp.exp(-ex_gate))
        ex_hidden = jnp.where(owned[e], ex_gate * ex_sig * ex_up, 0.0).astype(bf16)
        outs.append(matmul(ex_hidden, exdown_w[e]) * e_gate)
        ex_dh = matmul_nt(e_dy, exdown_w[e])
        dgates.append(jnp.sum(ex_hidden.astype(f32) * ex_dh, 1))
        ex_dh = jnp.where(owned[e], ex_dh * e_gate, 0.0)
        ex_dgate = (ex_dh * ex_up * ex_sig * (1.0 + ex_gate * (1.0 - ex_sig))).astype(bf16)
        ex_dup = (ex_dh * ex_gate * ex_sig).astype(bf16)
        drows.append(matmul_nt(ex_dgate, exgate_w[e]) + matmul_nt(ex_dup, exup_w[e]))
        exgate_grad.append(matmul_tn(e_rows, ex_dgate))
        exup_grad.append(matmul_tn(e_rows, ex_dup))
        exdown_grad.append(
            matmul_tn((ex_hidden.astype(f32) * e_gate).astype(bf16), e_dy)
        )
    out_rows = join(*outs).astype(bf16)
    drow_rows = join(*drows).astype(bf16)
    dgate_rows = exchange(from_experts(join(*dgates), owner_count)).reshape(-1)

    def give_back(value):
        summed = lanes_sum([quarter_of(value, step) for step in range(4)])
        back = exchange(from_experts(summed, owner_count)).reshape(slot_rows, -1)
        return matmul_tn(pick, back)

    routed_grad_q = give_back(drow_rows)
    routed_q = give_back(out_rows)
    layer_q = (quarter_of(mid_resid, 0) + routed_q + shared_q).astype(bf16)
    layer_out = gather_quarters(layer_q)

    dgate_part = jnp.stack(
        [jnp.sum(jnp.where(matches[k], dgate_rows[:, None], 0.0), 0) for k in range(TOPK)], 1
    )
    dgate_all = sum_small(dgate_part)
    weighted = jnp.sum(dgate_all * gate_vals, -1, keepdims=True) / route_scale
    dsel_vals = route_scale / sel_total * (dgate_all - weighted)
    dchosen = dsel_vals * sel_vals * (1.0 - sel_vals)
    dlogits = jnp.sum(onehot * dchosen[:, :, None], 1).astype(bf16)
    router_grad = matmul_tn(normed2, dlogits)
    dnormed2 = gather_quarters((routed_grad_q + sh_dnormed_q).astype(bf16)).astype(f32)
    dnormed2 = dnormed2 + matmul_nt(dlogits, router_full)
    dmid_norm, midnorm_grad = rms_back(mid_resid, mid_scale, mid_weight, dnormed2)
    dmid = upstream + dmid_norm
    dmid16 = dmid.astype(bf16)
    output_grad_t = matmul_tn(dmid16, attended)
    dattended = matmul(dmid16, output_t).astype(bf16).reshape(tok_count, head_count, DV)
    dprobs = jnp.einsum("thd,shd->hts", dattended, values, preferred_element_type=f32)
    dscores = (probs * (dprobs - jnp.sum(probs * dprobs, -1, keepdims=True))).astype(bf16)
    dq_all = (
        jnp.einsum("hts,shd->thd", dscores, key_all, preferred_element_type=f32) * score_scale
    )
    dkey_all = jnp.einsum("hts,thd->shd", dscores, q_all, preferred_element_type=f32) * score_scale
    dvalues = jnp.einsum("hts,thd->shd", probs16, dattended, preferred_element_type=f32)
    dquery = jnp.concatenate(
        [dq_all[..., :DN], rotate(dq_all[..., DN:], cos_tab[:, None, :], -sine_tab[:, None, :])], -1
    )
    dquery = dquery.reshape(tok_count, head_count * (DN + DR)).astype(bf16)
    dkeyval = (
        jnp.concatenate([dkey_all[..., :DN], dvalues], -1)
        .reshape(tok_count, head_count * (DN + DV))
        .astype(bf16)
    )
    keyval_grad = matmul_tn(latent_n, dkeyval)
    dlatent_part = matmul_nt(dkeyval, keyval_full)
    dkey_part = jnp.sum(dkey_all[..., DN:], 1)
    dlat_sum = sum_small(jnp.concatenate([dlatent_part, dkey_part], 1).astype(bf16))
    dnormed_q = sum_to_quarter(matmul_nt(dquery, query_full))
    dlatent, latnorm_grad = rms_back(latent, lat_scale, lat_weight, dlat_sum[:, :KVR])
    dlatent_all = jnp.concatenate(
        [dlatent, rotate(dlat_sum[:, KVR:], cos_tab, -sine_tab)], -1
    ).astype(bf16)
    dnormed = gather_quarters(dnormed_q.astype(bf16)).astype(f32) + matmul_nt(
        dlatent_all, latent_full
    )
    dtokens, prenorm_grad = rms_back(resid_in, pre_scale, pre_weight, dnormed)
    tokens_grad = (dmid + dtokens).astype(bf16)
    gain_grads = jnp.stack(
        [
            prenorm_grad,
            jnp.pad(
                latnorm_grad.reshape(owner_count, -1),
                ((0, 0), (0, shard - latnorm.shape[0])),
            ).reshape(-1),
            midnorm_grad,
        ],
        1,
    )
    gain_grads = jnp.pad(gain_grads, ((0, 0), (0, 128 - gain_grads.shape[1])))
    first_grad = jnp.concatenate(
        [
            matmul_tn(normed, dquery).astype(bf16),
            matmul_tn(normed, dlatent_all).astype(bf16),
            router_grad.astype(bf16),
            keyval_grad.astype(bf16).reshape(D, kv_cols),
            output_grad_t.astype(bf16),
            gain_grads.astype(bf16),
        ],
        1,
    )
    first_sum = lax.psum_scatter(first_grad, "ep", scatter_dimension=0, tiled=True).astype(f32)
    second_sum = second_sum.astype(f32)
    return (
        layer_out,
        tokens_grad,
        first_sum[:, edges[5]],
        first_sum[:, edges[0] : edges[1]],
        first_sum[:, edges[1] : edges[2]],
        first_sum[: latnorm.shape[0], edges[5] + 1],
        first_sum[:, edges[3] : edges[4]].reshape(keyval_w.shape),
        first_sum[:, edges[4] : edges[5]].T,
        first_sum[:, edges[5] + 2],
        first_sum[:, edges[2] : edges[3]],
        second_sum[:, :sh_cols],
        second_sum[:, sh_cols : 2 * sh_cols],
        second_sum[:, 2 * sh_cols :].T,
        jnp.stack(exgate_grad),
        jnp.stack(exup_grad),
        jnp.stack(exdown_grad),
    )


def solution(mesh):
    in_specs = (
        P("ep", None),
        P("ep", None),
        P("ep", None),
        P("ep", None),
        P("ep"),
        P("ep", "tp"),
        P("ep", None),
        P("ep"),
        P("ep", "tp"),
        P("tp", "ep"),
        P("ep"),
        P("ep", None),
        P("ep", "tp"),
        P("ep", "tp"),
        P("tp", "ep"),
        P("ep", None, "tp"),
        P("ep", None, "tp"),
        P("ep", "tp", None),
        P("ep", None),
    )
    out_specs = (
        P("ep", None),
        P("ep", None),
        P("ep"),
        P("ep", "tp"),
        P("ep", None),
        P("ep"),
        P("ep", "tp"),
        P("tp", "ep"),
        P("ep"),
        P("ep", None),
        P("ep", "tp"),
        P("ep", "tp"),
        P("tp", "ep"),
        P("ep", None, "tp"),
        P("ep", None, "tp"),
        P("ep", "tp", None),
    )
    return jax.shard_map(
        per_device, mesh=mesh, in_specs=in_specs, out_specs=out_specs, check_vma=False
    )
```

```python
import functools

import jax
import jax.numpy as jnp
from jax import lax
from jax.experimental import pallas as pl
from jax.experimental.pallas import tpu as pltpu
from jax.sharding import PartitionSpec as P

D = 2048
DN = 128
DR = 64
DV = 128
KVR = 512
TOPK = 6
EXP_DEV = 2
MAIN = 32

epsilon = 1e-06
route_scale = 2.446
rope_base = 50000.0
masked_fill = -1000000000.0

bf16 = jnp.bfloat16
f32 = jnp.float32


def matmul(left_mat, right_mat):
    return jnp.dot(left_mat, right_mat, preferred_element_type=f32)


def matmul_nt(left_mat, right_mat):
    return lax.dot_general(
        left_mat, right_mat, (((1,), (1,)), ((), ())), preferred_element_type=f32
    )


def matmul_tn(left_mat, right_mat):
    return lax.dot_general(
        left_mat, right_mat, (((0,), (0,)), ((), ())), preferred_element_type=f32
    )


def rms_scale(values):
    return lax.rsqrt(jnp.mean(values * values, -1, keepdims=True) + epsilon)


def rms_back(values, scale_vals, gain_vec, upstream):
    weighted = upstream * gain_vec
    inner_mean = jnp.mean(weighted * values, -1, keepdims=True)
    grad_in = scale_vals * weighted - values * scale_vals * scale_vals * scale_vals * inner_mean
    grad_gain = jnp.sum(upstream * values * scale_vals, 0)
    return (grad_in, grad_gain)


def rope_tables(row_count):
    half_dim = DR // 2
    freq_vec = rope_base ** (-(jnp.arange(half_dim, dtype=f32) * (2.0 / DR)))
    angle_tab = jnp.arange(row_count, dtype=f32)[:, None] * freq_vec[None, :]
    return (jnp.cos(angle_tab), jnp.sin(angle_tab))


def rotate(values, cos_tab, sine_tab):
    half_dim = values.shape[-1] // 2
    first_half = values[..., :half_dim]
    second_half = values[..., half_dim:]
    return jnp.concatenate(
        [
            first_half * cos_tab - second_half * sine_tab,
            second_half * cos_tab + first_half * sine_tab,
        ],
        -1,
    )


def shift(value, step):
    lanes = lax.axis_size("tp")
    return lax.ppermute(value, "tp", [(i, (i + step) % lanes) for i in range(lanes)])


def quarter_of(value, step):
    lanes = lax.axis_size("tp")
    width = value.shape[1] // lanes
    lane = lax.rem(lax.axis_index("tp") + step, lanes)
    return lax.dynamic_slice_in_dim(value, lane * width, width, 1)


def sum_to_quarter(partial):
    low = partial.astype(bf16)
    total = quarter_of(low, 0).astype(f32)
    for step in (1, 3, 2):
        total = total + shift(quarter_of(low, step), step).astype(f32)
    return total


def gather_quarters(piece):
    lanes = lax.axis_size("tp")
    lane = lax.axis_index("tp")
    parts = [piece] + [None] * (lanes - 1)
    for step in (1, 3, 2):
        parts[step] = shift(piece, lanes - step)
    full = jnp.concatenate(parts, 1)
    width = piece.shape[1]
    parts = []
    for step in range(lanes):
        at = lax.rem(lanes - lane + step, lanes) * width
        parts.append(lax.dynamic_slice_in_dim(full, at, width, 1))
    return jnp.concatenate(parts, 1)


def sum_small(partial):
    total = partial.astype(f32)
    for step in (1, 3, 2):
        total = total + shift(partial, step).astype(f32)
    return total


def exchange(value):
    return lax.all_to_all(value, "ep", 0, 0, tiled=True)


def to_experts(value):
    blocks = value.shape[0]
    rest = value.shape[2:]
    return jnp.concatenate(
        [
            value[:, :MAIN].reshape(blocks * MAIN, *rest),
            value[:, MAIN:-MAIN].reshape(-1, *rest),
            value[:, -MAIN:].reshape(blocks * MAIN, *rest),
        ],
        0,
    )


def from_experts(value, blocks):
    rest = value.shape[1:]
    edge = blocks * MAIN
    return jnp.concatenate(
        [
            value[:edge].reshape(blocks, MAIN, *rest),
            value[edge:-edge].reshape(blocks, -1, *rest),
            value[-edge:].reshape(blocks, MAIN, *rest),
        ],
        1,
    )


def after(value, *others):
    return lax.optimization_barrier((value, others))[0]


def plus(one, two):
    return (one.astype(f32) + two.astype(f32)).astype(bf16)


def ring_gather_first(one, two):
    return shift(one, 1), shift(two, 3), shift(two, 1), shift(one, 3)


def ring_gather_second(first):
    return shift(first[0], 1), shift(first[1], 3)


def ring_gather_parts(one, two, first, second):
    one_prev, two_next, two_prev, one_next = first
    return (one, two, one_next, two_next, second[0], second[1], one_prev, two_prev)


def ring_sum_first(far, others):
    return shift(far[0], 1), shift(far[1], 3), shift(others[4], 3), shift(others[3], 1)


def ring_sum_second(first, others):
    return shift(plus(others[2], first[0]), 1), shift(plus(others[5], first[1]), 3)


def add_three(one, two, three):
    return (one.astype(f32) + two.astype(f32) + three.astype(f32)).astype(bf16)


VMEM_BYTES = 44 * 1024 * 1024


def first_owner_rows(tiles, tile, spill):
    row = lax.broadcasted_iota(jnp.int32, (tile, 1), 0) + (pl.program_id(0) - tiles[0]) * tile
    return lax.rem(row, EXP_DEV * spill) < spill


def per_owner(tiles, tile, spill, run):
    first, mixed = tiles
    step = pl.program_id(0)
    mine = first_owner_rows(tiles, tile, spill)
    is_mixed = (step >= first) & (step < first + mixed)

    @pl.when(is_mixed)
    def _():
        run(None, mine)

    @pl.when(jnp.logical_not(is_mixed))
    def _():
        run(jnp.where(step < first, 0, 1), None)


def hidden_back_kernel(tiles, spill, *refs):
    pieces, weight, out = refs[:-2], refs[-2], refs[-1]
    rows = jnp.concatenate([p[...] for p in pieces], 1)

    def run(owner, mine):
        if owner is None:
            out[...] = jnp.where(mine, matmul_nt(rows, weight[0]), matmul_nt(rows, weight[1]))
        else:
            out[...] = matmul_nt(rows, weight[owner])

    per_owner(tiles, rows.shape[0], spill, run)


def hidden_kernel(tiles, spill, *refs):
    pieces, (weight, dh_ref, gate_ref, hid, dboth, dgate, acc) = refs[:8], refs[8:]
    rows = jnp.concatenate([p[...] for p in pieces], 1)

    def run(owner, mine):
        if owner is None:
            acc[...] = jnp.where(mine, matmul(rows, weight[0]), matmul(rows, weight[1]))
        else:
            acc[...] = matmul(rows, weight[owner])

    per_owner(tiles, rows.shape[0], spill, run)
    wide = hid.shape[1]
    up = acc[:, wide:]
    pre = acc[:, :wide]
    sig = 1.0 / (1.0 + jnp.exp(-pre))
    act = pre * sig
    hidden = (act * up).astype(bf16).astype(f32)
    gate = gate_ref[...]
    dh = dh_ref[...]
    dgate[...] = jnp.sum(hidden * dh, 1, keepdims=True)
    hid[...] = (hidden * gate).astype(bf16)
    dh = dh * gate
    dboth[:, :wide] = (dh * up * (sig * (1.0 + pre * (1.0 - sig)))).astype(bf16)
    dboth[:, wide:] = (dh * act).astype(bf16)


def rows_kernel(tiles, spill, transposed, spots, *refs):
    value, weight, outs = refs[0], refs[1], refs[2:]

    def run(owner, mine):
        rows = value[...]
        halves = ((rows, owner),)
        if owner is None:
            none = jnp.zeros_like(rows)
            halves = ((jnp.where(mine, rows, none), 0), (jnp.where(mine, none, rows), 1))
        for out, spot in zip(outs, spots):
            cols = slice(spot, spot + out.shape[1])
            total = None
            for part, who in halves:
                if transposed:
                    term = matmul_nt(part, weight[who, cols, :])
                else:
                    term = matmul(part, weight[who, :, cols])
                total = term if total is None else total + term
            out[...] = total.astype(bf16)

    per_owner(tiles, value.shape[0], spill, run)


def tile_spec(tile, width):
    return pl.BlockSpec((tile, width), lambda i: (i, 0))


def whole_spec(shape):
    return pl.BlockSpec(shape, lambda i: (0,) * len(shape))


def row_call(body, tile, total, ins, in_specs, outs, flops, scratch=()):
    out_shape = [jax.ShapeDtypeStruct((total, w), t) for w, t in outs]
    moved = sum(a.size * a.dtype.itemsize for a in (*ins, *out_shape))
    return pl.pallas_call(
        body,
        grid=(total // tile,),
        in_specs=in_specs,
        out_specs=[tile_spec(tile, w) for w, _ in outs],
        out_shape=out_shape,
        scratch_shapes=list(scratch),
        cost_estimate=pl.CostEstimate(flops=flops, bytes_accessed=moved, transcendentals=0),
        compiler_params=pltpu.CompilerParams(
            dimension_semantics=("arbitrary",), vmem_limit_bytes=VMEM_BYTES
        ),
    )(*ins)


def first_grad_kernel(
    kv_rows,
    normed,
    normed2,
    dmid,
    dquery,
    dlat,
    dlogits,
    attended,
    latent_n,
    dkeyval,
    gains,
    out,
    kv_grad,
):
    step = pl.program_id(0)

    @pl.when(step == 0)
    def _():
        kv_grad[...] = matmul_tn(latent_n[...], dkeyval[...]).astype(bf16)

    rows, kv_cols = out.shape[0], 256
    at_lat = dquery.shape[1]
    at_kv = at_lat + dlat.shape[1]
    at_out = at_kv + kv_cols
    at_gain = at_out + attended.shape[1]
    mine = normed[...]
    out[:, :at_lat] = matmul_tn(mine, dquery[...]).astype(bf16)
    out[:, at_lat:at_kv] = (
        matmul_tn(mine, dlat[...]) + matmul_tn(normed2[...], dlogits[...])
    ).astype(bf16)
    out[:, at_out:at_gain] = matmul_tn(dmid[...], attended[...]).astype(bf16)
    out[:, at_gain:] = gains[...]
    splits = kv_grad.shape[1] // kv_cols
    count = rows // kv_rows
    for j in range(count):
        if count % splits == 0:
            group = step * (count // splits) + j // splits
            lanes = slice(j % splits * kv_cols, (j % splits + 1) * kv_cols)
        else:
            group = (step * count + j) // splits
            lanes = pl.ds((step * count + j) % splits * kv_cols, kv_cols)
        from_rows = pl.ds(pl.multiple_of(group * kv_rows, kv_rows), kv_rows)
        out[j * kv_rows : (j + 1) * kv_rows, at_kv:at_out] = kv_grad[from_rows, lanes]


def first_grads(kv_rows, normed, normed2, dmid, dquery, dlat, dlogits, attended, latent_n, dkeyval, gains):
    block = 256
    cols = pl.BlockSpec((normed.shape[0], block), lambda i: (0, i))
    width = dquery.shape[1] + dlat.shape[1] + 256 + attended.shape[1] + gains.shape[1]
    whole = (dquery, dlat, dlogits, attended, latent_n, dkeyval)
    return pl.pallas_call(
        functools.partial(first_grad_kernel, kv_rows),
        grid=(D // block,),
        in_specs=[cols, cols, cols]
        + [whole_spec(a.shape) for a in whole]
        + [tile_spec(block, gains.shape[1])],
        out_specs=tile_spec(block, width),
        out_shape=jax.ShapeDtypeStruct((D, width), bf16),
        scratch_shapes=[pltpu.VMEM((KVR, dkeyval.shape[1]), bf16)],
        cost_estimate=pl.CostEstimate(
            flops=2 * D * width * normed.shape[0], bytes_accessed=3 * D * width, transcendentals=0
        ),
        compiler_params=pltpu.CompilerParams(
            dimension_semantics=("arbitrary",), vmem_limit_bytes=VMEM_BYTES
        ),
    )(normed, normed2, dmid, *whole, gains)


def second_grad_kernel(normed2, cotangent, dboth, hidden, out):
    split = dboth.shape[1]
    out[:, :split] = matmul_tn(normed2[...], dboth[...]).astype(bf16)
    out[:, split:] = matmul_tn(cotangent[...], hidden[...]).astype(bf16)


def second_grads(normed2, cotangent, dboth, hidden):
    block = 256
    cols = pl.BlockSpec((normed2.shape[0], block), lambda i: (0, i))
    width = dboth.shape[1] + hidden.shape[1]
    return pl.pallas_call(
        second_grad_kernel,
        grid=(D // block,),
        in_specs=[cols, cols, whole_spec(dboth.shape), whole_spec(hidden.shape)],
        out_specs=tile_spec(block, width),
        out_shape=jax.ShapeDtypeStruct((D, width), bf16),
        cost_estimate=pl.CostEstimate(
            flops=2 * D * width * normed2.shape[0], bytes_accessed=3 * D * width, transcendentals=0
        ),
        compiler_params=pltpu.CompilerParams(
            dimension_semantics=("arbitrary",), vmem_limit_bytes=VMEM_BYTES
        ),
    )(normed2, cotangent, dboth, hidden)


def per_device(
    tokens,
    expert_ids,
    route_slots,
    doc_ids,
    prenorm,
    query_w,
    latent_w,
    latnorm,
    keyval_w,
    output_w,
    midnorm,
    router_w,
    shgate_w,
    shup_w,
    shdown_w,
    exgate_w,
    exup_w,
    exdown_w,
    cotangent,
):
    owner_count = lax.axis_size("ep")
    experts = owner_count * EXP_DEV
    tok_count = tokens.shape[0]
    capacity = 2 * tok_count * TOPK // experts
    spill = capacity - MAIN
    width = EXP_DEV * capacity
    slot_rows = owner_count * width
    head_count = query_w.shape[1] // (DN + DR)
    score_scale = (DN + DR) ** (-0.5)
    shard = query_w.shape[0]
    q_cols = query_w.shape[1]
    lat_cols = latent_w.shape[1]
    kv_rows = keyval_w.shape[0]
    kv_cols = kv_rows * keyval_w.shape[1] // shard
    out_cols = output_w.shape[0]
    sh_cols = shgate_w.shape[1]

    gains = jnp.stack(
        [prenorm, jnp.pad(latnorm, (0, shard - latnorm.shape[0])), midnorm], 1
    )
    gains = jnp.pad(gains, ((0, 0), (0, 128 - gains.shape[1])))
    first_pack = jnp.concatenate(
        [
            query_w,
            latent_w,
            router_w,
            keyval_w.reshape(kv_rows, -1, kv_cols).transpose(1, 0, 2).reshape(shard, kv_cols),
            output_w.T,
            gains,
        ],
        1,
    )
    first_full = lax.all_gather(first_pack, "ep", axis=0, tiled=True)
    local = expert_ids % EXP_DEV
    inside = jnp.where(
        route_slots < MAIN,
        local * (MAIN + EXP_DEV * spill) + route_slots,
        MAIN + local * spill + (route_slots - MAIN),
    )
    place = (expert_ids // EXP_DEV) * width + inside
    row_iota = lax.broadcasted_iota(jnp.int32, (slot_rows, tok_count), 0)
    matches = [row_iota == place[:, k][None, :] for k in range(TOPK)]
    pick = matches[0]
    for k in range(1, TOPK):
        pick = pick | matches[k]
    pick = pick.astype(bf16)

    half = D // 8
    dy_sent = matmul(pick, quarter_of(cotangent, 0)).astype(bf16)
    dy_sent = to_experts(exchange(dy_sent.reshape(owner_count, width, -1)))
    lanes = lax.axis_size("tp")
    lane = lax.axis_index("tp")
    quarter = D // lanes
    hid_cols = exgate_w.shape[2]
    hid_wide = -(-hid_cols // 128) * 128

    def from_lane(value, axis):
        parts = []
        for step in range(lanes):
            at = lax.rem(lane + step, lanes) * quarter
            parts.append(lax.dynamic_slice_in_dim(value, at, quarter, axis))
        return jnp.concatenate(parts, axis)

    def to_lane(value, axis):
        parts = []
        for step in range(lanes):
            at = lax.rem(lanes - lane + step, lanes) * quarter
            parts.append(lax.dynamic_slice_in_dim(value, at, quarter, axis))
        return jnp.concatenate(parts, axis)

    fill = hid_wide - hid_cols
    gateup_w = jnp.concatenate(
        [
            jnp.pad(from_lane(exgate_w, 1), ((0, 0), (0, 0), (0, fill))),
            jnp.pad(from_lane(exup_w, 1), ((0, 0), (0, 0), (0, fill))),
        ],
        2,
    )
    down_plain = jnp.pad(exdown_w, ((0, 0), (0, fill), (0, 0)))
    down_w = jnp.pad(from_lane(exdown_w, 2), ((0, 0), (0, fill), (0, 0)))
    edge = owner_count * MAIN
    extra = slot_rows - 2 * edge
    span = edge + extra
    tile = 256 if edge % 256 == 0 else 128
    tiles = (edge // tile, extra // tile)
    big = 2 * (slot_rows + extra) * D * hid_wide
    first_full, dy_sent, gateup_w, down_w, down_plain = lax.optimization_barrier(
        (first_full, dy_sent, gateup_w, down_w, down_plain)
    )
    second_pack = jnp.concatenate([shgate_w, shup_w, shdown_w.T], 1)
    second_full = lax.all_gather(after(second_pack, first_full), "ep", axis=0, tiled=True)
    edges = [0]
    for cols in (q_cols, lat_cols, experts, kv_cols, out_cols, 128):
        edges.append(edges[-1] + cols)
    query_full = first_full[:, edges[0] : edges[1]]
    latent_full = first_full[:, edges[1] : edges[2]]
    router_full = first_full[:, edges[2] : edges[3]]
    keyval_full = first_full[:, edges[3] : edges[4]].reshape(owner_count, -1, kv_rows, kv_cols)
    keyval_full = keyval_full.transpose(0, 2, 1, 3).reshape(KVR, keyval_w.shape[1])
    output_t = first_full[:, edges[4] : edges[5]]
    pre_gain = first_full[:, edges[5]]
    lat_gain = first_full[:, edges[5] + 1].reshape(owner_count, shard)[:, : latnorm.shape[0]]
    lat_gain = lat_gain.reshape(KVR)
    mid_gain = first_full[:, edges[5] + 2]


    resid_in = tokens.astype(f32)
    pre_scale = rms_scale(resid_in)
    pre_weight = pre_gain.astype(f32)
    normed = (resid_in * pre_scale * pre_weight).astype(bf16)
    query_raw = matmul(normed, query_full).reshape(tok_count, head_count, DN + DR)
    latent_all = matmul(normed, latent_full)
    latent = latent_all[:, :KVR]
    lat_scale = rms_scale(latent)
    lat_weight = lat_gain.astype(f32)
    latent_n = (latent * lat_scale * lat_weight).astype(bf16)
    keyval = matmul(latent_n, keyval_full).astype(bf16).reshape(tok_count, head_count, DN + DV)
    cos_tab, sine_tab = rope_tables(tok_count)
    q_all = jnp.concatenate(
        [
            query_raw[..., :DN],
            rotate(query_raw[..., DN:], cos_tab[:, None, :], sine_tab[:, None, :]),
        ],
        -1,
    ).astype(bf16)
    key_rot = rotate(latent_all[:, KVR:], cos_tab, sine_tab).astype(bf16)
    key_all = jnp.concatenate(
        [keyval[..., :DN], jnp.broadcast_to(key_rot[:, None, :], (tok_count, head_count, DR))], -1
    )
    values = keyval[..., DN:]
    position = jnp.arange(tok_count)
    doc_row = doc_ids[0]
    allowed = ((doc_row[:, None] == doc_row[None, :]) & (position[:, None] >= position[None, :]))[
        None
    ]
    raw_scores = (
        jnp.einsum("thd,shd->hts", q_all, key_all, preferred_element_type=f32) * score_scale
    )
    masked = jnp.where(allowed, raw_scores, masked_fill)
    row_max = jnp.max(masked, -1, keepdims=True)
    exp_scores = jnp.exp(masked - row_max)
    softmax_sum = jnp.sum(exp_scores, -1, keepdims=True)
    probs = exp_scores / softmax_sum
    probs16 = probs.astype(bf16)
    attended = jnp.einsum("hts,shd->thd", probs16, values, preferred_element_type=f32)
    attended = attended.reshape(tok_count, head_count * DV).astype(bf16)
    dy_all = lax.all_gather(after(dy_sent, attended), "tp", axis=0, tiled=True)
    attn_sum = gather_quarters(sum_to_quarter(matmul_nt(attended, output_t)).astype(bf16))
    mid_resid = resid_in + attn_sum.astype(f32)
    mid_scale = rms_scale(mid_resid)
    mid_weight = mid_gain.astype(f32)
    normed2 = (mid_resid * mid_scale * mid_weight).astype(bf16)

    sent = matmul(pick, quarter_of(normed2, 0)).astype(bf16).reshape(owner_count, width, -1)
    one = exchange(sent[:, :, :half])
    two = exchange(after(sent[:, :, half:], one))
    own = (to_experts(one), to_experts(two))
    first = ring_gather_first(*own)
    dy_all = after(dy_all, two)
    (ex_dh,) = row_call(
        functools.partial(hidden_back_kernel, tiles, spill),
        tile,
        slot_rows,
        (*[dy_all] * lanes, down_plain),
        [
            pl.BlockSpec((tile, quarter), lambda i, q=q: (q * (slot_rows // tile) + i, 0))
            for q in range(lanes)
        ]
        + [whole_spec(down_plain.shape)],
        [(hid_wide, f32)],
        big,
    )

    upstream = cotangent.astype(f32)
    sh_in, sh_dy = after((normed2, cotangent), two)
    gateup_full = second_full[:, : 2 * sh_cols]
    shdown_t = second_full[:, 2 * sh_cols :]
    sh_both = matmul(sh_in, gateup_full)
    sh_gate = sh_both[:, :sh_cols]
    sh_up = sh_both[:, sh_cols:]
    sh_sig = 1.0 / (1.0 + jnp.exp(-sh_gate))
    sh_hidden = (sh_gate * sh_sig * sh_up).astype(bf16)
    shared_part = matmul_nt(sh_hidden, shdown_t).astype(bf16)
    sh_dhidden = matmul(sh_dy, shdown_t)
    sh_dgate = (sh_dhidden * sh_up * sh_sig * (1.0 + sh_gate * (1.0 - sh_sig))).astype(bf16)
    sh_dup = (sh_dhidden * sh_gate * sh_sig).astype(bf16)
    sh_dboth = jnp.concatenate([sh_dgate, sh_dup], 1)
    sh_dnormed_part = matmul_nt(sh_dboth, gateup_full).astype(bf16)
    second_grad = second_grads(normed2, cotangent, sh_dboth, sh_hidden)
    second_sum = lax.psum_scatter(second_grad, "ep", scatter_dimension=0, tiled=True)

    first, shared_part, sh_dnormed_part, second_grad = lax.optimization_barrier(
        (first, shared_part, sh_dnormed_part, second_grad)
    )
    shared_q = sum_to_quarter(shared_part)
    sh_dnormed_q = sum_to_quarter(sh_dnormed_part)
    rows = ring_gather_parts(*own, first, ring_gather_second(first))

    logits = matmul(normed2, router_full)
    onehot = (
        expert_ids[:, :, None] == jnp.arange(experts, dtype=jnp.int32)[None, None, :]
    ).astype(f32)
    chosen = jnp.sum(onehot * logits[:, None, :], -1)
    sel_vals = 1.0 / (1.0 + jnp.exp(-chosen))
    sel_total = jnp.sum(sel_vals, -1, keepdims=True)
    gate_vals = route_scale * sel_vals / sel_total
    gate_rows = jnp.zeros((slot_rows, tok_count), f32)
    for k in range(TOPK):
        gate_rows = gate_rows + jnp.where(matches[k], gate_vals[:, k][None, :], 0.0)
    gate_rows = jnp.sum(gate_rows, 1).reshape(owner_count, width)
    gate_rows = to_experts(exchange(after(gate_rows, two)))[:, None]

    ex_hidden, ex_dboth, dgate_rows = row_call(
        functools.partial(hidden_kernel, tiles, spill),
        tile,
        slot_rows,
        (*rows, gateup_w, ex_dh, gate_rows),
        [tile_spec(tile, half)] * 8
        + [whole_spec(gateup_w.shape), tile_spec(tile, hid_wide), tile_spec(tile, 1)],
        [(hid_wide, bf16), (2 * hid_wide, bf16), (1, f32)],
        2 * big,
        [pltpu.VMEM((tile, 2 * hid_wide), f32)],
    )

    def row_parts(value, weight, transposed, spots):
        return row_call(
            functools.partial(rows_kernel, tiles, spill, transposed, spots),
            tile,
            slot_rows,
            (value, weight),
            [tile_spec(tile, value.shape[1]), whole_spec(weight.shape)],
            [(half, bf16)] * len(spots),
            2 * (slot_rows + extra) * value.shape[1] * half * len(spots),
        )

    far_spots = [2 * quarter, 2 * quarter + half]
    other_spots = [0, half, quarter, quarter + half, 3 * quarter, 3 * quarter + half]

    extra_iota = lax.broadcasted_iota(jnp.int32, (span, 1), 0)
    owned = (
        (extra_iota < edge) | ((extra_iota - edge) % (EXP_DEV * spill) < spill),
        (extra_iota >= extra) | (extra_iota % (EXP_DEV * spill) >= spill),
    )

    def expert_rows(value, e):
        return value[:span] if e == 0 else value[edge:]

    def grads_of(e, left, right, cols):
        kept = jnp.where(owned[e], expert_rows(right, e)[:, cols], jnp.zeros((), bf16))
        return matmul_tn(expert_rows(left, e), kept)

    def grads_of_down(late):
        wide_dy = after(dy_all, late).reshape(lanes, slot_rows, quarter)
        wide_dy = jnp.concatenate([wide_dy[q] for q in range(lanes)], 1)
        hidden = after(ex_hidden[:, :hid_cols], late)
        parts = []
        for e in range(EXP_DEV):
            kept = jnp.where(owned[e], expert_rows(hidden, e), jnp.zeros((), bf16))
            parts.append(matmul_tn(kept, expert_rows(wide_dy, e)))
        return jnp.stack(parts)

    def bring_back(one, two):
        back_one = exchange(from_experts(one, owner_count)).reshape(slot_rows, -1)
        back_two = exchange(from_experts(two, owner_count)).reshape(slot_rows, -1)
        return jnp.concatenate([matmul_tn(pick, back_one), matmul_tn(pick, back_two)], 1)

    drow_far = row_parts(ex_dboth, gateup_w, True, far_spots)
    drow = row_parts(ex_dboth, gateup_w, True, other_spots)
    top = shift(drow_far[0], 1)
    bottom = shift(drow_far[1], 3)
    from_next_one = shift(drow[4], 3)
    dgate_rows = after(dgate_rows[:, 0], drow_far)
    dgate_rows = exchange(from_experts(dgate_rows, owner_count)).reshape(-1)
    top, dgate_rows = lax.optimization_barrier((top, dgate_rows))
    next_one = plus(drow[2], top)
    from_prev_one = shift(next_one, 1)
    from_prev_two = shift(after(drow[3], from_prev_one), 1)
    from_next_two = shift(plus(drow[5], bottom), 3)
    drow_one = add_three(drow[0], from_prev_one, from_next_one)
    drow_two = add_three(drow[1], from_prev_two, from_next_two)
    routed_grad_q = bring_back(drow_one, drow_two)
    out_parts = row_parts(ex_hidden, down_w, False, far_spots + other_spots)
    out_far, out_own = after(tuple(out_parts[:2]), drow_two), out_parts[2:]
    out_first = ring_sum_first(out_far, out_own)

    dgate_part = jnp.stack(
        [jnp.sum(jnp.where(matches[k], dgate_rows[:, None], 0.0), 0) for k in range(TOPK)], 1
    )
    dgate_all = sum_small(dgate_part)
    weighted = jnp.sum(dgate_all * gate_vals, -1, keepdims=True) / route_scale
    dsel_vals = route_scale / sel_total * (dgate_all - weighted)
    dchosen = dsel_vals * sel_vals * (1.0 - sel_vals)
    dlogits = jnp.sum(onehot * dchosen[:, :, None], 1).astype(bf16)
    dnormed2 = gather_quarters((routed_grad_q + sh_dnormed_q).astype(bf16)).astype(f32)
    dnormed2 = dnormed2 + matmul_nt(dlogits, router_full)
    dmid_norm, midnorm_grad = rms_back(mid_resid, mid_scale, mid_weight, dnormed2)
    dmid = upstream + dmid_norm
    dmid16, out_first = lax.optimization_barrier((dmid.astype(bf16), out_first))
    out_second = ring_sum_second(out_first, out_own)
    dattended = matmul(dmid16, output_t).astype(bf16).reshape(tok_count, head_count, DV)
    dprobs = jnp.einsum("thd,shd->hts", dattended, values, preferred_element_type=f32)
    dscores = (probs * (dprobs - jnp.sum(probs * dprobs, -1, keepdims=True))).astype(bf16)
    dq_all = (
        jnp.einsum("hts,shd->thd", dscores, key_all, preferred_element_type=f32) * score_scale
    )
    dkey_all = jnp.einsum("hts,thd->shd", dscores, q_all, preferred_element_type=f32) * score_scale
    dvalues = jnp.einsum("hts,thd->shd", probs16, dattended, preferred_element_type=f32)
    dquery = jnp.concatenate(
        [dq_all[..., :DN], rotate(dq_all[..., DN:], cos_tab[:, None, :], -sine_tab[:, None, :])], -1
    )
    dquery = dquery.reshape(tok_count, head_count * (DN + DR)).astype(bf16)
    dkeyval = (
        jnp.concatenate([dkey_all[..., :DN], dvalues], -1)
        .reshape(tok_count, head_count * (DN + DV))
        .astype(bf16)
    )
    dlatent_part = matmul_nt(dkeyval, keyval_full)
    dkey_part = jnp.sum(dkey_all[..., DN:], 1)
    dlat_sum = sum_small(jnp.concatenate([dlatent_part, dkey_part], 1).astype(bf16))
    dnormed_q = sum_to_quarter(matmul_nt(dquery, query_full))
    dlat_sum, second_sum, out_second = lax.optimization_barrier((dlat_sum, second_sum, out_second))
    dlatent, latnorm_grad = rms_back(latent, lat_scale, lat_weight, dlat_sum[:, :KVR])
    dlatent_all = jnp.concatenate(
        [dlatent, rotate(dlat_sum[:, KVR:], cos_tab, -sine_tab)], -1
    ).astype(bf16)
    dnormed = gather_quarters(dnormed_q.astype(bf16)).astype(f32) + matmul_nt(
        dlatent_all, latent_full
    )
    dtokens, prenorm_grad = rms_back(resid_in, pre_scale, pre_weight, dnormed)
    tokens_grad = (dmid + dtokens).astype(bf16)
    prenorm_sum = jnp.sum(exchange(prenorm_grad.reshape(owner_count, shard)), 0)
    gain_grads = jnp.stack(
        [
            jnp.pad(
                latnorm_grad.reshape(owner_count, -1),
                ((0, 0), (0, shard - latnorm.shape[0])),
            ).reshape(-1),
            midnorm_grad,
        ],
        1,
    )
    gain_grads = jnp.pad(gain_grads, ((0, 0), (0, 128 - gain_grads.shape[1])))
    first_grad = first_grads(
        kv_rows,
        normed,
        normed2,
        dmid16,
        dquery,
        jnp.pad(dlatent_all, ((0, 0), (0, experts))),
        jnp.pad(dlogits, ((0, 0), (lat_cols, 0))),
        attended,
        latent_n,
        dkeyval,
        gain_grads.astype(bf16),
    )
    down_grad = grads_of_down(first_grad)
    all_rows = jnp.concatenate(after(rows, first_grad), 1)
    late_dboth = after(ex_dboth, first_grad)
    exgate_grad = jnp.stack(
        [grads_of(e, all_rows, late_dboth, slice(0, hid_cols)) for e in range(EXP_DEV)]
    )
    exup_grad = jnp.stack(
        [
            grads_of(e, all_rows, late_dboth, slice(hid_wide, hid_wide + hid_cols))
            for e in range(EXP_DEV)
        ]
    )
    exgate_grad = to_lane(exgate_grad, 1)
    exup_grad = to_lane(exup_grad, 1)
    out_one = add_three(out_own[0], *after((out_second[0], out_first[2]), first_grad, dnormed))
    out_two = add_three(out_own[1], *after((out_first[3], out_second[1]), first_grad, dnormed))
    routed_q = bring_back(out_one, out_two)
    layer_q = (quarter_of(mid_resid, 0) + routed_q + shared_q).astype(bf16)
    layer_out = gather_quarters(layer_q)
    first_sum = lax.psum_scatter(first_grad, "ep", scatter_dimension=0, tiled=True).astype(f32)
    second_sum = second_sum.astype(f32)
    return (
        layer_out,
        tokens_grad,
        prenorm_sum,
        first_sum[:, edges[0] : edges[1]],
        first_sum[:, edges[1] : edges[2]],
        first_sum[: latnorm.shape[0], edges[5]],
        first_sum[:, edges[3] : edges[4]]
        .reshape(-1, kv_rows, kv_cols)
        .transpose(1, 0, 2)
        .reshape(keyval_w.shape),
        first_sum[:, edges[4] : edges[5]].T,
        first_sum[:, edges[5] + 1],
        first_sum[:, edges[2] : edges[3]],
        second_sum[:, :sh_cols],
        second_sum[:, sh_cols : 2 * sh_cols],
        second_sum[:, 2 * sh_cols :].T,
        exgate_grad,
        exup_grad,
        down_grad,
    )


def solution(mesh):
    in_specs = (
        P("ep", None),
        P("ep", None),
        P("ep", None),
        P("ep", None),
        P("ep"),
        P("ep", "tp"),
        P("ep", None),
        P("ep"),
        P("ep", "tp"),
        P("tp", "ep"),
        P("ep"),
        P("ep", None),
        P("ep", "tp"),
        P("ep", "tp"),
        P("tp", "ep"),
        P("ep", None, "tp"),
        P("ep", None, "tp"),
        P("ep", "tp", None),
        P("ep", None),
    )
    out_specs = (
        P("ep", None),
        P("ep", None),
        P("ep"),
        P("ep", "tp"),
        P("ep", None),
        P("ep"),
        P("ep", "tp"),
        P("tp", "ep"),
        P("ep"),
        P("ep", None),
        P("ep", "tp"),
        P("ep", "tp"),
        P("tp", "ep"),
        P("ep", None, "tp"),
        P("ep", None, "tp"),
        P("ep", "tp", None),
    )
    return jax.shard_map(
        per_device, mesh=mesh, in_specs=in_specs, out_specs=out_specs, check_vma=False
    )
```

```python
import functools

import jax
import jax.numpy as jnp
from jax import lax
from jax.experimental import pallas as pl
from jax.experimental.pallas import tpu as pltpu
from jax.sharding import PartitionSpec as P

D = 2048
DN = 128
DR = 64
DV = 128
KVR = 512
TOPK = 6
EXP_DEV = 2
MAIN = 32

epsilon = 1e-06
route_scale = 2.446
rope_base = 50000.0
masked_fill = -1000000000.0

bf16 = jnp.bfloat16
f32 = jnp.float32


def matmul(left_mat, right_mat):
    return jnp.dot(left_mat, right_mat, preferred_element_type=f32)


def matmul_nt(left_mat, right_mat):
    return lax.dot_general(
        left_mat, right_mat, (((1,), (1,)), ((), ())), preferred_element_type=f32
    )


def matmul_tn(left_mat, right_mat):
    return lax.dot_general(
        left_mat, right_mat, (((0,), (0,)), ((), ())), preferred_element_type=f32
    )


def rms_scale(values):
    return lax.rsqrt(jnp.mean(values * values, -1, keepdims=True) + epsilon)


def rms_back(values, scale_vals, gain_vec, upstream):
    weighted = upstream * gain_vec
    inner_mean = jnp.mean(weighted * values, -1, keepdims=True)
    grad_in = scale_vals * weighted - values * scale_vals * scale_vals * scale_vals * inner_mean
    grad_gain = jnp.sum(upstream * values * scale_vals, 0)
    return (grad_in, grad_gain)


def rope_tables(row_count):
    half_dim = DR // 2
    freq_vec = rope_base ** (-(jnp.arange(half_dim, dtype=f32) * (2.0 / DR)))
    angle_tab = jnp.arange(row_count, dtype=f32)[:, None] * freq_vec[None, :]
    return (jnp.cos(angle_tab), jnp.sin(angle_tab))


def rotate(values, cos_tab, sine_tab):
    half_dim = values.shape[-1] // 2
    first_half = values[..., :half_dim]
    second_half = values[..., half_dim:]
    return jnp.concatenate(
        [
            first_half * cos_tab - second_half * sine_tab,
            second_half * cos_tab + first_half * sine_tab,
        ],
        -1,
    )


def shift(value, step):
    lanes = lax.axis_size("tp")
    return lax.ppermute(value, "tp", [(i, (i + step) % lanes) for i in range(lanes)])


def quarter_of(value, step):
    lanes = lax.axis_size("tp")
    width = value.shape[1] // lanes
    lane = lax.rem(lax.axis_index("tp") + step, lanes)
    return lax.dynamic_slice_in_dim(value, lane * width, width, 1)


def sum_to_quarter(partial):
    low = partial.astype(bf16)
    total = quarter_of(low, 0).astype(f32)
    for step in (1, 3, 2):
        total = total + shift(quarter_of(low, step), step).astype(f32)
    return total


def gather_quarters(piece):
    lanes = lax.axis_size("tp")
    lane = lax.axis_index("tp")
    parts = [piece] + [None] * (lanes - 1)
    for step in (1, 3, 2):
        parts[step] = shift(piece, lanes - step)
    full = jnp.concatenate(parts, 1)
    width = piece.shape[1]
    parts = []
    for step in range(lanes):
        at = lax.rem(lanes - lane + step, lanes) * width
        parts.append(lax.dynamic_slice_in_dim(full, at, width, 1))
    return jnp.concatenate(parts, 1)


def sum_small(partial):
    total = partial.astype(f32)
    for step in (1, 3, 2):
        total = total + shift(partial, step).astype(f32)
    return total


def exchange(value):
    return lax.all_to_all(value, "ep", 0, 0, tiled=True)


def to_experts(value):
    blocks = value.shape[0]
    rest = value.shape[2:]
    return jnp.concatenate(
        [
            value[:, :MAIN].reshape(blocks * MAIN, *rest),
            value[:, MAIN:-MAIN].reshape(-1, *rest),
            value[:, -MAIN:].reshape(blocks * MAIN, *rest),
        ],
        0,
    )


def from_experts(value, blocks):
    rest = value.shape[1:]
    edge = blocks * MAIN
    return jnp.concatenate(
        [
            value[:edge].reshape(blocks, MAIN, *rest),
            value[edge:-edge].reshape(blocks, -1, *rest),
            value[-edge:].reshape(blocks, MAIN, *rest),
        ],
        1,
    )


def after(value, *others):
    return lax.optimization_barrier((value, others))[0]


def plus(one, two):
    return (one.astype(f32) + two.astype(f32)).astype(bf16)


def ring_gather_first(one, two):
    return shift(one, 1), shift(two, 3), shift(two, 1), shift(one, 3)


def ring_gather_second(first):
    return shift(first[0], 1), shift(first[1], 3)


def ring_gather_parts(one, two, first, second):
    one_prev, two_next, two_prev, one_next = first
    return (one, two, one_next, two_next, second[0], second[1], one_prev, two_prev)


def add_three(one, two, three):
    return (one.astype(f32) + two.astype(f32) + three.astype(f32)).astype(bf16)


VMEM_BYTES = 44 * 1024 * 1024


def first_owner_rows(tiles, tile, spill):
    row = lax.broadcasted_iota(jnp.int32, (tile, 1), 0) + (pl.program_id(0) - tiles[0]) * tile
    return lax.rem(row, EXP_DEV * spill) < spill


def per_owner(tiles, tile, spill, run):
    first, mixed = tiles
    step = pl.program_id(0)
    mine = first_owner_rows(tiles, tile, spill)
    is_mixed = (step >= first) & (step < first + mixed)

    @pl.when(is_mixed)
    def _():
        run(None, mine)

    @pl.when(jnp.logical_not(is_mixed))
    def _():
        run(jnp.where(step < first, 0, 1), None)


def hidden_back_kernel(tiles, spill, *refs):
    pieces, weight, out = refs[:-2], refs[-2], refs[-1]
    rows = jnp.concatenate([p[...] for p in pieces], 1)

    def run(owner, mine):
        if owner is None:
            out[...] = jnp.where(mine, matmul_nt(rows, weight[0]), matmul_nt(rows, weight[1]))
        else:
            out[...] = matmul_nt(rows, weight[owner])

    per_owner(tiles, rows.shape[0], spill, run)


def hidden_kernel(tiles, spill, *refs):
    pieces, (weight, dh_ref, gate_ref, hid, dboth, dgate), refs = refs[:8], refs[8:14], refs[14:]
    drow, acc = refs[:8], refs[8]
    rows = jnp.concatenate([p[...] for p in pieces], 1)

    def run(owner, mine):
        if owner is None:
            acc[...] = jnp.where(mine, matmul(rows, weight[0]), matmul(rows, weight[1]))
        else:
            acc[...] = matmul(rows, weight[owner])

    per_owner(tiles, rows.shape[0], spill, run)
    wide = hid.shape[1]
    up = acc[:, wide:]
    pre = acc[:, :wide]
    sig = 1.0 / (1.0 + jnp.exp(-pre))
    act = pre * sig
    hidden = (act * up).astype(bf16).astype(f32)
    gate = gate_ref[...]
    dh = dh_ref[...]
    dgate[...] = jnp.sum(hidden * dh, 1, keepdims=True)
    hid[...] = (hidden * gate).astype(bf16)
    dh = dh * gate
    dboth[:, :wide] = (dh * up * (sig * (1.0 + pre * (1.0 - sig)))).astype(bf16)
    dboth[:, wide:] = (dh * act).astype(bf16)

    def back(owner, mine):
        grad = dboth[...]
        cols = drow[0].shape[1]
        none = jnp.zeros_like(grad)
        for j, out in enumerate(drow):
            at = slice(j * cols, (j + 1) * cols)
            if owner is None:
                total = matmul_nt(jnp.where(mine, grad, none), weight[0, at, :])
                total = total + matmul_nt(jnp.where(mine, none, grad), weight[1, at, :])
            else:
                total = matmul_nt(grad, weight[owner, at, :])
            out[...] = total.astype(bf16)

    per_owner(tiles, rows.shape[0], spill, back)


def out_kernel(tiles, spill, value, weight, *outs):
    def run(owner, mine):
        rows = value[...]
        none = jnp.zeros_like(rows)
        for j, out in enumerate(outs):
            at = slice(j * out.shape[1], (j + 1) * out.shape[1])
            if owner is None:
                total = matmul(jnp.where(mine, rows, none), weight[0, :, at])
                total = total + matmul(jnp.where(mine, none, rows), weight[1, :, at])
            else:
                total = matmul(rows, weight[owner, :, at])
            out[...] = total.astype(bf16)

    per_owner(tiles, value.shape[0], spill, run)


def tile_spec(tile, width):
    return pl.BlockSpec((tile, width), lambda i: (i, 0))


def whole_spec(shape):
    return pl.BlockSpec(shape, lambda i: (0,) * len(shape))


def row_call(body, tile, total, ins, in_specs, outs, flops, scratch=()):
    out_shape = [jax.ShapeDtypeStruct((total, w), t) for w, t in outs]
    moved = sum(a.size * a.dtype.itemsize for a in (*ins, *out_shape))
    return pl.pallas_call(
        body,
        grid=(total // tile,),
        in_specs=in_specs,
        out_specs=[tile_spec(tile, w) for w, _ in outs],
        out_shape=out_shape,
        scratch_shapes=list(scratch),
        cost_estimate=pl.CostEstimate(flops=flops, bytes_accessed=moved, transcendentals=0),
        compiler_params=pltpu.CompilerParams(
            dimension_semantics=("arbitrary",), vmem_limit_bytes=VMEM_BYTES
        ),
    )(*ins)


def first_grad_kernel(
    kv_rows,
    normed,
    normed2,
    dmid,
    dquery,
    dlat,
    dlogits,
    attended,
    latent_n,
    dkeyval,
    gains,
    out,
    kv_grad,
):
    step = pl.program_id(0)

    @pl.when(step == 0)
    def _():
        kv_grad[...] = matmul_tn(latent_n[...], dkeyval[...]).astype(bf16)

    rows, kv_cols = out.shape[0], 256
    at_lat = dquery.shape[1]
    at_kv = at_lat + dlat.shape[1]
    at_out = at_kv + kv_cols
    at_gain = at_out + attended.shape[1]
    mine = normed[...]
    out[:, :at_lat] = matmul_tn(mine, dquery[...]).astype(bf16)
    out[:, at_lat:at_kv] = (
        matmul_tn(mine, dlat[...]) + matmul_tn(normed2[...], dlogits[...])
    ).astype(bf16)
    out[:, at_out:at_gain] = matmul_tn(dmid[...], attended[...]).astype(bf16)
    out[:, at_gain:] = gains[...]
    splits = kv_grad.shape[1] // kv_cols
    count = rows // kv_rows
    for j in range(count):
        if count % splits == 0:
            group = step * (count // splits) + j // splits
            lanes = slice(j % splits * kv_cols, (j % splits + 1) * kv_cols)
        else:
            group = (step * count + j) // splits
            lanes = pl.ds((step * count + j) % splits * kv_cols, kv_cols)
        from_rows = pl.ds(pl.multiple_of(group * kv_rows, kv_rows), kv_rows)
        out[j * kv_rows : (j + 1) * kv_rows, at_kv:at_out] = kv_grad[from_rows, lanes]


def first_grads(kv_rows, normed, normed2, dmid, dquery, dlat, dlogits, attended, latent_n, dkeyval, gains):
    block = 256
    cols = pl.BlockSpec((normed.shape[0], block), lambda i: (0, i))
    width = dquery.shape[1] + dlat.shape[1] + 256 + attended.shape[1] + gains.shape[1]
    whole = (dquery, dlat, dlogits, attended, latent_n, dkeyval)
    return pl.pallas_call(
        functools.partial(first_grad_kernel, kv_rows),
        grid=(D // block,),
        in_specs=[cols, cols, cols]
        + [whole_spec(a.shape) for a in whole]
        + [tile_spec(block, gains.shape[1])],
        out_specs=tile_spec(block, width),
        out_shape=jax.ShapeDtypeStruct((D, width), bf16),
        scratch_shapes=[pltpu.VMEM((KVR, dkeyval.shape[1]), bf16)],
        cost_estimate=pl.CostEstimate(
            flops=2 * D * width * normed.shape[0], bytes_accessed=3 * D * width, transcendentals=0
        ),
        compiler_params=pltpu.CompilerParams(
            dimension_semantics=("arbitrary",), vmem_limit_bytes=VMEM_BYTES
        ),
    )(normed, normed2, dmid, *whole, gains)


def second_grad_kernel(normed2, cotangent, dboth, hidden, out):
    split = dboth.shape[1]
    out[:, :split] = matmul_tn(normed2[...], dboth[...]).astype(bf16)
    out[:, split:] = matmul_tn(cotangent[...], hidden[...]).astype(bf16)


def second_grads(normed2, cotangent, dboth, hidden):
    block = 256
    cols = pl.BlockSpec((normed2.shape[0], block), lambda i: (0, i))
    width = dboth.shape[1] + hidden.shape[1]
    return pl.pallas_call(
        second_grad_kernel,
        grid=(D // block,),
        in_specs=[cols, cols, whole_spec(dboth.shape), whole_spec(hidden.shape)],
        out_specs=tile_spec(block, width),
        out_shape=jax.ShapeDtypeStruct((D, width), bf16),
        cost_estimate=pl.CostEstimate(
            flops=2 * D * width * normed2.shape[0], bytes_accessed=3 * D * width, transcendentals=0
        ),
        compiler_params=pltpu.CompilerParams(
            dimension_semantics=("arbitrary",), vmem_limit_bytes=VMEM_BYTES
        ),
    )(normed2, cotangent, dboth, hidden)


def per_device(
    tokens,
    expert_ids,
    route_slots,
    doc_ids,
    prenorm,
    query_w,
    latent_w,
    latnorm,
    keyval_w,
    output_w,
    midnorm,
    router_w,
    shgate_w,
    shup_w,
    shdown_w,
    exgate_w,
    exup_w,
    exdown_w,
    cotangent,
):
    owner_count = lax.axis_size("ep")
    experts = owner_count * EXP_DEV
    tok_count = tokens.shape[0]
    capacity = 2 * tok_count * TOPK // experts
    spill = capacity - MAIN
    width = EXP_DEV * capacity
    slot_rows = owner_count * width
    head_count = query_w.shape[1] // (DN + DR)
    score_scale = (DN + DR) ** (-0.5)
    shard = query_w.shape[0]
    q_cols = query_w.shape[1]
    lat_cols = latent_w.shape[1]
    kv_rows = keyval_w.shape[0]
    kv_cols = kv_rows * keyval_w.shape[1] // shard
    out_cols = output_w.shape[0]
    sh_cols = shgate_w.shape[1]

    gains = jnp.stack(
        [prenorm, jnp.pad(latnorm, (0, shard - latnorm.shape[0])), midnorm], 1
    )
    gains = jnp.pad(gains, ((0, 0), (0, 128 - gains.shape[1])))
    first_pack = jnp.concatenate(
        [
            query_w,
            latent_w,
            router_w,
            keyval_w.reshape(kv_rows, -1, kv_cols).transpose(1, 0, 2).reshape(shard, kv_cols),
            output_w.T,
            gains,
        ],
        1,
    )
    first_full = lax.all_gather(first_pack, "ep", axis=0, tiled=True)
    local = expert_ids % EXP_DEV
    inside = jnp.where(
        route_slots < MAIN,
        local * (MAIN + EXP_DEV * spill) + route_slots,
        MAIN + local * spill + (route_slots - MAIN),
    )
    place = (expert_ids // EXP_DEV) * width + inside
    row_iota = lax.broadcasted_iota(jnp.int32, (slot_rows, tok_count), 0)
    matches = [row_iota == place[:, k][None, :] for k in range(TOPK)]
    pick = matches[0]
    for k in range(1, TOPK):
        pick = pick | matches[k]
    pick = pick.astype(bf16)

    half = D // 8
    dy_sent = matmul(pick, quarter_of(cotangent, 0)).astype(bf16)
    dy_sent = to_experts(exchange(dy_sent.reshape(owner_count, width, -1)))
    lanes = lax.axis_size("tp")
    lane = lax.axis_index("tp")
    quarter = D // lanes
    hid_cols = exgate_w.shape[2]
    hid_wide = -(-hid_cols // 128) * 128

    def from_lane(value, axis):
        parts = []
        for step in range(lanes):
            at = lax.rem(lane + step, lanes) * quarter
            parts.append(lax.dynamic_slice_in_dim(value, at, quarter, axis))
        return jnp.concatenate(parts, axis)

    def to_lane(value, axis):
        parts = []
        for step in range(lanes):
            at = lax.rem(lanes - lane + step, lanes) * quarter
            parts.append(lax.dynamic_slice_in_dim(value, at, quarter, axis))
        return jnp.concatenate(parts, axis)

    fill = hid_wide - hid_cols
    gateup_w = jnp.concatenate(
        [
            jnp.pad(from_lane(exgate_w, 1), ((0, 0), (0, 0), (0, fill))),
            jnp.pad(from_lane(exup_w, 1), ((0, 0), (0, 0), (0, fill))),
        ],
        2,
    )
    down_plain = jnp.pad(exdown_w, ((0, 0), (0, fill), (0, 0)))
    down_w = jnp.pad(from_lane(exdown_w, 2), ((0, 0), (0, fill), (0, 0)))
    edge = owner_count * MAIN
    extra = slot_rows - 2 * edge
    span = edge + extra
    tile = 256 if edge % 256 == 0 else 128
    tiles = (edge // tile, extra // tile)
    big = 2 * (slot_rows + extra) * D * hid_wide
    first_full, dy_sent, gateup_w, down_w, down_plain = lax.optimization_barrier(
        (first_full, dy_sent, gateup_w, down_w, down_plain)
    )
    dy_all = lax.all_gather(after(dy_sent, first_full), "tp", axis=0, tiled=True)
    edges = [0]
    for cols in (q_cols, lat_cols, experts, kv_cols, out_cols, 128):
        edges.append(edges[-1] + cols)
    query_full = first_full[:, edges[0] : edges[1]]
    latent_full = first_full[:, edges[1] : edges[2]]
    router_full = first_full[:, edges[2] : edges[3]]
    keyval_full = first_full[:, edges[3] : edges[4]].reshape(owner_count, -1, kv_rows, kv_cols)
    keyval_full = keyval_full.transpose(0, 2, 1, 3).reshape(KVR, keyval_w.shape[1])
    output_t = first_full[:, edges[4] : edges[5]]
    pre_gain = first_full[:, edges[5]]
    lat_gain = first_full[:, edges[5] + 1].reshape(owner_count, shard)[:, : latnorm.shape[0]]
    lat_gain = lat_gain.reshape(KVR)
    mid_gain = first_full[:, edges[5] + 2]


    resid_in = tokens.astype(f32)
    pre_scale = rms_scale(resid_in)
    pre_weight = pre_gain.astype(f32)
    normed = (resid_in * pre_scale * pre_weight).astype(bf16)
    query_raw = matmul(normed, query_full).reshape(tok_count, head_count, DN + DR)
    latent_all = matmul(normed, latent_full)
    latent = latent_all[:, :KVR]
    lat_scale = rms_scale(latent)
    lat_weight = lat_gain.astype(f32)
    latent_n = (latent * lat_scale * lat_weight).astype(bf16)
    keyval = matmul(latent_n, keyval_full).astype(bf16).reshape(tok_count, head_count, DN + DV)
    cos_tab, sine_tab = rope_tables(tok_count)
    q_all = jnp.concatenate(
        [
            query_raw[..., :DN],
            rotate(query_raw[..., DN:], cos_tab[:, None, :], sine_tab[:, None, :]),
        ],
        -1,
    ).astype(bf16)
    key_rot = rotate(latent_all[:, KVR:], cos_tab, sine_tab).astype(bf16)
    key_all = jnp.concatenate(
        [keyval[..., :DN], jnp.broadcast_to(key_rot[:, None, :], (tok_count, head_count, DR))], -1
    )
    values = keyval[..., DN:]
    position = jnp.arange(tok_count)
    doc_row = doc_ids[0]
    allowed = ((doc_row[:, None] == doc_row[None, :]) & (position[:, None] >= position[None, :]))[
        None
    ]
    raw_scores = (
        jnp.einsum("thd,shd->hts", q_all, key_all, preferred_element_type=f32) * score_scale
    )
    masked = jnp.where(allowed, raw_scores, masked_fill)
    row_max = jnp.max(masked, -1, keepdims=True)
    exp_scores = jnp.exp(masked - row_max)
    softmax_sum = jnp.sum(exp_scores, -1, keepdims=True)
    probs = exp_scores / softmax_sum
    probs16 = probs.astype(bf16)
    attended = jnp.einsum("hts,shd->thd", probs16, values, preferred_element_type=f32)
    attended = attended.reshape(tok_count, head_count * DV).astype(bf16)
    second_pack = jnp.concatenate([shgate_w, shup_w, shdown_w.T], 1)
    second_full = lax.all_gather(after(second_pack, attended), "ep", axis=0, tiled=True)
    attn_sum = gather_quarters(sum_to_quarter(matmul_nt(attended, output_t)).astype(bf16))
    mid_resid = resid_in + attn_sum.astype(f32)
    mid_scale = rms_scale(mid_resid)
    mid_weight = mid_gain.astype(f32)
    normed2 = (mid_resid * mid_scale * mid_weight).astype(bf16)

    sent = matmul(pick, quarter_of(normed2, 0)).astype(bf16).reshape(owner_count, width, -1)
    one = exchange(sent[:, :, :half])
    two = exchange(after(sent[:, :, half:], one))
    own = (to_experts(one), to_experts(two))
    first = ring_gather_first(*own)
    dy_all = after(dy_all, two)
    (ex_dh,) = row_call(
        functools.partial(hidden_back_kernel, tiles, spill),
        tile,
        slot_rows,
        (*[dy_all] * lanes, down_plain),
        [
            pl.BlockSpec((tile, quarter), lambda i, q=q: (q * (slot_rows // tile) + i, 0))
            for q in range(lanes)
        ]
        + [whole_spec(down_plain.shape)],
        [(hid_wide, f32)],
        big,
    )

    upstream = cotangent.astype(f32)
    sh_in, sh_dy = after((normed2, cotangent), two)
    gateup_full = second_full[:, : 2 * sh_cols]
    shdown_t = second_full[:, 2 * sh_cols :]
    sh_both = matmul(sh_in, gateup_full)
    sh_gate = sh_both[:, :sh_cols]
    sh_up = sh_both[:, sh_cols:]
    sh_sig = 1.0 / (1.0 + jnp.exp(-sh_gate))
    sh_hidden = (sh_gate * sh_sig * sh_up).astype(bf16)
    shared_part = matmul_nt(sh_hidden, shdown_t).astype(bf16)
    sh_dhidden = matmul(sh_dy, shdown_t)
    sh_dgate = (sh_dhidden * sh_up * sh_sig * (1.0 + sh_gate * (1.0 - sh_sig))).astype(bf16)
    sh_dup = (sh_dhidden * sh_gate * sh_sig).astype(bf16)
    sh_dboth = jnp.concatenate([sh_dgate, sh_dup], 1)
    sh_dnormed_part = matmul_nt(sh_dboth, gateup_full).astype(bf16)
    second_grad = second_grads(normed2, cotangent, sh_dboth, sh_hidden)
    second_sum = lax.psum_scatter(second_grad, "ep", scatter_dimension=0, tiled=True)

    going, shared_part, sh_dnormed_part, second_grad = lax.optimization_barrier(
        (first[:2], shared_part, sh_dnormed_part, second_grad)
    )
    first = (*going, *first[2:])
    shared_q = sum_to_quarter(shared_part)
    sh_dnormed_q = sum_to_quarter(sh_dnormed_part)
    rows = ring_gather_parts(*own, first, ring_gather_second(first))

    logits = matmul(normed2, router_full)
    onehot = (
        expert_ids[:, :, None] == jnp.arange(experts, dtype=jnp.int32)[None, None, :]
    ).astype(f32)
    chosen = jnp.sum(onehot * logits[:, None, :], -1)
    sel_vals = 1.0 / (1.0 + jnp.exp(-chosen))
    sel_total = jnp.sum(sel_vals, -1, keepdims=True)
    gate_vals = route_scale * sel_vals / sel_total
    gate_rows = jnp.zeros((slot_rows, tok_count), f32)
    for k in range(TOPK):
        gate_rows = gate_rows + jnp.where(matches[k], gate_vals[:, k][None, :], 0.0)
    gate_rows = jnp.sum(gate_rows, 1).reshape(owner_count, width)
    gate_rows = to_experts(exchange(after(gate_rows, two)))[:, None]

    ex_hidden, ex_dboth, dgate_rows, *drow = row_call(
        functools.partial(hidden_kernel, tiles, spill),
        tile,
        slot_rows,
        (*rows, gateup_w, ex_dh, gate_rows),
        [tile_spec(tile, half)] * 8
        + [whole_spec(gateup_w.shape), tile_spec(tile, hid_wide), tile_spec(tile, 1)],
        [(hid_wide, bf16), (2 * hid_wide, bf16), (1, f32)] + [(half, bf16)] * 8,
        4 * big,
        [pltpu.VMEM((tile, 2 * hid_wide), f32)],
    )

    extra_iota = lax.broadcasted_iota(jnp.int32, (span, 1), 0)
    owned = (
        (extra_iota < edge) | ((extra_iota - edge) % (EXP_DEV * spill) < spill),
        (extra_iota >= extra) | (extra_iota % (EXP_DEV * spill) >= spill),
    )

    def expert_rows(value, e):
        return value[:span] if e == 0 else value[edge:]

    def grads_of(e, left, right, cols):
        kept = jnp.where(owned[e], expert_rows(right, e)[:, cols], jnp.zeros((), bf16))
        return matmul_tn(expert_rows(left, e), kept)

    def grads_of_down(late):
        wide_dy = after(dy_all, late).reshape(lanes, slot_rows, quarter)
        wide_dy = jnp.concatenate([wide_dy[q] for q in range(lanes)], 1)
        hidden = after(ex_hidden[:, :hid_cols], late)
        parts = []
        for e in range(EXP_DEV):
            kept = jnp.where(owned[e], expert_rows(hidden, e), jnp.zeros((), bf16))
            parts.append(matmul_tn(kept, expert_rows(wide_dy, e)))
        return jnp.stack(parts)

    def bring_back(one, two):
        back_one = exchange(from_experts(one, owner_count)).reshape(slot_rows, -1)
        back_two = exchange(from_experts(two, owner_count)).reshape(slot_rows, -1)
        return jnp.concatenate([matmul_tn(pick, back_one), matmul_tn(pick, back_two)], 1)

    out_parts = row_call(
        functools.partial(out_kernel, tiles, spill),
        tile,
        slot_rows,
        (ex_hidden, down_w),
        [tile_spec(tile, hid_wide), whole_spec(down_w.shape)],
        [(half, bf16)] * 8,
        big,
    )
    top = shift(drow[4], 1)
    bottom = shift(drow[5], 3)
    dgate_rows = exchange(from_experts(dgate_rows[:, 0], owner_count)).reshape(-1)
    top, bottom, dgate_rows, out_parts = lax.optimization_barrier(
        (top, bottom, dgate_rows, out_parts)
    )
    from_prev_one = shift(plus(drow[2], top), 1)
    from_next_one = shift(after(drow[6], bottom), 3)
    next_two, prev_two = after(
        (drow[3], plus(drow[7], bottom)), from_prev_one, from_next_one
    )
    from_prev_two = shift(next_two, 1)
    from_next_two = shift(prev_two, 3)
    drow_one = add_three(drow[0], from_prev_one, from_next_one)
    drow_two = add_three(drow[1], from_prev_two, from_next_two)
    routed_grad_q = bring_back(drow_one, drow_two)
    out_far = after(tuple(out_parts[4:6]), drow_two)
    out_top = shift(out_far[0], 1)
    out_bottom = shift(out_far[1], 3)
    routed_grad_q, out_top, out_bottom = lax.optimization_barrier(
        (routed_grad_q, out_top, out_bottom)
    )

    dgate_part = jnp.stack(
        [jnp.sum(jnp.where(matches[k], dgate_rows[:, None], 0.0), 0) for k in range(TOPK)], 1
    )
    dgate_all = sum_small(dgate_part)
    weighted = jnp.sum(dgate_all * gate_vals, -1, keepdims=True) / route_scale
    dsel_vals = route_scale / sel_total * (dgate_all - weighted)
    dchosen = dsel_vals * sel_vals * (1.0 - sel_vals)
    dlogits = jnp.sum(onehot * dchosen[:, :, None], 1).astype(bf16)
    dnormed2 = gather_quarters((routed_grad_q + sh_dnormed_q).astype(bf16)).astype(f32)
    dnormed2 = dnormed2 + matmul_nt(dlogits, router_full)
    dmid_norm, midnorm_grad = rms_back(mid_resid, mid_scale, mid_weight, dnormed2)
    dmid = upstream + dmid_norm
    dmid16 = dmid.astype(bf16)
    out_prev_one, out_next_two = after(
        (plus(out_parts[2], out_top), plus(out_parts[7], out_bottom)), dmid16
    )
    out_prev_one = shift(out_prev_one, 1)
    out_next_two = shift(out_next_two, 3)
    dattended = matmul(dmid16, output_t).astype(bf16).reshape(tok_count, head_count, DV)
    dprobs = jnp.einsum("thd,shd->hts", dattended, values, preferred_element_type=f32)
    dscores = (probs * (dprobs - jnp.sum(probs * dprobs, -1, keepdims=True))).astype(bf16)
    dq_all = (
        jnp.einsum("hts,shd->thd", dscores, key_all, preferred_element_type=f32) * score_scale
    )
    dkey_all = jnp.einsum("hts,thd->shd", dscores, q_all, preferred_element_type=f32) * score_scale
    dvalues = jnp.einsum("hts,thd->shd", probs16, dattended, preferred_element_type=f32)
    dquery = jnp.concatenate(
        [dq_all[..., :DN], rotate(dq_all[..., DN:], cos_tab[:, None, :], -sine_tab[:, None, :])], -1
    )
    dquery = dquery.reshape(tok_count, head_count * (DN + DR)).astype(bf16)
    dkeyval = (
        jnp.concatenate([dkey_all[..., :DN], dvalues], -1)
        .reshape(tok_count, head_count * (DN + DV))
        .astype(bf16)
    )
    dlatent_part = matmul_nt(dkeyval, keyval_full)
    dkey_part = jnp.sum(dkey_all[..., DN:], 1)
    dlat_part = jnp.concatenate([dlatent_part, dkey_part], 1).astype(bf16)
    dlat_part, out_prev_one, out_next_two = lax.optimization_barrier(
        (dlat_part, out_prev_one, out_next_two)
    )
    dlat_sum = sum_small(dlat_part)
    dnormed_q = sum_to_quarter(matmul_nt(dquery, query_full))
    dlat_sum, second_sum = lax.optimization_barrier((dlat_sum, second_sum))
    dlatent, latnorm_grad = rms_back(latent, lat_scale, lat_weight, dlat_sum[:, :KVR])
    dlatent_all = jnp.concatenate(
        [dlatent, rotate(dlat_sum[:, KVR:], cos_tab, -sine_tab)], -1
    ).astype(bf16)
    dnormed = gather_quarters(dnormed_q.astype(bf16)).astype(f32) + matmul_nt(
        dlatent_all, latent_full
    )
    dtokens, prenorm_grad = rms_back(resid_in, pre_scale, pre_weight, dnormed)
    tokens_grad = (dmid + dtokens).astype(bf16)
    prenorm_sum = jnp.sum(exchange(prenorm_grad.reshape(owner_count, shard)), 0)
    gain_grads = jnp.stack(
        [
            jnp.pad(
                latnorm_grad.reshape(owner_count, -1),
                ((0, 0), (0, shard - latnorm.shape[0])),
            ).reshape(-1),
            midnorm_grad,
        ],
        1,
    )
    gain_grads = jnp.pad(gain_grads, ((0, 0), (0, 128 - gain_grads.shape[1])))
    first_grad = first_grads(
        kv_rows,
        normed,
        normed2,
        dmid16,
        dquery,
        jnp.pad(dlatent_all, ((0, 0), (0, experts))),
        jnp.pad(dlogits, ((0, 0), (lat_cols, 0))),
        attended,
        latent_n,
        dkeyval,
        gain_grads.astype(bf16),
    )
    down_grad = grads_of_down(first_grad)
    all_rows = jnp.concatenate(after(rows, first_grad), 1)
    late_dboth = after(ex_dboth, first_grad)
    exgate_grad = jnp.stack(
        [grads_of(e, all_rows, late_dboth, slice(0, hid_cols)) for e in range(EXP_DEV)]
    )
    exup_grad = jnp.stack(
        [
            grads_of(e, all_rows, late_dboth, slice(hid_wide, hid_wide + hid_cols))
            for e in range(EXP_DEV)
        ]
    )
    exgate_grad = to_lane(exgate_grad, 1)
    exup_grad = to_lane(exup_grad, 1)
    out_late = after((out_parts[6], out_parts[3]), first_grad)
    out_next_one = shift(out_late[0], 3)
    out_prev_two = shift(out_late[1], 1)
    routed_q = bring_back(
        add_three(out_parts[0], out_prev_one, out_next_one),
        add_three(out_parts[1], out_prev_two, out_next_two),
    )
    layer_q = (quarter_of(mid_resid, 0) + routed_q + shared_q).astype(bf16)
    layer_out = gather_quarters(layer_q)
    first_sum = lax.psum_scatter(first_grad, "ep", scatter_dimension=0, tiled=True).astype(f32)
    second_sum = second_sum.astype(f32)
    return (
        layer_out,
        tokens_grad,
        prenorm_sum,
        first_sum[:, edges[0] : edges[1]],
        first_sum[:, edges[1] : edges[2]],
        first_sum[: latnorm.shape[0], edges[5]],
        first_sum[:, edges[3] : edges[4]]
        .reshape(-1, kv_rows, kv_cols)
        .transpose(1, 0, 2)
        .reshape(keyval_w.shape),
        first_sum[:, edges[4] : edges[5]].T,
        first_sum[:, edges[5] + 1],
        first_sum[:, edges[2] : edges[3]],
        second_sum[:, :sh_cols],
        second_sum[:, sh_cols : 2 * sh_cols],
        second_sum[:, 2 * sh_cols :].T,
        exgate_grad,
        exup_grad,
        down_grad,
    )


def solution(mesh):
    in_specs = (
        P("ep", None),
        P("ep", None),
        P("ep", None),
        P("ep", None),
        P("ep"),
        P("ep", "tp"),
        P("ep", None),
        P("ep"),
        P("ep", "tp"),
        P("tp", "ep"),
        P("ep"),
        P("ep", None),
        P("ep", "tp"),
        P("ep", "tp"),
        P("tp", "ep"),
        P("ep", None, "tp"),
        P("ep", None, "tp"),
        P("ep", "tp", None),
        P("ep", None),
    )
    out_specs = (
        P("ep", None),
        P("ep", None),
        P("ep"),
        P("ep", "tp"),
        P("ep", None),
        P("ep"),
        P("ep", "tp"),
        P("tp", "ep"),
        P("ep"),
        P("ep", None),
        P("ep", "tp"),
        P("ep", "tp"),
        P("tp", "ep"),
        P("ep", None, "tp"),
        P("ep", None, "tp"),
        P("ep", "tp", None),
    )
    return jax.shard_map(
        per_device, mesh=mesh, in_specs=in_specs, out_specs=out_specs, check_vma=False
    )
```

```python
import functools

import jax
import jax.numpy as jnp
from jax import lax
from jax.experimental import pallas as pl
from jax.experimental.pallas import tpu as pltpu
from jax.sharding import PartitionSpec as P

D = 2048
DN = 128
DR = 64
DV = 128
KVR = 512
TOPK = 6
EXP_DEV = 2
MAIN = 32

epsilon = 1e-06
route_scale = 2.446
rope_base = 50000.0
masked_fill = -1000000000.0

bf16 = jnp.bfloat16
f32 = jnp.float32


def matmul(left_mat, right_mat):
    return jnp.dot(left_mat, right_mat, preferred_element_type=f32)


def matmul_nt(left_mat, right_mat):
    return lax.dot_general(
        left_mat, right_mat, (((1,), (1,)), ((), ())), preferred_element_type=f32
    )


def matmul_tn(left_mat, right_mat):
    return lax.dot_general(
        left_mat, right_mat, (((0,), (0,)), ((), ())), preferred_element_type=f32
    )


def rms_scale(values):
    return lax.rsqrt(jnp.mean(values * values, -1, keepdims=True) + epsilon)


def rms_back(values, scale_vals, gain_vec, upstream):
    weighted = upstream * gain_vec
    inner_mean = jnp.mean(weighted * values, -1, keepdims=True)
    grad_in = scale_vals * weighted - values * scale_vals * scale_vals * scale_vals * inner_mean
    grad_gain = jnp.sum(upstream * values * scale_vals, 0)
    return (grad_in, grad_gain)


def rope_tables(row_count):
    half_dim = DR // 2
    freq_vec = rope_base ** (-(jnp.arange(half_dim, dtype=f32) * (2.0 / DR)))
    angle_tab = jnp.arange(row_count, dtype=f32)[:, None] * freq_vec[None, :]
    return (jnp.cos(angle_tab), jnp.sin(angle_tab))


def rotate(values, cos_tab, sine_tab):
    half_dim = values.shape[-1] // 2
    first_half = values[..., :half_dim]
    second_half = values[..., half_dim:]
    return jnp.concatenate(
        [
            first_half * cos_tab - second_half * sine_tab,
            second_half * cos_tab + first_half * sine_tab,
        ],
        -1,
    )


def shift(value, step):
    lanes = lax.axis_size("tp")
    return lax.ppermute(value, "tp", [(i, (i + step) % lanes) for i in range(lanes)])


def quarter_of(value, step):
    lanes = lax.axis_size("tp")
    width = value.shape[1] // lanes
    lane = lax.rem(lax.axis_index("tp") + step, lanes)
    return lax.dynamic_slice_in_dim(value, lane * width, width, 1)


def sum_to_quarter(partial):
    low = partial.astype(bf16)
    total = quarter_of(low, 0).astype(f32)
    for step in (1, 3, 2):
        total = total + shift(quarter_of(low, step), step).astype(f32)
    return total


def gather_quarters(piece):
    lanes = lax.axis_size("tp")
    lane = lax.axis_index("tp")
    parts = [piece] + [None] * (lanes - 1)
    for step in (1, 3, 2):
        parts[step] = shift(piece, lanes - step)
    full = jnp.concatenate(parts, 1)
    width = piece.shape[1]
    parts = []
    for step in range(lanes):
        at = lax.rem(lanes - lane + step, lanes) * width
        parts.append(lax.dynamic_slice_in_dim(full, at, width, 1))
    return jnp.concatenate(parts, 1)


def sum_small(partial):
    total = partial.astype(f32)
    for step in (1, 3, 2):
        total = total + shift(partial, step).astype(f32)
    return total


def exchange(value):
    return lax.all_to_all(value, "ep", 0, 0, tiled=True)


def to_experts(value):
    blocks = value.shape[0]
    rest = value.shape[2:]
    return jnp.concatenate(
        [
            value[:, :MAIN].reshape(blocks * MAIN, *rest),
            value[:, MAIN:-MAIN].reshape(-1, *rest),
            value[:, -MAIN:].reshape(blocks * MAIN, *rest),
        ],
        0,
    )


def from_experts(value, blocks):
    rest = value.shape[1:]
    edge = blocks * MAIN
    return jnp.concatenate(
        [
            value[:edge].reshape(blocks, MAIN, *rest),
            value[edge:-edge].reshape(blocks, -1, *rest),
            value[-edge:].reshape(blocks, MAIN, *rest),
        ],
        1,
    )


def after(value, *others):
    return lax.optimization_barrier((value, others))[0]


def plus(one, two):
    return (one.astype(f32) + two.astype(f32)).astype(bf16)


def ring_gather_first(one, two):
    return shift(one, 1), shift(two, 3), shift(two, 1), shift(one, 3)


def ring_gather_second(first):
    return shift(first[0], 1), shift(first[1], 3)


def ring_gather_parts(one, two, first, second):
    one_prev, two_next, two_prev, one_next = first
    return (one, two, one_next, two_next, second[0], second[1], one_prev, two_prev)


def add_three(one, two, three):
    return (one.astype(f32) + two.astype(f32) + three.astype(f32)).astype(bf16)


VMEM_BYTES = 44 * 1024 * 1024


def first_owner_rows(tiles, tile, spill):
    row = lax.broadcasted_iota(jnp.int32, (tile, 1), 0) + (pl.program_id(0) - tiles[0]) * tile
    return lax.rem(row, EXP_DEV * spill) < spill


def per_owner(tiles, tile, spill, run):
    first, mixed = tiles
    step = pl.program_id(0)
    mine = first_owner_rows(tiles, tile, spill)
    is_mixed = (step >= first) & (step < first + mixed)

    @pl.when(is_mixed)
    def _():
        run(None, mine)

    @pl.when(jnp.logical_not(is_mixed))
    def _():
        run(jnp.where(step < first, 0, 1), None)


def hidden_back_kernel(tiles, spill, *refs):
    pieces, weight, out = refs[:-2], refs[-2], refs[-1]
    rows = jnp.concatenate([p[...] for p in pieces], 1)

    def run(owner, mine):
        if owner is None:
            out[...] = jnp.where(mine, matmul_nt(rows, weight[0]), matmul_nt(rows, weight[1]))
        else:
            out[...] = matmul_nt(rows, weight[owner])

    per_owner(tiles, rows.shape[0], spill, run)


def hidden_kernel(tiles, spill, *refs):
    pieces, (weight, dh_ref, gate_ref, hid, dboth, dgate), refs = refs[:8], refs[8:14], refs[14:]
    drow, acc = refs[:8], refs[8]
    rows = jnp.concatenate([p[...] for p in pieces], 1)

    def run(owner, mine):
        if owner is None:
            acc[...] = jnp.where(mine, matmul(rows, weight[0]), matmul(rows, weight[1]))
        else:
            acc[...] = matmul(rows, weight[owner])

    per_owner(tiles, rows.shape[0], spill, run)
    wide = hid.shape[1]
    up = acc[:, wide:]
    pre = acc[:, :wide]
    sig = 1.0 / (1.0 + jnp.exp(-pre))
    act = pre * sig
    hidden = (act * up).astype(bf16).astype(f32)
    gate = gate_ref[...]
    dh = dh_ref[...]
    dgate[...] = jnp.sum(hidden * dh, 1, keepdims=True)
    hid[...] = (hidden * gate).astype(bf16)
    dh = dh * gate
    dboth[:, :wide] = (dh * up * (sig * (1.0 + pre * (1.0 - sig)))).astype(bf16)
    dboth[:, wide:] = (dh * act).astype(bf16)

    def back(owner, mine):
        grad = dboth[...]
        cols = drow[0].shape[1]
        none = jnp.zeros_like(grad)
        for j, out in enumerate(drow):
            at = slice(j * cols, (j + 1) * cols)
            if owner is None:
                total = matmul_nt(jnp.where(mine, grad, none), weight[0, at, :])
                total = total + matmul_nt(jnp.where(mine, none, grad), weight[1, at, :])
            else:
                total = matmul_nt(grad, weight[owner, at, :])
            out[...] = total.astype(bf16)

    per_owner(tiles, rows.shape[0], spill, back)


def out_kernel(tiles, spill, value, weight, *outs):
    def run(owner, mine):
        rows = value[...]
        none = jnp.zeros_like(rows)
        for j, out in enumerate(outs):
            at = slice(j * out.shape[1], (j + 1) * out.shape[1])
            if owner is None:
                total = matmul(jnp.where(mine, rows, none), weight[0, :, at])
                total = total + matmul(jnp.where(mine, none, rows), weight[1, :, at])
            else:
                total = matmul(rows, weight[owner, :, at])
            out[...] = total.astype(bf16)

    per_owner(tiles, value.shape[0], spill, run)


def tile_spec(tile, width):
    return pl.BlockSpec((tile, width), lambda i: (i, 0))


def whole_spec(shape):
    return pl.BlockSpec(shape, lambda i: (0,) * len(shape))


def row_call(body, tile, total, ins, in_specs, outs, flops, scratch=()):
    out_shape = [jax.ShapeDtypeStruct((total, w), t) for w, t in outs]
    moved = sum(a.size * a.dtype.itemsize for a in (*ins, *out_shape))
    return pl.pallas_call(
        body,
        grid=(total // tile,),
        in_specs=in_specs,
        out_specs=[tile_spec(tile, w) for w, _ in outs],
        out_shape=out_shape,
        scratch_shapes=list(scratch),
        cost_estimate=pl.CostEstimate(flops=flops, bytes_accessed=moved, transcendentals=0),
        compiler_params=pltpu.CompilerParams(
            dimension_semantics=("arbitrary",), vmem_limit_bytes=VMEM_BYTES
        ),
    )(*ins)


def first_grad_kernel(
    kv_rows,
    normed,
    normed2,
    dmid,
    dquery,
    dlat,
    dlogits,
    attended,
    latent_n,
    dkeyval,
    gains,
    out,
    kv_grad,
):
    step = pl.program_id(0)

    @pl.when(step == 0)
    def _():
        kv_grad[...] = matmul_tn(latent_n[...], dkeyval[...]).astype(bf16)

    rows, kv_cols = out.shape[0], 256
    at_lat = dquery.shape[1]
    at_kv = at_lat + dlat.shape[1]
    at_out = at_kv + kv_cols
    at_gain = at_out + attended.shape[1]
    mine = normed[...]
    out[:, :at_lat] = matmul_tn(mine, dquery[...]).astype(bf16)
    out[:, at_lat:at_kv] = (
        matmul_tn(mine, dlat[...]) + matmul_tn(normed2[...], dlogits[...])
    ).astype(bf16)
    out[:, at_out:at_gain] = matmul_tn(dmid[...], attended[...]).astype(bf16)
    out[:, at_gain:] = gains[...]
    splits = kv_grad.shape[1] // kv_cols
    count = rows // kv_rows
    for j in range(count):
        if count % splits == 0:
            group = step * (count // splits) + j // splits
            lanes = slice(j % splits * kv_cols, (j % splits + 1) * kv_cols)
        else:
            group = (step * count + j) // splits
            lanes = pl.ds((step * count + j) % splits * kv_cols, kv_cols)
        from_rows = pl.ds(pl.multiple_of(group * kv_rows, kv_rows), kv_rows)
        out[j * kv_rows : (j + 1) * kv_rows, at_kv:at_out] = kv_grad[from_rows, lanes]


def first_grads(kv_rows, normed, normed2, dmid, dquery, dlat, dlogits, attended, latent_n, dkeyval, gains):
    block = 256
    cols = pl.BlockSpec((normed.shape[0], block), lambda i: (0, i))
    width = dquery.shape[1] + dlat.shape[1] + 256 + attended.shape[1] + gains.shape[1]
    whole = (dquery, dlat, dlogits, attended, latent_n, dkeyval)
    return pl.pallas_call(
        functools.partial(first_grad_kernel, kv_rows),
        grid=(D // block,),
        in_specs=[cols, cols, cols]
        + [whole_spec(a.shape) for a in whole]
        + [tile_spec(block, gains.shape[1])],
        out_specs=tile_spec(block, width),
        out_shape=jax.ShapeDtypeStruct((D, width), bf16),
        scratch_shapes=[pltpu.VMEM((KVR, dkeyval.shape[1]), bf16)],
        cost_estimate=pl.CostEstimate(
            flops=2 * D * width * normed.shape[0], bytes_accessed=3 * D * width, transcendentals=0
        ),
        compiler_params=pltpu.CompilerParams(
            dimension_semantics=("arbitrary",), vmem_limit_bytes=VMEM_BYTES
        ),
    )(normed, normed2, dmid, *whole, gains)


def second_grad_kernel(normed2, cotangent, dboth, hidden, out):
    split = dboth.shape[1]
    out[:, :split] = matmul_tn(normed2[...], dboth[...]).astype(bf16)
    out[:, split:] = matmul_tn(cotangent[...], hidden[...]).astype(bf16)


def second_grads(normed2, cotangent, dboth, hidden):
    block = 256
    cols = pl.BlockSpec((normed2.shape[0], block), lambda i: (0, i))
    width = dboth.shape[1] + hidden.shape[1]
    return pl.pallas_call(
        second_grad_kernel,
        grid=(D // block,),
        in_specs=[cols, cols, whole_spec(dboth.shape), whole_spec(hidden.shape)],
        out_specs=tile_spec(block, width),
        out_shape=jax.ShapeDtypeStruct((D, width), bf16),
        cost_estimate=pl.CostEstimate(
            flops=2 * D * width * normed2.shape[0], bytes_accessed=3 * D * width, transcendentals=0
        ),
        compiler_params=pltpu.CompilerParams(
            dimension_semantics=("arbitrary",), vmem_limit_bytes=VMEM_BYTES
        ),
    )(normed2, cotangent, dboth, hidden)


def per_device(
    tokens,
    expert_ids,
    route_slots,
    doc_ids,
    prenorm,
    query_w,
    latent_w,
    latnorm,
    keyval_w,
    output_w,
    midnorm,
    router_w,
    shgate_w,
    shup_w,
    shdown_w,
    exgate_w,
    exup_w,
    exdown_w,
    cotangent,
):
    owner_count = lax.axis_size("ep")
    experts = owner_count * EXP_DEV
    tok_count = tokens.shape[0]
    capacity = 2 * tok_count * TOPK // experts
    spill = capacity - MAIN
    width = EXP_DEV * capacity
    slot_rows = owner_count * width
    head_count = query_w.shape[1] // (DN + DR)
    score_scale = (DN + DR) ** (-0.5)
    shard = query_w.shape[0]
    q_cols = query_w.shape[1]
    lat_cols = latent_w.shape[1]
    kv_rows = keyval_w.shape[0]
    kv_cols = kv_rows * keyval_w.shape[1] // shard
    out_cols = output_w.shape[0]
    sh_cols = shgate_w.shape[1]

    gains = jnp.stack(
        [prenorm, jnp.pad(latnorm, (0, shard - latnorm.shape[0])), midnorm], 1
    )
    gains = jnp.pad(gains, ((0, 0), (0, 128 - gains.shape[1])))
    first_pack = jnp.concatenate(
        [
            query_w,
            latent_w,
            router_w,
            keyval_w.reshape(kv_rows, -1, kv_cols).transpose(1, 0, 2).reshape(shard, kv_cols),
            output_w.T,
            gains,
        ],
        1,
    )
    first_full = lax.all_gather(first_pack, "ep", axis=0, tiled=True)
    local = expert_ids % EXP_DEV
    inside = jnp.where(
        route_slots < MAIN,
        local * (MAIN + EXP_DEV * spill) + route_slots,
        MAIN + local * spill + (route_slots - MAIN),
    )
    place = (expert_ids // EXP_DEV) * width + inside
    row_iota = lax.broadcasted_iota(jnp.int32, (slot_rows, tok_count), 0)
    matches = [row_iota == place[:, k][None, :] for k in range(TOPK)]
    pick = matches[0]
    for k in range(1, TOPK):
        pick = pick | matches[k]
    pick = pick.astype(bf16)

    half = D // 8
    dy_sent = matmul(pick, quarter_of(cotangent, 0)).astype(bf16)
    dy_sent = to_experts(exchange(dy_sent.reshape(owner_count, width, -1)))
    lanes = lax.axis_size("tp")
    lane = lax.axis_index("tp")
    quarter = D // lanes
    hid_cols = exgate_w.shape[2]
    hid_wide = -(-hid_cols // 128) * 128

    def from_lane(value, axis):
        parts = []
        for step in range(lanes):
            at = lax.rem(lane + step, lanes) * quarter
            parts.append(lax.dynamic_slice_in_dim(value, at, quarter, axis))
        return jnp.concatenate(parts, axis)

    def to_lane(value, axis):
        parts = []
        for step in range(lanes):
            at = lax.rem(lanes - lane + step, lanes) * quarter
            parts.append(lax.dynamic_slice_in_dim(value, at, quarter, axis))
        return jnp.concatenate(parts, axis)

    fill = hid_wide - hid_cols
    gateup_w = jnp.concatenate(
        [
            jnp.pad(from_lane(exgate_w, 1), ((0, 0), (0, 0), (0, fill))),
            jnp.pad(from_lane(exup_w, 1), ((0, 0), (0, 0), (0, fill))),
        ],
        2,
    )
    down_plain = jnp.pad(exdown_w, ((0, 0), (0, fill), (0, 0)))
    down_w = jnp.pad(from_lane(exdown_w, 2), ((0, 0), (0, fill), (0, 0)))
    edge = owner_count * MAIN
    extra = slot_rows - 2 * edge
    span = edge + extra
    tile = 256 if edge % 256 == 0 else 128
    tiles = (edge // tile, extra // tile)
    big = 2 * (slot_rows + extra) * D * hid_wide
    first_full, dy_sent, gateup_w, down_w, down_plain = lax.optimization_barrier(
        (first_full, dy_sent, gateup_w, down_w, down_plain)
    )
    dy_all = lax.all_gather(after(dy_sent, first_full), "tp", axis=0, tiled=True)
    edges = [0]
    for cols in (q_cols, lat_cols, experts, kv_cols, out_cols, 128):
        edges.append(edges[-1] + cols)
    query_full = first_full[:, edges[0] : edges[1]]
    latent_full = first_full[:, edges[1] : edges[2]]
    router_full = first_full[:, edges[2] : edges[3]]
    keyval_full = first_full[:, edges[3] : edges[4]].reshape(owner_count, -1, kv_rows, kv_cols)
    keyval_full = keyval_full.transpose(0, 2, 1, 3).reshape(KVR, keyval_w.shape[1])
    output_t = first_full[:, edges[4] : edges[5]]
    pre_gain = first_full[:, edges[5]]
    lat_gain = first_full[:, edges[5] + 1].reshape(owner_count, shard)[:, : latnorm.shape[0]]
    lat_gain = lat_gain.reshape(KVR)
    mid_gain = first_full[:, edges[5] + 2]


    resid_in = tokens.astype(f32)
    pre_scale = rms_scale(resid_in)
    pre_weight = pre_gain.astype(f32)
    normed = (resid_in * pre_scale * pre_weight).astype(bf16)
    query_raw = matmul(normed, query_full).reshape(tok_count, head_count, DN + DR)
    latent_all = matmul(normed, latent_full)
    latent = latent_all[:, :KVR]
    lat_scale = rms_scale(latent)
    lat_weight = lat_gain.astype(f32)
    latent_n = (latent * lat_scale * lat_weight).astype(bf16)
    keyval = matmul(latent_n, keyval_full).astype(bf16).reshape(tok_count, head_count, DN + DV)
    cos_tab, sine_tab = rope_tables(tok_count)
    q_all = jnp.concatenate(
        [
            query_raw[..., :DN],
            rotate(query_raw[..., DN:], cos_tab[:, None, :], sine_tab[:, None, :]),
        ],
        -1,
    ).astype(bf16)
    key_rot = rotate(latent_all[:, KVR:], cos_tab, sine_tab).astype(bf16)
    key_all = jnp.concatenate(
        [keyval[..., :DN], jnp.broadcast_to(key_rot[:, None, :], (tok_count, head_count, DR))], -1
    )
    values = keyval[..., DN:]
    position = jnp.arange(tok_count)
    doc_row = doc_ids[0]
    allowed = ((doc_row[:, None] == doc_row[None, :]) & (position[:, None] >= position[None, :]))[
        None
    ]
    raw_scores = (
        jnp.einsum("thd,shd->hts", q_all, key_all, preferred_element_type=f32) * score_scale
    )
    masked = jnp.where(allowed, raw_scores, masked_fill)
    row_max = jnp.max(masked, -1, keepdims=True)
    exp_scores = jnp.exp(masked - row_max)
    softmax_sum = jnp.sum(exp_scores, -1, keepdims=True)
    probs = exp_scores / softmax_sum
    probs16 = probs.astype(bf16)
    attended = jnp.einsum("hts,shd->thd", probs16, values, preferred_element_type=f32)
    attended = attended.reshape(tok_count, head_count * DV).astype(bf16)
    attn_sum = gather_quarters(sum_to_quarter(matmul_nt(attended, output_t)).astype(bf16))
    mid_resid = resid_in + attn_sum.astype(f32)
    mid_scale = rms_scale(mid_resid)
    mid_weight = mid_gain.astype(f32)
    normed2 = (mid_resid * mid_scale * mid_weight).astype(bf16)

    sent = matmul(pick, quarter_of(normed2, 0)).astype(bf16).reshape(owner_count, width, -1)
    one = exchange(sent[:, :, :half])
    two = exchange(after(sent[:, :, half:], one))
    second_pack = jnp.concatenate([shgate_w, shup_w, shdown_w.T], 1)
    second_full = lax.all_gather(after(second_pack, dy_all, one), "ep", axis=0, tiled=True)
    own = (to_experts(one), to_experts(two))
    first = ring_gather_first(*own)
    dy_all = after(dy_all, two)
    (ex_dh,) = row_call(
        functools.partial(hidden_back_kernel, tiles, spill),
        tile,
        slot_rows,
        (*[dy_all] * lanes, down_plain),
        [
            pl.BlockSpec((tile, quarter), lambda i, q=q: (q * (slot_rows // tile) + i, 0))
            for q in range(lanes)
        ]
        + [whole_spec(down_plain.shape)],
        [(hid_wide, f32)],
        big,
    )

    upstream = cotangent.astype(f32)
    sh_in, sh_dy = after((normed2, cotangent), two)
    gateup_full = second_full[:, : 2 * sh_cols]
    shdown_t = second_full[:, 2 * sh_cols :]
    sh_both = matmul(sh_in, gateup_full)
    sh_gate = sh_both[:, :sh_cols]
    sh_up = sh_both[:, sh_cols:]
    sh_sig = 1.0 / (1.0 + jnp.exp(-sh_gate))
    sh_hidden = (sh_gate * sh_sig * sh_up).astype(bf16)
    shared_part = matmul_nt(sh_hidden, shdown_t).astype(bf16)
    sh_dhidden = matmul(sh_dy, shdown_t)
    sh_dgate = (sh_dhidden * sh_up * sh_sig * (1.0 + sh_gate * (1.0 - sh_sig))).astype(bf16)
    sh_dup = (sh_dhidden * sh_gate * sh_sig).astype(bf16)
    sh_dboth = jnp.concatenate([sh_dgate, sh_dup], 1)
    sh_dnormed_part = matmul_nt(sh_dboth, gateup_full).astype(bf16)
    second_grad = second_grads(normed2, cotangent, sh_dboth, sh_hidden)
    second_sum = lax.psum_scatter(second_grad, "ep", scatter_dimension=0, tiled=True)

    going, shared_part, sh_dnormed_part, second_grad = lax.optimization_barrier(
        (first[:2], shared_part, sh_dnormed_part, second_grad)
    )
    first = (*going, *first[2:])
    shared_q = sum_to_quarter(shared_part)
    sh_dnormed_q = sum_to_quarter(sh_dnormed_part)
    rows = ring_gather_parts(*own, first, ring_gather_second(first))

    logits = matmul(normed2, router_full)
    onehot = (
        expert_ids[:, :, None] == jnp.arange(experts, dtype=jnp.int32)[None, None, :]
    ).astype(f32)
    chosen = jnp.sum(onehot * logits[:, None, :], -1)
    sel_vals = 1.0 / (1.0 + jnp.exp(-chosen))
    sel_total = jnp.sum(sel_vals, -1, keepdims=True)
    gate_vals = route_scale * sel_vals / sel_total
    gate_rows = jnp.zeros((slot_rows, tok_count), f32)
    for k in range(TOPK):
        gate_rows = gate_rows + jnp.where(matches[k], gate_vals[:, k][None, :], 0.0)
    gate_rows = jnp.sum(gate_rows, 1).reshape(owner_count, width)
    gate_rows = to_experts(exchange(after(gate_rows, two)))[:, None]

    ex_hidden, ex_dboth, dgate_rows, *drow = row_call(
        functools.partial(hidden_kernel, tiles, spill),
        tile,
        slot_rows,
        (*rows, gateup_w, ex_dh, gate_rows),
        [tile_spec(tile, half)] * 8
        + [whole_spec(gateup_w.shape), tile_spec(tile, hid_wide), tile_spec(tile, 1)],
        [(hid_wide, bf16), (2 * hid_wide, bf16), (1, f32)] + [(half, bf16)] * 8,
        4 * big,
        [pltpu.VMEM((tile, 2 * hid_wide), f32)],
    )

    extra_iota = lax.broadcasted_iota(jnp.int32, (span, 1), 0)
    owned = (
        (extra_iota < edge) | ((extra_iota - edge) % (EXP_DEV * spill) < spill),
        (extra_iota >= extra) | (extra_iota % (EXP_DEV * spill) >= spill),
    )

    def expert_rows(value, e):
        return value[:span] if e == 0 else value[edge:]

    def grads_of(e, left, right, cols):
        kept = jnp.where(owned[e], expert_rows(right, e)[:, cols], jnp.zeros((), bf16))
        return matmul_tn(expert_rows(left, e), kept)

    def grads_of_down(late):
        wide_dy = after(dy_all, late).reshape(lanes, slot_rows, quarter)
        wide_dy = jnp.concatenate([wide_dy[q] for q in range(lanes)], 1)
        hidden = after(ex_hidden[:, :hid_cols], late)
        parts = []
        for e in range(EXP_DEV):
            kept = jnp.where(owned[e], expert_rows(hidden, e), jnp.zeros((), bf16))
            parts.append(matmul_tn(kept, expert_rows(wide_dy, e)))
        return jnp.stack(parts)

    def bring_back(one, two):
        back_one = exchange(from_experts(one, owner_count)).reshape(slot_rows, -1)
        back_two = exchange(from_experts(two, owner_count)).reshape(slot_rows, -1)
        return jnp.concatenate([matmul_tn(pick, back_one), matmul_tn(pick, back_two)], 1)

    out_parts = row_call(
        functools.partial(out_kernel, tiles, spill),
        tile,
        slot_rows,
        (ex_hidden, down_w),
        [tile_spec(tile, hid_wide), whole_spec(down_w.shape)],
        [(half, bf16)] * 8,
        big,
    )
    top = shift(drow[4], 1)
    bottom = shift(drow[5], 3)
    dgate_rows = exchange(from_experts(dgate_rows[:, 0], owner_count)).reshape(-1)
    top, bottom, dgate_rows, out_parts = lax.optimization_barrier(
        (top, bottom, dgate_rows, out_parts)
    )
    from_prev_one = shift(plus(drow[2], top), 1)
    from_next_one = shift(after(drow[6], bottom), 3)
    next_two, prev_two = after(
        (drow[3], plus(drow[7], bottom)), from_prev_one, from_next_one
    )
    from_prev_two = shift(next_two, 1)
    from_next_two = shift(prev_two, 3)
    drow_one = add_three(drow[0], from_prev_one, from_next_one)
    drow_two = add_three(drow[1], from_prev_two, from_next_two)
    routed_grad_q = bring_back(drow_one, drow_two)
    out_far = after(tuple(out_parts[4:6]), drow_two)
    out_top = shift(out_far[0], 1)
    out_bottom = shift(out_far[1], 3)

    dgate_part = jnp.stack(
        [jnp.sum(jnp.where(matches[k], dgate_rows[:, None], 0.0), 0) for k in range(TOPK)], 1
    )
    dgate_all = sum_small(dgate_part)
    weighted = jnp.sum(dgate_all * gate_vals, -1, keepdims=True) / route_scale
    dsel_vals = route_scale / sel_total * (dgate_all - weighted)
    dchosen = dsel_vals * sel_vals * (1.0 - sel_vals)
    dlogits = jnp.sum(onehot * dchosen[:, :, None], 1).astype(bf16)
    dnormed2 = gather_quarters((routed_grad_q + sh_dnormed_q).astype(bf16)).astype(f32)
    dnormed2 = dnormed2 + matmul_nt(dlogits, router_full)
    dmid_norm, midnorm_grad = rms_back(mid_resid, mid_scale, mid_weight, dnormed2)
    dmid = upstream + dmid_norm
    dmid16 = dmid.astype(bf16)
    dattended = matmul(dmid16, output_t).astype(bf16).reshape(tok_count, head_count, DV)
    dprobs = jnp.einsum("thd,shd->hts", dattended, values, preferred_element_type=f32)
    dscores = (probs * (dprobs - jnp.sum(probs * dprobs, -1, keepdims=True))).astype(bf16)
    dq_all = (
        jnp.einsum("hts,shd->thd", dscores, key_all, preferred_element_type=f32) * score_scale
    )
    dkey_all = jnp.einsum("hts,thd->shd", dscores, q_all, preferred_element_type=f32) * score_scale
    dvalues = jnp.einsum("hts,thd->shd", probs16, dattended, preferred_element_type=f32)
    dquery = jnp.concatenate(
        [dq_all[..., :DN], rotate(dq_all[..., DN:], cos_tab[:, None, :], -sine_tab[:, None, :])], -1
    )
    dquery = dquery.reshape(tok_count, head_count * (DN + DR)).astype(bf16)
    dkeyval = (
        jnp.concatenate([dkey_all[..., :DN], dvalues], -1)
        .reshape(tok_count, head_count * (DN + DV))
        .astype(bf16)
    )
    dlatent_part = matmul_nt(dkeyval, keyval_full)
    dkey_part = jnp.sum(dkey_all[..., DN:], 1)
    dlat_part = jnp.concatenate([dlatent_part, dkey_part], 1).astype(bf16)
    dlat_sum = sum_small(dlat_part)
    dlat_sum, second_sum, out_top, out_bottom = lax.optimization_barrier(
        (dlat_sum, second_sum, out_top, out_bottom)
    )
    dlatent, latnorm_grad = rms_back(latent, lat_scale, lat_weight, dlat_sum[:, :KVR])
    dlatent_all = jnp.concatenate(
        [dlatent, rotate(dlat_sum[:, KVR:], cos_tab, -sine_tab)], -1
    ).astype(bf16)
    gain_grads = jnp.stack(
        [
            jnp.pad(
                latnorm_grad.reshape(owner_count, -1),
                ((0, 0), (0, shard - latnorm.shape[0])),
            ).reshape(-1),
            midnorm_grad,
        ],
        1,
    )
    gain_grads = jnp.pad(gain_grads, ((0, 0), (0, 128 - gain_grads.shape[1])))
    first_grad = first_grads(
        kv_rows,
        normed,
        normed2,
        dmid16,
        dquery,
        jnp.pad(dlatent_all, ((0, 0), (0, experts))),
        jnp.pad(dlogits, ((0, 0), (lat_cols, 0))),
        attended,
        latent_n,
        dkeyval,
        gain_grads.astype(bf16),
    )
    out_late = after((*out_parts, out_top, out_bottom), first_grad)
    out_prev_one = shift(plus(out_late[2], out_late[8]), 1)
    out_next_one = shift(out_late[6], 3)
    out_prev_two, out_next_two = after(
        (out_late[3], plus(out_late[7], out_late[9])), out_prev_one, out_next_one
    )
    out_prev_two = shift(out_prev_two, 1)
    out_next_two = shift(out_next_two, 3)
    out_one = add_three(out_parts[0], out_prev_one, out_next_one)
    out_two = add_three(out_parts[1], out_prev_two, out_next_two)
    back_one = exchange(from_experts(out_one, owner_count))
    out_two = after(out_two, back_one)
    back_two = exchange(from_experts(out_two, owner_count))
    routed_q = jnp.concatenate(
        [matmul_tn(pick, b.reshape(slot_rows, -1)) for b in (back_one, back_two)], 1
    )
    late_dquery, late_dlat = after((dquery, dlatent_all), out_prev_one, out_next_one)
    dnormed_q = sum_to_quarter(matmul_nt(late_dquery, query_full))
    dnormed = gather_quarters(dnormed_q.astype(bf16)).astype(f32) + matmul_nt(
        late_dlat, latent_full
    )
    dtokens, prenorm_grad = rms_back(resid_in, pre_scale, pre_weight, dnormed)
    tokens_grad = (dmid + dtokens).astype(bf16)
    prenorm_sum = jnp.sum(exchange(prenorm_grad.reshape(owner_count, shard)), 0)
    down_grad = grads_of_down(back_one)
    all_rows = jnp.concatenate(after(rows, back_one), 1)
    late_dboth = after(ex_dboth, back_one)
    exgate_grad = jnp.stack(
        [grads_of(e, all_rows, late_dboth, slice(0, hid_cols)) for e in range(EXP_DEV)]
    )
    exup_grad = jnp.stack(
        [
            grads_of(e, all_rows, late_dboth, slice(hid_wide, hid_wide + hid_cols))
            for e in range(EXP_DEV)
        ]
    )
    exgate_grad = to_lane(exgate_grad, 1)
    exup_grad = to_lane(exup_grad, 1)
    layer_q = (quarter_of(mid_resid, 0) + routed_q + shared_q).astype(bf16)
    layer_out = gather_quarters(layer_q)
    first_sum = lax.psum_scatter(first_grad, "ep", scatter_dimension=0, tiled=True).astype(f32)
    second_sum = second_sum.astype(f32)
    return (
        layer_out,
        tokens_grad,
        prenorm_sum,
        first_sum[:, edges[0] : edges[1]],
        first_sum[:, edges[1] : edges[2]],
        first_sum[: latnorm.shape[0], edges[5]],
        first_sum[:, edges[3] : edges[4]]
        .reshape(-1, kv_rows, kv_cols)
        .transpose(1, 0, 2)
        .reshape(keyval_w.shape),
        first_sum[:, edges[4] : edges[5]].T,
        first_sum[:, edges[5] + 1],
        first_sum[:, edges[2] : edges[3]],
        second_sum[:, :sh_cols],
        second_sum[:, sh_cols : 2 * sh_cols],
        second_sum[:, 2 * sh_cols :].T,
        exgate_grad,
        exup_grad,
        down_grad,
    )


def solution(mesh):
    in_specs = (
        P("ep", None),
        P("ep", None),
        P("ep", None),
        P("ep", None),
        P("ep"),
        P("ep", "tp"),
        P("ep", None),
        P("ep"),
        P("ep", "tp"),
        P("tp", "ep"),
        P("ep"),
        P("ep", None),
        P("ep", "tp"),
        P("ep", "tp"),
        P("tp", "ep"),
        P("ep", None, "tp"),
        P("ep", None, "tp"),
        P("ep", "tp", None),
        P("ep", None),
    )
    out_specs = (
        P("ep", None),
        P("ep", None),
        P("ep"),
        P("ep", "tp"),
        P("ep", None),
        P("ep"),
        P("ep", "tp"),
        P("tp", "ep"),
        P("ep"),
        P("ep", None),
        P("ep", "tp"),
        P("ep", "tp"),
        P("tp", "ep"),
        P("ep", None, "tp"),
        P("ep", None, "tp"),
        P("ep", "tp", None),
    )
    return jax.shard_map(
        per_device, mesh=mesh, in_specs=in_specs, out_specs=out_specs, check_vma=False
    )
```

```python
import functools

import jax
import jax.numpy as jnp
from jax import lax
from jax.experimental import pallas as pl
from jax.experimental.pallas import tpu as pltpu
from jax.sharding import PartitionSpec as P

D = 2048
DN = 128
DR = 64
DV = 128
KVR = 512
TOPK = 6
EXP_DEV = 2
MAIN = 32

epsilon = 1e-06
route_scale = 2.446
rope_base = 50000.0
masked_fill = -1000000000.0

bf16 = jnp.bfloat16
f32 = jnp.float32


def matmul(left_mat, right_mat):
    return jnp.dot(left_mat, right_mat, preferred_element_type=f32)


def matmul_nt(left_mat, right_mat):
    return lax.dot_general(
        left_mat, right_mat, (((1,), (1,)), ((), ())), preferred_element_type=f32
    )


def matmul_tn(left_mat, right_mat):
    return lax.dot_general(
        left_mat, right_mat, (((0,), (0,)), ((), ())), preferred_element_type=f32
    )


def rms_scale(values):
    return lax.rsqrt(jnp.mean(values * values, -1, keepdims=True) + epsilon)


def rms_back(values, scale_vals, gain_vec, upstream):
    weighted = upstream * gain_vec
    inner_mean = jnp.mean(weighted * values, -1, keepdims=True)
    grad_in = scale_vals * weighted - values * scale_vals * scale_vals * scale_vals * inner_mean
    grad_gain = jnp.sum(upstream * values * scale_vals, 0)
    return (grad_in, grad_gain)


def rope_tables(row_count):
    half_dim = DR // 2
    freq_vec = rope_base ** (-(jnp.arange(half_dim, dtype=f32) * (2.0 / DR)))
    angle_tab = jnp.arange(row_count, dtype=f32)[:, None] * freq_vec[None, :]
    return (jnp.cos(angle_tab), jnp.sin(angle_tab))


def rotate(values, cos_tab, sine_tab):
    half_dim = values.shape[-1] // 2
    first_half = values[..., :half_dim]
    second_half = values[..., half_dim:]
    return jnp.concatenate(
        [
            first_half * cos_tab - second_half * sine_tab,
            second_half * cos_tab + first_half * sine_tab,
        ],
        -1,
    )


def shift(value, step):
    lanes = lax.axis_size("tp")
    return lax.ppermute(value, "tp", [(i, (i + step) % lanes) for i in range(lanes)])


def quarter_of(value, step):
    lanes = lax.axis_size("tp")
    width = value.shape[1] // lanes
    lane = lax.rem(lax.axis_index("tp") + step, lanes)
    return lax.dynamic_slice_in_dim(value, lane * width, width, 1)


def sum_to_quarter(partial):
    low = partial.astype(bf16)
    total = quarter_of(low, 0).astype(f32)
    for step in (1, 3, 2):
        total = total + shift(quarter_of(low, step), step).astype(f32)
    return total


def gather_quarters(piece):
    lanes = lax.axis_size("tp")
    lane = lax.axis_index("tp")
    parts = [piece] + [None] * (lanes - 1)
    for step in (1, 3, 2):
        parts[step] = shift(piece, lanes - step)
    full = jnp.concatenate(parts, 1)
    width = piece.shape[1]
    parts = []
    for step in range(lanes):
        at = lax.rem(lanes - lane + step, lanes) * width
        parts.append(lax.dynamic_slice_in_dim(full, at, width, 1))
    return jnp.concatenate(parts, 1)


def sum_small(partial):
    total = partial.astype(f32)
    for step in (1, 3, 2):
        total = total + shift(partial, step).astype(f32)
    return total


def exchange(value):
    return lax.all_to_all(value, "ep", 0, 0, tiled=True)


def to_experts(value):
    blocks = value.shape[0]
    rest = value.shape[2:]
    return jnp.concatenate(
        [
            value[:, :MAIN].reshape(blocks * MAIN, *rest),
            value[:, MAIN:-MAIN].reshape(-1, *rest),
            value[:, -MAIN:].reshape(blocks * MAIN, *rest),
        ],
        0,
    )


def from_experts(value, blocks):
    rest = value.shape[1:]
    edge = blocks * MAIN
    return jnp.concatenate(
        [
            value[:edge].reshape(blocks, MAIN, *rest),
            value[edge:-edge].reshape(blocks, -1, *rest),
            value[-edge:].reshape(blocks, MAIN, *rest),
        ],
        1,
    )


def after(value, *others):
    return lax.optimization_barrier((value, others))[0]


def plus(one, two):
    return (one.astype(f32) + two.astype(f32)).astype(bf16)


def ring_gather_first(one, two):
    return shift(one, 1), shift(two, 3), shift(two, 1), shift(one, 3)


def ring_gather_second(first):
    return shift(first[0], 1), shift(first[1], 3)


def ring_gather_parts(one, two, first, second):
    one_prev, two_next, two_prev, one_next = first
    return (one, two, one_next, two_next, second[0], second[1], one_prev, two_prev)


def add_three(one, two, three):
    return (one.astype(f32) + two.astype(f32) + three.astype(f32)).astype(bf16)


VMEM_BYTES = 44 * 1024 * 1024


def first_owner_rows(tiles, tile, spill):
    row = lax.broadcasted_iota(jnp.int32, (tile, 1), 0) + (pl.program_id(0) - tiles[0]) * tile
    return lax.rem(row, EXP_DEV * spill) < spill


def per_owner(tiles, tile, spill, run):
    first, mixed = tiles
    step = pl.program_id(0)
    mine = first_owner_rows(tiles, tile, spill)
    is_mixed = (step >= first) & (step < first + mixed)

    @pl.when(is_mixed)
    def _():
        run(None, mine)

    @pl.when(jnp.logical_not(is_mixed))
    def _():
        run(jnp.where(step < first, 0, 1), None)


def hidden_back_kernel(tiles, spill, *refs):
    value, weight, out = refs
    rows = value[...]

    def run(owner, mine):
        if owner is None:
            out[...] = jnp.where(mine, matmul_nt(rows, weight[0]), matmul_nt(rows, weight[1]))
        else:
            out[...] = matmul_nt(rows, weight[owner])

    per_owner(tiles, rows.shape[0], spill, run)


def hidden_kernel(tiles, spill, *refs):
    pieces, (weight, dh_ref, gate_ref, hid, dboth, dgate), refs = refs[:8], refs[8:14], refs[14:]
    drow, acc = refs[:8], refs[8]
    rows = jnp.concatenate([p[...] for p in pieces], 1)

    def run(owner, mine):
        if owner is None:
            acc[...] = jnp.where(mine, matmul(rows, weight[0]), matmul(rows, weight[1]))
        else:
            acc[...] = matmul(rows, weight[owner])

    per_owner(tiles, rows.shape[0], spill, run)
    wide = hid.shape[1]
    up = acc[:, wide:]
    pre = acc[:, :wide]
    sig = 1.0 / (1.0 + jnp.exp(-pre))
    act = pre * sig
    hidden = (act * up).astype(bf16).astype(f32)
    gate = gate_ref[...]
    dh = dh_ref[...]
    dgate[...] = jnp.sum(hidden * dh, 1, keepdims=True)
    hid[...] = (hidden * gate).astype(bf16)
    dh = dh * gate
    dboth[:, :wide] = (dh * up * (sig * (1.0 + pre * (1.0 - sig)))).astype(bf16)
    dboth[:, wide:] = (dh * act).astype(bf16)

    def back(owner, mine):
        grad = dboth[...]
        cols = drow[0].shape[1]
        none = jnp.zeros_like(grad)
        for j, out in enumerate(drow):
            at = slice(j * cols, (j + 1) * cols)
            if owner is None:
                total = matmul_nt(jnp.where(mine, grad, none), weight[0, at, :])
                total = total + matmul_nt(jnp.where(mine, none, grad), weight[1, at, :])
            else:
                total = matmul_nt(grad, weight[owner, at, :])
            out[...] = total.astype(bf16)

    per_owner(tiles, rows.shape[0], spill, back)


def out_kernel(tiles, spill, value, weight, out):
    def run(owner, mine):
        rows = value[...]
        none = jnp.zeros_like(rows)
        for j in range(out.shape[0]):
            at = slice(j * out.shape[2], (j + 1) * out.shape[2])
            if owner is None:
                total = matmul(jnp.where(mine, rows, none), weight[0, :, at])
                total = total + matmul(jnp.where(mine, none, rows), weight[1, :, at])
            else:
                total = matmul(rows, weight[owner, :, at])
            out[j] = total.astype(bf16)

    per_owner(tiles, value.shape[0], spill, run)


def tile_spec(tile, width):
    return pl.BlockSpec((tile, width), lambda i: (i, 0))


def whole_spec(shape):
    return pl.BlockSpec(shape, lambda i: (0,) * len(shape))


def row_call(body, tile, total, ins, in_specs, outs, flops, scratch=()):
    out_shape = [jax.ShapeDtypeStruct((total, w), t) for w, t in outs]
    moved = sum(a.size * a.dtype.itemsize for a in (*ins, *out_shape))
    return pl.pallas_call(
        body,
        grid=(total // tile,),
        in_specs=in_specs,
        out_specs=[tile_spec(tile, w) for w, _ in outs],
        out_shape=out_shape,
        scratch_shapes=list(scratch),
        cost_estimate=pl.CostEstimate(flops=flops, bytes_accessed=moved, transcendentals=0),
        compiler_params=pltpu.CompilerParams(
            dimension_semantics=("arbitrary",), vmem_limit_bytes=VMEM_BYTES
        ),
    )(*ins)


def first_grad_kernel(
    kv_rows,
    normed,
    normed2,
    dmid,
    dquery,
    dlat,
    dlogits,
    attended,
    latent_n,
    dkeyval,
    gains,
    out,
    kv_grad,
):
    step = pl.program_id(0)

    @pl.when(step == 0)
    def _():
        kv_grad[...] = matmul_tn(latent_n[...], dkeyval[...]).astype(bf16)

    rows, kv_cols = out.shape[0], 256
    at_lat = dquery.shape[1]
    at_kv = at_lat + dlat.shape[1]
    at_out = at_kv + kv_cols
    at_gain = at_out + attended.shape[1]
    mine = normed[...]
    out[:, :at_lat] = matmul_tn(mine, dquery[...]).astype(bf16)
    out[:, at_lat:at_kv] = (
        matmul_tn(mine, dlat[...]) + matmul_tn(normed2[...], dlogits[...])
    ).astype(bf16)
    out[:, at_out:at_gain] = matmul_tn(dmid[...], attended[...]).astype(bf16)
    out[:, at_gain:] = gains[...]
    splits = kv_grad.shape[1] // kv_cols
    count = rows // kv_rows
    for j in range(count):
        if count % splits == 0:
            group = step * (count // splits) + j // splits
            lanes = slice(j % splits * kv_cols, (j % splits + 1) * kv_cols)
        else:
            group = (step * count + j) // splits
            lanes = pl.ds((step * count + j) % splits * kv_cols, kv_cols)
        from_rows = pl.ds(pl.multiple_of(group * kv_rows, kv_rows), kv_rows)
        out[j * kv_rows : (j + 1) * kv_rows, at_kv:at_out] = kv_grad[from_rows, lanes]


def first_grads(kv_rows, normed, normed2, dmid, dquery, dlat, dlogits, attended, latent_n, dkeyval, gains):
    block = 256
    cols = pl.BlockSpec((normed.shape[0], block), lambda i: (0, i))
    width = dquery.shape[1] + dlat.shape[1] + 256 + attended.shape[1] + gains.shape[1]
    whole = (dquery, dlat, dlogits, attended, latent_n, dkeyval)
    return pl.pallas_call(
        functools.partial(first_grad_kernel, kv_rows),
        grid=(D // block,),
        in_specs=[cols, cols, cols]
        + [whole_spec(a.shape) for a in whole]
        + [tile_spec(block, gains.shape[1])],
        out_specs=tile_spec(block, width),
        out_shape=jax.ShapeDtypeStruct((D, width), bf16),
        scratch_shapes=[pltpu.VMEM((KVR, dkeyval.shape[1]), bf16)],
        cost_estimate=pl.CostEstimate(
            flops=2 * D * width * normed.shape[0], bytes_accessed=3 * D * width, transcendentals=0
        ),
        compiler_params=pltpu.CompilerParams(
            dimension_semantics=("arbitrary",), vmem_limit_bytes=VMEM_BYTES
        ),
    )(normed, normed2, dmid, *whole, gains)


def second_grad_kernel(normed2, cotangent, dboth, hidden, out):
    split = dboth.shape[1]
    out[:, :split] = matmul_tn(normed2[...], dboth[...]).astype(bf16)
    out[:, split:] = matmul_tn(cotangent[...], hidden[...]).astype(bf16)


def second_grads(normed2, cotangent, dboth, hidden):
    block = 256
    cols = pl.BlockSpec((normed2.shape[0], block), lambda i: (0, i))
    width = dboth.shape[1] + hidden.shape[1]
    return pl.pallas_call(
        second_grad_kernel,
        grid=(D // block,),
        in_specs=[cols, cols, whole_spec(dboth.shape), whole_spec(hidden.shape)],
        out_specs=tile_spec(block, width),
        out_shape=jax.ShapeDtypeStruct((D, width), bf16),
        cost_estimate=pl.CostEstimate(
            flops=2 * D * width * normed2.shape[0], bytes_accessed=3 * D * width, transcendentals=0
        ),
        compiler_params=pltpu.CompilerParams(
            dimension_semantics=("arbitrary",), vmem_limit_bytes=VMEM_BYTES
        ),
    )(normed2, cotangent, dboth, hidden)


def per_device(
    tokens,
    expert_ids,
    route_slots,
    doc_ids,
    prenorm,
    query_w,
    latent_w,
    latnorm,
    keyval_w,
    output_w,
    midnorm,
    router_w,
    shgate_w,
    shup_w,
    shdown_w,
    exgate_w,
    exup_w,
    exdown_w,
    cotangent,
):
    owner_count = lax.axis_size("ep")
    experts = owner_count * EXP_DEV
    tok_count = tokens.shape[0]
    capacity = 2 * tok_count * TOPK // experts
    spill = capacity - MAIN
    width = EXP_DEV * capacity
    slot_rows = owner_count * width
    head_count = query_w.shape[1] // (DN + DR)
    score_scale = (DN + DR) ** (-0.5)
    shard = query_w.shape[0]
    q_cols = query_w.shape[1]
    lat_cols = latent_w.shape[1]
    kv_rows = keyval_w.shape[0]
    kv_cols = kv_rows * keyval_w.shape[1] // shard
    out_cols = output_w.shape[0]
    sh_cols = shgate_w.shape[1]

    gains = jnp.stack(
        [prenorm, jnp.pad(latnorm, (0, shard - latnorm.shape[0])), midnorm], 1
    )
    gains = jnp.pad(gains, ((0, 0), (0, 128 - gains.shape[1])))
    first_pack = jnp.concatenate(
        [
            query_w,
            latent_w,
            router_w,
            keyval_w.reshape(kv_rows, -1, kv_cols).transpose(1, 0, 2).reshape(shard, kv_cols),
            output_w.T,
            gains,
        ],
        1,
    )
    first_full = lax.all_gather(first_pack, "ep", axis=0, tiled=True)
    local = expert_ids % EXP_DEV
    inside = jnp.where(
        route_slots < MAIN,
        local * (MAIN + EXP_DEV * spill) + route_slots,
        MAIN + local * spill + (route_slots - MAIN),
    )
    place = (expert_ids // EXP_DEV) * width + inside
    row_iota = lax.broadcasted_iota(jnp.int32, (slot_rows, tok_count), 0)
    matches = [row_iota == place[:, k][None, :] for k in range(TOPK)]
    pick = matches[0]
    for k in range(1, TOPK):
        pick = pick | matches[k]
    pick = pick.astype(bf16)

    token_iota = lax.broadcasted_iota(jnp.int32, (slot_rows, tok_count), 1)
    table = jnp.sum(jnp.where(pick > 0, token_iota + 1, 0), 1).astype(jnp.int32) - 1
    table = exchange(table.reshape(owner_count, width))
    half = D // 8
    lanes = lax.axis_size("tp")
    lane = lax.axis_index("tp")
    quarter = D // lanes
    hid_cols = exgate_w.shape[2]
    hid_wide = -(-hid_cols // 128) * 128

    def from_lane(value, axis):
        parts = []
        for step in range(lanes):
            at = lax.rem(lane + step, lanes) * quarter
            parts.append(lax.dynamic_slice_in_dim(value, at, quarter, axis))
        return jnp.concatenate(parts, axis)

    def to_lane(value, axis):
        parts = []
        for step in range(lanes):
            at = lax.rem(lanes - lane + step, lanes) * quarter
            parts.append(lax.dynamic_slice_in_dim(value, at, quarter, axis))
        return jnp.concatenate(parts, axis)

    fill = hid_wide - hid_cols
    gateup_w = jnp.concatenate(
        [
            jnp.pad(from_lane(exgate_w, 1), ((0, 0), (0, 0), (0, fill))),
            jnp.pad(from_lane(exup_w, 1), ((0, 0), (0, 0), (0, fill))),
        ],
        2,
    )
    down_plain = jnp.pad(exdown_w, ((0, 0), (0, fill), (0, 0)))
    edge = owner_count * MAIN
    extra = slot_rows - 2 * edge
    span = edge + extra
    tile = 256 if edge % 256 == 0 else 128
    tiles = (edge // tile, extra // tile)
    big = 2 * (slot_rows + extra) * D * hid_wide
    first_full, table, gateup_w, down_plain = lax.optimization_barrier(
        (first_full, table, gateup_w, down_plain)
    )
    dy_all = lax.all_gather(after(cotangent, first_full), "ep", axis=0, tiled=True)
    edges = [0]
    for cols in (q_cols, lat_cols, experts, kv_cols, out_cols, 128):
        edges.append(edges[-1] + cols)
    query_full = first_full[:, edges[0] : edges[1]]
    latent_full = first_full[:, edges[1] : edges[2]]
    router_full = first_full[:, edges[2] : edges[3]]
    keyval_full = first_full[:, edges[3] : edges[4]].reshape(owner_count, -1, kv_rows, kv_cols)
    keyval_full = keyval_full.transpose(0, 2, 1, 3).reshape(KVR, keyval_w.shape[1])
    output_t = first_full[:, edges[4] : edges[5]]
    pre_gain = first_full[:, edges[5]]
    lat_gain = first_full[:, edges[5] + 1].reshape(owner_count, shard)[:, : latnorm.shape[0]]
    lat_gain = lat_gain.reshape(KVR)
    mid_gain = first_full[:, edges[5] + 2]


    resid_in = tokens.astype(f32)
    pre_scale = rms_scale(resid_in)
    pre_weight = pre_gain.astype(f32)
    normed = (resid_in * pre_scale * pre_weight).astype(bf16)
    query_raw = matmul(normed, query_full).reshape(tok_count, head_count, DN + DR)
    latent_all = matmul(normed, latent_full)
    latent = latent_all[:, :KVR]
    lat_scale = rms_scale(latent)
    lat_weight = lat_gain.astype(f32)
    latent_n = (latent * lat_scale * lat_weight).astype(bf16)
    keyval = matmul(latent_n, keyval_full).astype(bf16).reshape(tok_count, head_count, DN + DV)
    cos_tab, sine_tab = rope_tables(tok_count)
    q_all = jnp.concatenate(
        [
            query_raw[..., :DN],
            rotate(query_raw[..., DN:], cos_tab[:, None, :], sine_tab[:, None, :]),
        ],
        -1,
    ).astype(bf16)
    key_rot = rotate(latent_all[:, KVR:], cos_tab, sine_tab).astype(bf16)
    key_all = jnp.concatenate(
        [keyval[..., :DN], jnp.broadcast_to(key_rot[:, None, :], (tok_count, head_count, DR))], -1
    )
    values = keyval[..., DN:]
    position = jnp.arange(tok_count)
    doc_row = doc_ids[0]
    allowed = ((doc_row[:, None] == doc_row[None, :]) & (position[:, None] >= position[None, :]))[
        None
    ]
    raw_scores = (
        jnp.einsum("thd,shd->hts", q_all, key_all, preferred_element_type=f32) * score_scale
    )
    masked = jnp.where(allowed, raw_scores, masked_fill)
    row_max = jnp.max(masked, -1, keepdims=True)
    exp_scores = jnp.exp(masked - row_max)
    softmax_sum = jnp.sum(exp_scores, -1, keepdims=True)
    probs = exp_scores / softmax_sum
    probs16 = probs.astype(bf16)
    attended = jnp.einsum("hts,shd->thd", probs16, values, preferred_element_type=f32)
    attended = attended.reshape(tok_count, head_count * DV).astype(bf16)
    attn_sum = gather_quarters(sum_to_quarter(matmul_nt(attended, output_t)).astype(bf16))
    mid_resid = resid_in + attn_sum.astype(f32)
    mid_scale = rms_scale(mid_resid)
    mid_weight = mid_gain.astype(f32)
    normed2 = (mid_resid * mid_scale * mid_weight).astype(bf16)

    sent = matmul(pick, quarter_of(normed2, 0)).astype(bf16).reshape(owner_count, width, -1)
    one = exchange(sent[:, :, :half])
    two = exchange(after(sent[:, :, half:], one))
    second_pack = jnp.concatenate([shgate_w, shup_w, shdown_w.T], 1)
    second_full = lax.all_gather(after(second_pack, dy_all, one), "ep", axis=0, tiled=True)
    own = (to_experts(one), to_experts(two))
    first = ring_gather_first(*own)
    pick_in = (
        table[:, :, None] == lax.broadcasted_iota(jnp.int32, (owner_count, width, tok_count), 2)
    ).astype(bf16)
    dy_rows = jnp.einsum(
        "ist,itd->isd",
        pick_in,
        after(dy_all, two).reshape(owner_count, tok_count, D),
        preferred_element_type=f32,
    )
    dy_rows = to_experts(dy_rows.astype(bf16))
    (ex_dh,) = row_call(
        functools.partial(hidden_back_kernel, tiles, spill),
        tile,
        slot_rows,
        (dy_rows, down_plain),
        [tile_spec(tile, D), whole_spec(down_plain.shape)],
        [(hid_wide, f32)],
        big,
    )

    upstream = cotangent.astype(f32)
    sh_in, sh_dy = after((normed2, cotangent), two)
    gateup_full = second_full[:, : 2 * sh_cols]
    shdown_t = second_full[:, 2 * sh_cols :]
    sh_both = matmul(sh_in, gateup_full)
    sh_gate = sh_both[:, :sh_cols]
    sh_up = sh_both[:, sh_cols:]
    sh_sig = 1.0 / (1.0 + jnp.exp(-sh_gate))
    sh_hidden = (sh_gate * sh_sig * sh_up).astype(bf16)
    shared_part = matmul_nt(sh_hidden, shdown_t).astype(bf16)
    sh_dhidden = matmul(sh_dy, shdown_t)
    sh_dgate = (sh_dhidden * sh_up * sh_sig * (1.0 + sh_gate * (1.0 - sh_sig))).astype(bf16)
    sh_dup = (sh_dhidden * sh_gate * sh_sig).astype(bf16)
    sh_dboth = jnp.concatenate([sh_dgate, sh_dup], 1)
    sh_dnormed_part = matmul_nt(sh_dboth, gateup_full).astype(bf16)
    second_grad = second_grads(normed2, cotangent, sh_dboth, sh_hidden)
    second_sum = lax.psum_scatter(second_grad, "ep", scatter_dimension=0, tiled=True)

    logits = matmul(normed2, router_full)
    onehot = (
        expert_ids[:, :, None] == jnp.arange(experts, dtype=jnp.int32)[None, None, :]
    ).astype(f32)
    chosen = jnp.sum(onehot * logits[:, None, :], -1)
    sel_vals = 1.0 / (1.0 + jnp.exp(-chosen))
    sel_total = jnp.sum(sel_vals, -1, keepdims=True)
    gate_vals = route_scale * sel_vals / sel_total
    gate_rows = jnp.zeros((slot_rows, tok_count), f32)
    for k in range(TOPK):
        gate_rows = gate_rows + jnp.where(matches[k], gate_vals[:, k][None, :], 0.0)
    gate_rows = jnp.sum(gate_rows, 1).reshape(owner_count, width)
    gate_rows = to_experts(exchange(after(gate_rows, two)))[:, None]

    going, ex_dh, gate_rows = lax.optimization_barrier((first[:2], ex_dh, gate_rows))
    rows = ring_gather_parts(*own, (*going, *first[2:]), ring_gather_second(going))
    ex_dh, shared_part, sh_dnormed_part, second_grad = lax.optimization_barrier(
        (ex_dh, shared_part, sh_dnormed_part, second_grad)
    )
    shared_q = sum_to_quarter(shared_part)
    sh_dnormed_q = sum_to_quarter(sh_dnormed_part)
    ex_hidden, ex_dboth, dgate_rows, *drow = row_call(
        functools.partial(hidden_kernel, tiles, spill),
        tile,
        slot_rows,
        (*rows, gateup_w, ex_dh, gate_rows),
        [tile_spec(tile, half)] * 8
        + [whole_spec(gateup_w.shape), tile_spec(tile, hid_wide), tile_spec(tile, 1)],
        [(hid_wide, bf16), (2 * hid_wide, bf16), (1, f32)] + [(half, bf16)] * 8,
        4 * big,
        [pltpu.VMEM((tile, 2 * hid_wide), f32)],
    )

    extra_iota = lax.broadcasted_iota(jnp.int32, (span, 1), 0)
    owned = (
        (extra_iota < edge) | ((extra_iota - edge) % (EXP_DEV * spill) < spill),
        (extra_iota >= extra) | (extra_iota % (EXP_DEV * spill) >= spill),
    )

    def expert_rows(value, e):
        return value[:span] if e == 0 else value[edge:]

    def grads_of(e, left, right, cols):
        kept = jnp.where(owned[e], expert_rows(right, e)[:, cols], jnp.zeros((), bf16))
        return matmul_tn(expert_rows(left, e), kept)

    def grads_of_down(late):
        wide_dy = after(dy_rows, late)
        hidden = after(ex_hidden[:, :hid_cols], late)
        parts = []
        for e in range(EXP_DEV):
            kept = jnp.where(owned[e], expert_rows(hidden, e), jnp.zeros((), bf16))
            parts.append(matmul_tn(kept, expert_rows(wide_dy, e)))
        return jnp.stack(parts)

    def bring_back(one, two):
        back_one = exchange(from_experts(one, owner_count)).reshape(slot_rows, -1)
        back_two = exchange(from_experts(two, owner_count)).reshape(slot_rows, -1)
        return jnp.concatenate([matmul_tn(pick, back_one), matmul_tn(pick, back_two)], 1)

    out_rows = pl.pallas_call(
        functools.partial(out_kernel, tiles, spill),
        grid=(slot_rows // tile,),
        in_specs=[tile_spec(tile, hid_wide), whole_spec(down_plain.shape)],
        out_specs=pl.BlockSpec((lanes, tile, quarter), lambda i: (0, i, 0)),
        out_shape=jax.ShapeDtypeStruct((lanes, slot_rows, quarter), bf16),
        cost_estimate=pl.CostEstimate(
            flops=big, bytes_accessed=3 * slot_rows * D, transcendentals=0
        ),
        compiler_params=pltpu.CompilerParams(
            dimension_semantics=("arbitrary",), vmem_limit_bytes=VMEM_BYTES
        ),
    )(ex_hidden, down_plain).reshape(lanes * slot_rows, quarter)
    top = shift(drow[4], 1)
    bottom = shift(drow[5], 3)
    dgate_rows = exchange(from_experts(dgate_rows[:, 0], owner_count)).reshape(-1)
    top, bottom, dgate_rows, out_rows = lax.optimization_barrier(
        (top, bottom, dgate_rows, out_rows)
    )
    from_prev_one = shift(plus(drow[2], top), 1)
    from_next_one = shift(after(drow[6], bottom), 3)
    next_two, prev_two = after(
        (drow[3], plus(drow[7], bottom)), from_prev_one, from_next_one
    )
    from_prev_two = shift(next_two, 1)
    from_next_two = shift(prev_two, 3)
    drow_one = add_three(drow[0], from_prev_one, from_next_one)
    drow_two = add_three(drow[1], from_prev_two, from_next_two)
    routed_grad_q = bring_back(drow_one, drow_two)
    out_rows = after(out_rows, drow_one, second_sum)
    out_sum = lax.psum_scatter(out_rows, "tp", scatter_dimension=0, tiled=True)

    dgate_part = jnp.stack(
        [jnp.sum(jnp.where(matches[k], dgate_rows[:, None], 0.0), 0) for k in range(TOPK)], 1
    )
    dgate_all = sum_small(dgate_part)
    weighted = jnp.sum(dgate_all * gate_vals, -1, keepdims=True) / route_scale
    dsel_vals = route_scale / sel_total * (dgate_all - weighted)
    dchosen = dsel_vals * sel_vals * (1.0 - sel_vals)
    dlogits = jnp.sum(onehot * dchosen[:, :, None], 1).astype(bf16)
    dnormed2 = gather_quarters((routed_grad_q + sh_dnormed_q).astype(bf16)).astype(f32)
    dnormed2 = dnormed2 + matmul_nt(dlogits, router_full)
    dmid_norm, midnorm_grad = rms_back(mid_resid, mid_scale, mid_weight, dnormed2)
    dmid = upstream + dmid_norm
    dmid16 = dmid.astype(bf16)
    dattended = matmul(dmid16, output_t).astype(bf16).reshape(tok_count, head_count, DV)
    dprobs = jnp.einsum("thd,shd->hts", dattended, values, preferred_element_type=f32)
    dscores = (probs * (dprobs - jnp.sum(probs * dprobs, -1, keepdims=True))).astype(bf16)
    dq_all = (
        jnp.einsum("hts,shd->thd", dscores, key_all, preferred_element_type=f32) * score_scale
    )
    dkey_all = jnp.einsum("hts,thd->shd", dscores, q_all, preferred_element_type=f32) * score_scale
    dvalues = jnp.einsum("hts,thd->shd", probs16, dattended, preferred_element_type=f32)
    dquery = jnp.concatenate(
        [dq_all[..., :DN], rotate(dq_all[..., DN:], cos_tab[:, None, :], -sine_tab[:, None, :])], -1
    )
    dquery = dquery.reshape(tok_count, head_count * (DN + DR)).astype(bf16)
    dkeyval = (
        jnp.concatenate([dkey_all[..., :DN], dvalues], -1)
        .reshape(tok_count, head_count * (DN + DV))
        .astype(bf16)
    )
    dlatent_part = matmul_nt(dkeyval, keyval_full)
    dkey_part = jnp.sum(dkey_all[..., DN:], 1)
    dlat_part = jnp.concatenate([dlatent_part, dkey_part], 1).astype(bf16)
    dlat_sum = sum_small(dlat_part)
    dlatent, latnorm_grad = rms_back(latent, lat_scale, lat_weight, dlat_sum[:, :KVR])
    dlatent_all = jnp.concatenate(
        [dlatent, rotate(dlat_sum[:, KVR:], cos_tab, -sine_tab)], -1
    ).astype(bf16)
    gain_grads = jnp.stack(
        [
            jnp.pad(
                latnorm_grad.reshape(owner_count, -1),
                ((0, 0), (0, shard - latnorm.shape[0])),
            ).reshape(-1),
            midnorm_grad,
        ],
        1,
    )
    gain_grads = jnp.pad(gain_grads, ((0, 0), (0, 128 - gain_grads.shape[1])))
    first_grad = first_grads(
        kv_rows,
        normed,
        normed2,
        dmid16,
        dquery,
        jnp.pad(dlatent_all, ((0, 0), (0, experts))),
        jnp.pad(dlogits, ((0, 0), (lat_cols, 0))),
        attended,
        latent_n,
        dkeyval,
        after(gain_grads.astype(bf16), out_sum),
    )
    late = shift(first_grad[:16, :128], 1)
    back = exchange(from_experts(after(out_sum, late), owner_count)).reshape(slot_rows, -1)
    routed_q = matmul_tn(pick, back)
    late_dquery, late_dlat = after((dquery, dlatent_all), late)
    dnormed_q = sum_to_quarter(matmul_nt(late_dquery, query_full))
    dnormed = gather_quarters(dnormed_q.astype(bf16)).astype(f32) + matmul_nt(
        late_dlat, latent_full
    )
    dtokens, prenorm_grad = rms_back(resid_in, pre_scale, pre_weight, dnormed)
    tokens_grad = (dmid + dtokens).astype(bf16)
    prenorm_sum = jnp.sum(exchange(prenorm_grad.reshape(owner_count, shard)), 0)
    down_grad = grads_of_down(late)
    all_rows = jnp.concatenate(after(rows, late), 1)
    late_dboth = after(ex_dboth, late)
    exgate_grad = jnp.stack(
        [grads_of(e, all_rows, late_dboth, slice(0, hid_cols)) for e in range(EXP_DEV)]
    )
    exup_grad = jnp.stack(
        [
            grads_of(e, all_rows, late_dboth, slice(hid_wide, hid_wide + hid_cols))
            for e in range(EXP_DEV)
        ]
    )
    exgate_grad = to_lane(exgate_grad, 1)
    exup_grad = to_lane(exup_grad, 1)
    layer_q = (quarter_of(mid_resid, 0) + routed_q + shared_q).astype(bf16)
    layer_out = gather_quarters(layer_q)
    first_sum = lax.psum_scatter(first_grad, "ep", scatter_dimension=0, tiled=True).astype(f32)
    second_sum = second_sum.astype(f32)
    return (
        layer_out,
        tokens_grad,
        prenorm_sum,
        first_sum[:, edges[0] : edges[1]],
        first_sum[:, edges[1] : edges[2]],
        first_sum[: latnorm.shape[0], edges[5]],
        first_sum[:, edges[3] : edges[4]]
        .reshape(-1, kv_rows, kv_cols)
        .transpose(1, 0, 2)
        .reshape(keyval_w.shape),
        first_sum[:, edges[4] : edges[5]].T,
        first_sum[:, edges[5] + 1],
        first_sum[:, edges[2] : edges[3]],
        second_sum[:, :sh_cols],
        second_sum[:, sh_cols : 2 * sh_cols],
        second_sum[:, 2 * sh_cols :].T,
        exgate_grad,
        exup_grad,
        down_grad,
    )


def solution(mesh):
    in_specs = (
        P("ep", None),
        P("ep", None),
        P("ep", None),
        P("ep", None),
        P("ep"),
        P("ep", "tp"),
        P("ep", None),
        P("ep"),
        P("ep", "tp"),
        P("tp", "ep"),
        P("ep"),
        P("ep", None),
        P("ep", "tp"),
        P("ep", "tp"),
        P("tp", "ep"),
        P("ep", None, "tp"),
        P("ep", None, "tp"),
        P("ep", "tp", None),
        P("ep", None),
    )
    out_specs = (
        P("ep", None),
        P("ep", None),
        P("ep"),
        P("ep", "tp"),
        P("ep", None),
        P("ep"),
        P("ep", "tp"),
        P("tp", "ep"),
        P("ep"),
        P("ep", None),
        P("ep", "tp"),
        P("ep", "tp"),
        P("tp", "ep"),
        P("ep", None, "tp"),
        P("ep", None, "tp"),
        P("ep", "tp", None),
    )
    return jax.shard_map(
        per_device, mesh=mesh, in_specs=in_specs, out_specs=out_specs, check_vma=False
    )
```

```python
import functools

import jax
import jax.numpy as jnp
from jax import lax
from jax.experimental import pallas as pl
from jax.experimental.pallas import tpu as pltpu
from jax.sharding import PartitionSpec as P

D = 2048
DN = 128
DR = 64
DV = 128
KVR = 512
TOPK = 6
EXP_DEV = 2
MAIN = 32

epsilon = 1e-06
route_scale = 2.446
rope_base = 50000.0
masked_fill = -1000000000.0

bf16 = jnp.bfloat16
f32 = jnp.float32


def matmul(left_mat, right_mat):
    return jnp.dot(left_mat, right_mat, preferred_element_type=f32)


def matmul_nt(left_mat, right_mat):
    return lax.dot_general(
        left_mat, right_mat, (((1,), (1,)), ((), ())), preferred_element_type=f32
    )


def matmul_tn(left_mat, right_mat):
    return lax.dot_general(
        left_mat, right_mat, (((0,), (0,)), ((), ())), preferred_element_type=f32
    )


def rms_scale(values):
    return lax.rsqrt(jnp.mean(values * values, -1, keepdims=True) + epsilon)


def rms_back(values, scale_vals, gain_vec, upstream):
    weighted = upstream * gain_vec
    inner_mean = jnp.mean(weighted * values, -1, keepdims=True)
    grad_in = scale_vals * weighted - values * scale_vals * scale_vals * scale_vals * inner_mean
    grad_gain = jnp.sum(upstream * values * scale_vals, 0)
    return (grad_in, grad_gain)


def rope_tables(row_count):
    half_dim = DR // 2
    freq_vec = rope_base ** (-(jnp.arange(half_dim, dtype=f32) * (2.0 / DR)))
    angle_tab = jnp.arange(row_count, dtype=f32)[:, None] * freq_vec[None, :]
    return (jnp.cos(angle_tab), jnp.sin(angle_tab))


def rotate(values, cos_tab, sine_tab):
    half_dim = values.shape[-1] // 2
    first_half = values[..., :half_dim]
    second_half = values[..., half_dim:]
    return jnp.concatenate(
        [
            first_half * cos_tab - second_half * sine_tab,
            second_half * cos_tab + first_half * sine_tab,
        ],
        -1,
    )


def shift(value, step):
    lanes = lax.axis_size("tp")
    return lax.ppermute(value, "tp", [(i, (i + step) % lanes) for i in range(lanes)])


def quarter_of(value, step):
    lanes = lax.axis_size("tp")
    width = value.shape[1] // lanes
    lane = lax.rem(lax.axis_index("tp") + step, lanes)
    return lax.dynamic_slice_in_dim(value, lane * width, width, 1)


def sum_to_quarter(partial):
    low = partial.astype(bf16)
    total = quarter_of(low, 0).astype(f32)
    for step in (1, 3, 2):
        total = total + shift(quarter_of(low, step), step).astype(f32)
    return total


def gather_quarters(piece):
    lanes = lax.axis_size("tp")
    lane = lax.axis_index("tp")
    parts = [piece] + [None] * (lanes - 1)
    for step in (1, 3, 2):
        parts[step] = shift(piece, lanes - step)
    full = jnp.concatenate(parts, 1)
    width = piece.shape[1]
    parts = []
    for step in range(lanes):
        at = lax.rem(lanes - lane + step, lanes) * width
        parts.append(lax.dynamic_slice_in_dim(full, at, width, 1))
    return jnp.concatenate(parts, 1)


def sum_small(partial):
    total = partial.astype(f32)
    for step in (1, 3, 2):
        total = total + shift(partial, step).astype(f32)
    return total


def exchange(value):
    return lax.all_to_all(value, "ep", 0, 0, tiled=True)


def to_experts(value):
    blocks = value.shape[0]
    rest = value.shape[2:]
    return jnp.concatenate(
        [
            value[:, :MAIN].reshape(blocks * MAIN, *rest),
            value[:, MAIN:-MAIN].reshape(-1, *rest),
            value[:, -MAIN:].reshape(blocks * MAIN, *rest),
        ],
        0,
    )


def from_experts(value, blocks):
    rest = value.shape[1:]
    edge = blocks * MAIN
    return jnp.concatenate(
        [
            value[:edge].reshape(blocks, MAIN, *rest),
            value[edge:-edge].reshape(blocks, -1, *rest),
            value[-edge:].reshape(blocks, MAIN, *rest),
        ],
        1,
    )


def after(value, *others):
    return lax.optimization_barrier((value, others))[0]


def plus(one, two):
    return (one.astype(f32) + two.astype(f32)).astype(bf16)


def ring_gather_first(one, two):
    return shift(one, 1), shift(two, 3), shift(two, 1), shift(one, 3)


def ring_gather_second(first):
    return shift(first[0], 1), shift(first[1], 3)


def ring_gather_parts(one, two, first, second):
    one_prev, two_next, two_prev, one_next = first
    return (one, two, one_next, two_next, second[0], second[1], one_prev, two_prev)


def add_three(one, two, three):
    return (one.astype(f32) + two.astype(f32) + three.astype(f32)).astype(bf16)


VMEM_BYTES = 44 * 1024 * 1024


def first_owner_rows(tiles, tile, spill):
    row = lax.broadcasted_iota(jnp.int32, (tile, 1), 0) + (pl.program_id(0) - tiles[0]) * tile
    return lax.rem(row, EXP_DEV * spill) < spill


def per_owner(tiles, tile, spill, run):
    first, mixed = tiles
    step = pl.program_id(0)
    mine = first_owner_rows(tiles, tile, spill)
    is_mixed = (step >= first) & (step < first + mixed)

    @pl.when(is_mixed)
    def _():
        run(None, mine)

    @pl.when(jnp.logical_not(is_mixed))
    def _():
        run(jnp.where(step < first, 0, 1), None)


def hidden_back_kernel(tiles, spill, *refs):
    value, weight, out = refs
    rows = value[...]

    def run(owner, mine):
        if owner is None:
            out[...] = jnp.where(mine, matmul_nt(rows, weight[0]), matmul_nt(rows, weight[1]))
        else:
            out[...] = matmul_nt(rows, weight[owner])

    per_owner(tiles, rows.shape[0], spill, run)


def hidden_kernel(tiles, spill, *refs):
    pieces, (weight, dh_ref, gate_ref, hid, dboth, dgate), refs = refs[:8], refs[8:14], refs[14:]
    drow, rows_out, acc = refs[:8], refs[8], refs[9]
    rows = jnp.concatenate([p[...] for p in pieces], 1)
    rows_out[...] = rows

    def run(owner, mine):
        if owner is None:
            acc[...] = jnp.where(mine, matmul(rows, weight[0]), matmul(rows, weight[1]))
        else:
            acc[...] = matmul(rows, weight[owner])

    per_owner(tiles, rows.shape[0], spill, run)
    wide = hid.shape[1]
    up = acc[:, wide:]
    pre = acc[:, :wide]
    sig = 1.0 / (1.0 + jnp.exp(-pre))
    act = pre * sig
    hidden = (act * up).astype(bf16).astype(f32)
    gate = gate_ref[...]
    dh = dh_ref[...]
    dgate[...] = jnp.sum(hidden * dh, 1, keepdims=True)
    hid[...] = (hidden * gate).astype(bf16)
    dh = dh * gate
    dboth[:, :wide] = (dh * up * (sig * (1.0 + pre * (1.0 - sig)))).astype(bf16)
    dboth[:, wide:] = (dh * act).astype(bf16)

    def back(owner, mine):
        grad = dboth[...]
        cols = drow[0].shape[1]
        none = jnp.zeros_like(grad)
        for j, out in enumerate(drow):
            at = slice(j * cols, (j + 1) * cols)
            if owner is None:
                total = matmul_nt(jnp.where(mine, grad, none), weight[0, at, :])
                total = total + matmul_nt(jnp.where(mine, none, grad), weight[1, at, :])
            else:
                total = matmul_nt(grad, weight[owner, at, :])
            out[...] = total.astype(bf16)

    per_owner(tiles, rows.shape[0], spill, back)


def out_kernel(tiles, spill, value, weight, out):
    def run(owner, mine):
        rows = value[...]
        none = jnp.zeros_like(rows)
        for j in range(out.shape[0]):
            at = slice(j * out.shape[2], (j + 1) * out.shape[2])
            if owner is None:
                total = matmul(jnp.where(mine, rows, none), weight[0, :, at])
                total = total + matmul(jnp.where(mine, none, rows), weight[1, :, at])
            else:
                total = matmul(rows, weight[owner, :, at])
            out[j] = total.astype(bf16)

    per_owner(tiles, value.shape[0], spill, run)


def tile_spec(tile, width):
    return pl.BlockSpec((tile, width), lambda i: (i, 0))


def whole_spec(shape):
    return pl.BlockSpec(shape, lambda i: (0,) * len(shape))


def row_call(body, tile, total, ins, in_specs, outs, flops, scratch=()):
    out_shape = [jax.ShapeDtypeStruct((total, w), t) for w, t in outs]
    moved = sum(a.size * a.dtype.itemsize for a in (*ins, *out_shape))
    return pl.pallas_call(
        body,
        grid=(total // tile,),
        in_specs=in_specs,
        out_specs=[tile_spec(tile, w) for w, _ in outs],
        out_shape=out_shape,
        scratch_shapes=list(scratch),
        cost_estimate=pl.CostEstimate(flops=flops, bytes_accessed=moved, transcendentals=0),
        compiler_params=pltpu.CompilerParams(
            dimension_semantics=("arbitrary",), vmem_limit_bytes=VMEM_BYTES
        ),
    )(*ins)


def first_grad_kernel(
    kv_rows,
    normed,
    normed2,
    dmid,
    dquery,
    dlat,
    dlogits,
    attended,
    latent_n,
    dkeyval,
    gains,
    out,
    kv_grad,
):
    step = pl.program_id(0)

    @pl.when(step == 0)
    def _():
        kv_grad[...] = matmul_tn(latent_n[...], dkeyval[...]).astype(bf16)

    rows, kv_cols = out.shape[0], 256
    at_lat = dquery.shape[1]
    at_kv = at_lat + dlat.shape[1]
    at_out = at_kv + kv_cols
    at_gain = at_out + attended.shape[1]
    mine = normed[...]
    out[:, :at_lat] = matmul_tn(mine, dquery[...]).astype(bf16)
    out[:, at_lat:at_kv] = (
        matmul_tn(mine, dlat[...]) + matmul_tn(normed2[...], dlogits[...])
    ).astype(bf16)
    out[:, at_out:at_gain] = matmul_tn(dmid[...], attended[...]).astype(bf16)
    out[:, at_gain:] = gains[...]
    splits = kv_grad.shape[1] // kv_cols
    count = rows // kv_rows
    for j in range(count):
        if count % splits == 0:
            group = step * (count // splits) + j // splits
            lanes = slice(j % splits * kv_cols, (j % splits + 1) * kv_cols)
        else:
            group = (step * count + j) // splits
            lanes = pl.ds((step * count + j) % splits * kv_cols, kv_cols)
        from_rows = pl.ds(pl.multiple_of(group * kv_rows, kv_rows), kv_rows)
        out[j * kv_rows : (j + 1) * kv_rows, at_kv:at_out] = kv_grad[from_rows, lanes]


def first_grads(kv_rows, normed, normed2, dmid, dquery, dlat, dlogits, attended, latent_n, dkeyval, gains):
    block = 256
    cols = pl.BlockSpec((normed.shape[0], block), lambda i: (0, i))
    width = dquery.shape[1] + dlat.shape[1] + 256 + attended.shape[1] + gains.shape[1]
    whole = (dquery, dlat, dlogits, attended, latent_n, dkeyval)
    return pl.pallas_call(
        functools.partial(first_grad_kernel, kv_rows),
        grid=(D // block,),
        in_specs=[cols, cols, cols]
        + [whole_spec(a.shape) for a in whole]
        + [tile_spec(block, gains.shape[1])],
        out_specs=tile_spec(block, width),
        out_shape=jax.ShapeDtypeStruct((D, width), bf16),
        scratch_shapes=[pltpu.VMEM((KVR, dkeyval.shape[1]), bf16)],
        cost_estimate=pl.CostEstimate(
            flops=2 * D * width * normed.shape[0], bytes_accessed=3 * D * width, transcendentals=0
        ),
        compiler_params=pltpu.CompilerParams(
            dimension_semantics=("arbitrary",), vmem_limit_bytes=VMEM_BYTES
        ),
    )(normed, normed2, dmid, *whole, gains)


def second_grad_kernel(normed2, cotangent, dboth, hidden, out):
    split = dboth.shape[1]
    out[:, :split] = matmul_tn(normed2[...], dboth[...]).astype(bf16)
    out[:, split:] = matmul_tn(cotangent[...], hidden[...]).astype(bf16)


def second_grads(normed2, cotangent, dboth, hidden):
    block = 256
    cols = pl.BlockSpec((normed2.shape[0], block), lambda i: (0, i))
    width = dboth.shape[1] + hidden.shape[1]
    return pl.pallas_call(
        second_grad_kernel,
        grid=(D // block,),
        in_specs=[cols, cols, whole_spec(dboth.shape), whole_spec(hidden.shape)],
        out_specs=tile_spec(block, width),
        out_shape=jax.ShapeDtypeStruct((D, width), bf16),
        cost_estimate=pl.CostEstimate(
            flops=2 * D * width * normed2.shape[0], bytes_accessed=3 * D * width, transcendentals=0
        ),
        compiler_params=pltpu.CompilerParams(
            dimension_semantics=("arbitrary",), vmem_limit_bytes=VMEM_BYTES
        ),
    )(normed2, cotangent, dboth, hidden)


def weight_grad_kernel(edge, spill, lane, rows, dy, dboth, hid, gate_out, up_out, down_out, dm, hm):
    span = dm.shape[1]

    @pl.when((pl.program_id(0) == 0) & (pl.program_id(1) == 0))
    def _():
        row = lax.broadcasted_iota(jnp.int32, (span, 1), 0)
        first = (row < edge) | (lax.rem(jnp.maximum(row - edge, 0), EXP_DEV * spill) < spill)
        second = (row >= span - edge) | (lax.rem(row, EXP_DEV * spill) >= spill)
        for e, (at, keep) in enumerate(((0, first), (edge, second))):
            part = dboth[at : at + span, :]
            dm[e] = jnp.where(keep, part, jnp.zeros_like(part))
            part = hid[at : at + span, :]
            hm[e] = jnp.where(keep, part, jnp.zeros_like(part))

    owner = pl.program_id(1)
    at = pl.ds(pl.multiple_of(owner * edge, edge), span)
    cols = gate_out.shape[2]
    wide = hid.shape[1]
    both = matmul_tn(rows[at, :], dm[owner])
    gate_out[0] = both[:, :cols]
    up_out[0] = both[:, wide : wide + cols]
    down_out[0] = matmul_tn(hm[owner], dy[at, :])[:cols]


def weight_grads(edge, spill, hid_cols, lane, rows, dy, dboth, hid):
    total = rows.shape[0]
    span = total - edge
    block = D // 8
    assert (span - edge) % (EXP_DEV * spill) == 0
    up_shape = jax.ShapeDtypeStruct((EXP_DEV, D, hid_cols), f32)
    up_spec = pl.BlockSpec(
        (1, block, hid_cols), lambda j, e, lane: (e, lax.rem(lane[0] * 2 + j, 8), 0)
    )
    col_spec = pl.BlockSpec((total, block), lambda j, e, lane: (0, j))
    grid_spec = pltpu.PrefetchScalarGridSpec(
        num_scalar_prefetch=1,
        grid=(8, EXP_DEV),
        in_specs=[
            col_spec,
            col_spec,
            pl.BlockSpec(dboth.shape, lambda j, e, lane: (0, 0)),
            pl.BlockSpec(hid.shape, lambda j, e, lane: (0, 0)),
        ],
        out_specs=[
            up_spec,
            up_spec,
            pl.BlockSpec((1, hid_cols, block), lambda j, e, lane: (e, 0, j)),
        ],
        scratch_shapes=[
            pltpu.VMEM((EXP_DEV, span, dboth.shape[1]), bf16),
            pltpu.VMEM((EXP_DEV, span, hid.shape[1]), bf16),
        ],
    )
    return pl.pallas_call(
        functools.partial(weight_grad_kernel, edge, spill),
        grid_spec=grid_spec,
        out_shape=[up_shape, up_shape, jax.ShapeDtypeStruct((EXP_DEV, hid_cols, D), f32)],
        cost_estimate=pl.CostEstimate(
            flops=4 * EXP_DEV * span * D * (dboth.shape[1] + hid.shape[1]) // 2,
            bytes_accessed=4 * total * D + 12 * EXP_DEV * hid_cols * D,
            transcendentals=0,
        ),
        compiler_params=pltpu.CompilerParams(
            dimension_semantics=("arbitrary", "arbitrary"), vmem_limit_bytes=VMEM_BYTES
        ),
    )(lane.reshape(1), rows, dy, dboth, hid)


def per_device(
    tokens,
    expert_ids,
    route_slots,
    doc_ids,
    prenorm,
    query_w,
    latent_w,
    latnorm,
    keyval_w,
    output_w,
    midnorm,
    router_w,
    shgate_w,
    shup_w,
    shdown_w,
    exgate_w,
    exup_w,
    exdown_w,
    cotangent,
):
    owner_count = lax.axis_size("ep")
    experts = owner_count * EXP_DEV
    tok_count = tokens.shape[0]
    capacity = 2 * tok_count * TOPK // experts
    spill = capacity - MAIN
    width = EXP_DEV * capacity
    slot_rows = owner_count * width
    head_count = query_w.shape[1] // (DN + DR)
    score_scale = (DN + DR) ** (-0.5)
    shard = query_w.shape[0]
    q_cols = query_w.shape[1]
    lat_cols = latent_w.shape[1]
    kv_rows = keyval_w.shape[0]
    kv_cols = kv_rows * keyval_w.shape[1] // shard
    out_cols = output_w.shape[0]
    sh_cols = shgate_w.shape[1]

    gains = jnp.stack(
        [prenorm, jnp.pad(latnorm, (0, shard - latnorm.shape[0])), midnorm], 1
    )
    gains = jnp.pad(gains, ((0, 0), (0, 128 - gains.shape[1])))
    first_pack = jnp.concatenate(
        [
            query_w,
            latent_w,
            router_w,
            keyval_w.reshape(kv_rows, -1, kv_cols).transpose(1, 0, 2).reshape(shard, kv_cols),
            output_w.T,
            gains,
        ],
        1,
    )
    first_full = lax.all_gather(first_pack, "ep", axis=0, tiled=True)
    local = expert_ids % EXP_DEV
    inside = jnp.where(
        route_slots < MAIN,
        local * (MAIN + EXP_DEV * spill) + route_slots,
        MAIN + local * spill + (route_slots - MAIN),
    )
    place = (expert_ids // EXP_DEV) * width + inside
    row_iota = lax.broadcasted_iota(jnp.int32, (slot_rows, tok_count), 0)
    matches = [row_iota == place[:, k][None, :] for k in range(TOPK)]
    pick = matches[0]
    for k in range(1, TOPK):
        pick = pick | matches[k]
    pick = pick.astype(bf16)

    token_iota = lax.broadcasted_iota(jnp.int32, (slot_rows, tok_count), 1)
    table = jnp.sum(jnp.where(pick > 0, token_iota + 1, 0), 1).astype(jnp.int32) - 1
    table = exchange(table.reshape(owner_count, width))
    half = D // 8
    lanes = lax.axis_size("tp")
    lane = lax.axis_index("tp")
    quarter = D // lanes
    hid_cols = exgate_w.shape[2]
    hid_wide = -(-hid_cols // 128) * 128

    def from_lane(value, axis):
        parts = []
        for step in range(lanes):
            at = lax.rem(lane + step, lanes) * quarter
            parts.append(lax.dynamic_slice_in_dim(value, at, quarter, axis))
        return jnp.concatenate(parts, axis)

    fill = hid_wide - hid_cols
    gateup_w = jnp.concatenate(
        [
            jnp.pad(from_lane(exgate_w, 1), ((0, 0), (0, 0), (0, fill))),
            jnp.pad(from_lane(exup_w, 1), ((0, 0), (0, 0), (0, fill))),
        ],
        2,
    )
    down_plain = jnp.pad(exdown_w, ((0, 0), (0, fill), (0, 0)))
    edge = owner_count * MAIN
    extra = slot_rows - 2 * edge
    span = edge + extra
    tile = 256 if edge % 256 == 0 else 128
    tiles = (edge // tile, extra // tile)
    big = 2 * (slot_rows + extra) * D * hid_wide
    first_full, table, gateup_w, down_plain = lax.optimization_barrier(
        (first_full, table, gateup_w, down_plain)
    )
    dy_all = lax.all_gather(after(cotangent, first_full), "ep", axis=0, tiled=True)
    edges = [0]
    for cols in (q_cols, lat_cols, experts, kv_cols, out_cols, 128):
        edges.append(edges[-1] + cols)
    query_full = first_full[:, edges[0] : edges[1]]
    latent_full = first_full[:, edges[1] : edges[2]]
    router_full = first_full[:, edges[2] : edges[3]]
    keyval_full = first_full[:, edges[3] : edges[4]].reshape(owner_count, -1, kv_rows, kv_cols)
    keyval_full = keyval_full.transpose(0, 2, 1, 3).reshape(KVR, keyval_w.shape[1])
    output_t = first_full[:, edges[4] : edges[5]]
    pre_gain = first_full[:, edges[5]]
    lat_gain = first_full[:, edges[5] + 1].reshape(owner_count, shard)[:, : latnorm.shape[0]]
    lat_gain = lat_gain.reshape(KVR)
    mid_gain = first_full[:, edges[5] + 2]


    resid_in = tokens.astype(f32)
    pre_scale = rms_scale(resid_in)
    pre_weight = pre_gain.astype(f32)
    normed = (resid_in * pre_scale * pre_weight).astype(bf16)
    query_raw = matmul(normed, query_full).reshape(tok_count, head_count, DN + DR)
    latent_all = matmul(normed, latent_full)
    latent = latent_all[:, :KVR]
    lat_scale = rms_scale(latent)
    lat_weight = lat_gain.astype(f32)
    latent_n = (latent * lat_scale * lat_weight).astype(bf16)
    keyval = matmul(latent_n, keyval_full).astype(bf16).reshape(tok_count, head_count, DN + DV)
    cos_tab, sine_tab = rope_tables(tok_count)
    q_all = jnp.concatenate(
        [
            query_raw[..., :DN],
            rotate(query_raw[..., DN:], cos_tab[:, None, :], sine_tab[:, None, :]),
        ],
        -1,
    ).astype(bf16)
    key_rot = rotate(latent_all[:, KVR:], cos_tab, sine_tab).astype(bf16)
    key_all = jnp.concatenate(
        [keyval[..., :DN], jnp.broadcast_to(key_rot[:, None, :], (tok_count, head_count, DR))], -1
    )
    values = keyval[..., DN:]
    position = jnp.arange(tok_count)
    doc_row = doc_ids[0]
    allowed = ((doc_row[:, None] == doc_row[None, :]) & (position[:, None] >= position[None, :]))[
        None
    ]
    raw_scores = (
        jnp.einsum("thd,shd->hts", q_all, key_all, preferred_element_type=f32) * score_scale
    )
    masked = jnp.where(allowed, raw_scores, masked_fill)
    row_max = jnp.max(masked, -1, keepdims=True)
    exp_scores = jnp.exp(masked - row_max)
    softmax_sum = jnp.sum(exp_scores, -1, keepdims=True)
    probs = exp_scores / softmax_sum
    probs16 = probs.astype(bf16)
    attended = jnp.einsum("hts,shd->thd", probs16, values, preferred_element_type=f32)
    attended = attended.reshape(tok_count, head_count * DV).astype(bf16)
    attn_sum = gather_quarters(sum_to_quarter(matmul_nt(attended, output_t)).astype(bf16))
    mid_resid = resid_in + attn_sum.astype(f32)
    mid_scale = rms_scale(mid_resid)
    mid_weight = mid_gain.astype(f32)
    normed2 = (mid_resid * mid_scale * mid_weight).astype(bf16)

    sent = matmul(pick, quarter_of(normed2, 0)).astype(bf16).reshape(owner_count, width, -1)
    one = exchange(sent[:, :, :half])
    two = exchange(after(sent[:, :, half:], one))
    second_pack = jnp.concatenate([shgate_w, shup_w, shdown_w.T], 1)
    second_full = lax.all_gather(after(second_pack, dy_all, one), "ep", axis=0, tiled=True)
    own = (to_experts(one), to_experts(two))
    first = ring_gather_first(*own)
    pick_in = (
        table[:, :, None] == lax.broadcasted_iota(jnp.int32, (owner_count, width, tok_count), 2)
    ).astype(bf16)
    dy_rows = jnp.einsum(
        "ist,itd->isd",
        pick_in,
        after(dy_all, two).reshape(owner_count, tok_count, D),
        preferred_element_type=f32,
    )
    dy_rows = to_experts(dy_rows.astype(bf16))
    (ex_dh,) = row_call(
        functools.partial(hidden_back_kernel, tiles, spill),
        tile,
        slot_rows,
        (dy_rows, down_plain),
        [tile_spec(tile, D), whole_spec(down_plain.shape)],
        [(hid_wide, f32)],
        big,
    )

    logits = matmul(normed2, router_full)
    onehot = (
        expert_ids[:, :, None] == jnp.arange(experts, dtype=jnp.int32)[None, None, :]
    ).astype(f32)
    chosen = jnp.sum(onehot * logits[:, None, :], -1)
    sel_vals = 1.0 / (1.0 + jnp.exp(-chosen))
    sel_total = jnp.sum(sel_vals, -1, keepdims=True)
    gate_vals = route_scale * sel_vals / sel_total
    gate_rows = jnp.zeros((slot_rows, tok_count), f32)
    for k in range(TOPK):
        gate_rows = gate_rows + jnp.where(matches[k], gate_vals[:, k][None, :], 0.0)
    gate_rows = jnp.sum(gate_rows, 1).reshape(owner_count, width)
    gate_rows = to_experts(exchange(after(gate_rows, two)))[:, None]

    going, ex_dh, gate_rows = lax.optimization_barrier((first[:2], ex_dh, gate_rows))
    rows = ring_gather_parts(*own, (*going, *first[2:]), ring_gather_second(going))
    upstream = cotangent.astype(f32)
    sh_in, sh_dy = after((normed2, cotangent), going)
    gateup_full = second_full[:, : 2 * sh_cols]
    shdown_t = second_full[:, 2 * sh_cols :]
    sh_both = matmul(sh_in, gateup_full)
    sh_gate = sh_both[:, :sh_cols]
    sh_up = sh_both[:, sh_cols:]
    sh_sig = 1.0 / (1.0 + jnp.exp(-sh_gate))
    sh_hidden = (sh_gate * sh_sig * sh_up).astype(bf16)
    shared_part = matmul_nt(sh_hidden, shdown_t).astype(bf16)
    sh_dhidden = matmul(sh_dy, shdown_t)
    sh_dgate = (sh_dhidden * sh_up * sh_sig * (1.0 + sh_gate * (1.0 - sh_sig))).astype(bf16)
    sh_dup = (sh_dhidden * sh_gate * sh_sig).astype(bf16)
    sh_dboth = jnp.concatenate([sh_dgate, sh_dup], 1)
    sh_dnormed_part = matmul_nt(sh_dboth, gateup_full).astype(bf16)
    second_grad = second_grads(normed2, cotangent, sh_dboth, sh_hidden)
    second_sum = lax.psum_scatter(second_grad, "ep", scatter_dimension=0, tiled=True)

    ex_dh, shared_part, sh_dnormed_part, second_grad = lax.optimization_barrier(
        (ex_dh, shared_part, sh_dnormed_part, second_grad)
    )
    shared_q = sum_to_quarter(shared_part)
    sh_dnormed_q = sum_to_quarter(sh_dnormed_part)
    ex_hidden, ex_dboth, dgate_rows, *drow, all_rows = row_call(
        functools.partial(hidden_kernel, tiles, spill),
        tile,
        slot_rows,
        (*rows, gateup_w, ex_dh, gate_rows),
        [tile_spec(tile, half)] * 8
        + [whole_spec(gateup_w.shape), tile_spec(tile, hid_wide), tile_spec(tile, 1)],
        [(hid_wide, bf16), (2 * hid_wide, bf16), (1, f32)] + [(half, bf16)] * 8 + [(D, bf16)],
        4 * big,
        [pltpu.VMEM((tile, 2 * hid_wide), f32)],
    )

    out_rows = pl.pallas_call(
        functools.partial(out_kernel, tiles, spill),
        grid=(slot_rows // tile,),
        in_specs=[tile_spec(tile, hid_wide), whole_spec(down_plain.shape)],
        out_specs=pl.BlockSpec((lanes, tile, quarter), lambda i: (0, i, 0)),
        out_shape=jax.ShapeDtypeStruct((lanes, slot_rows, quarter), bf16),
        cost_estimate=pl.CostEstimate(
            flops=big, bytes_accessed=3 * slot_rows * D, transcendentals=0
        ),
        compiler_params=pltpu.CompilerParams(
            dimension_semantics=("arbitrary",), vmem_limit_bytes=VMEM_BYTES
        ),
    )(ex_hidden, down_plain).reshape(lanes * slot_rows, quarter)
    top = shift(drow[4], 1)
    bottom = shift(drow[5], 3)
    dgate_rows = exchange(from_experts(dgate_rows[:, 0], owner_count)).reshape(-1)
    top, bottom, dgate_rows, out_rows = lax.optimization_barrier(
        (top, bottom, dgate_rows, out_rows)
    )
    from_prev_one = shift(plus(drow[2], top), 1)
    from_next_one = shift(after(drow[6], bottom), 3)
    next_two, prev_two = after(
        (drow[3], plus(drow[7], bottom)), from_prev_one, from_next_one
    )
    from_prev_two = shift(next_two, 1)
    from_next_two = shift(prev_two, 3)
    drow_one = add_three(drow[0], from_prev_one, from_next_one)
    drow_two = add_three(drow[1], from_prev_two, from_next_two)
    back_one = exchange(from_experts(drow_one, owner_count))
    back_two = exchange(from_experts(drow_two, owner_count))
    routed_grad_q = jnp.concatenate(
        [matmul_tn(pick, b.reshape(slot_rows, -1)) for b in (back_one, back_two)], 1
    )
    out_rows = after(out_rows, drow_two, second_sum, back_one)
    out_sum = lax.psum_scatter(out_rows, "tp", scatter_dimension=0, tiled=True)

    dgate_part = jnp.stack(
        [jnp.sum(jnp.where(matches[k], dgate_rows[:, None], 0.0), 0) for k in range(TOPK)], 1
    )
    dgate_all = sum_small(dgate_part)
    weighted = jnp.sum(dgate_all * gate_vals, -1, keepdims=True) / route_scale
    dsel_vals = route_scale / sel_total * (dgate_all - weighted)
    dchosen = dsel_vals * sel_vals * (1.0 - sel_vals)
    dlogits = jnp.sum(onehot * dchosen[:, :, None], 1).astype(bf16)
    dnormed2 = gather_quarters((routed_grad_q + sh_dnormed_q).astype(bf16)).astype(f32)
    dnormed2 = dnormed2 + matmul_nt(dlogits, router_full)
    dmid_norm, midnorm_grad = rms_back(mid_resid, mid_scale, mid_weight, dnormed2)
    dmid = upstream + dmid_norm
    dmid16 = dmid.astype(bf16)
    dattended = matmul(dmid16, output_t).astype(bf16).reshape(tok_count, head_count, DV)
    dprobs = jnp.einsum("thd,shd->hts", dattended, values, preferred_element_type=f32)
    dscores = (probs * (dprobs - jnp.sum(probs * dprobs, -1, keepdims=True))).astype(bf16)
    dq_all = (
        jnp.einsum("hts,shd->thd", dscores, key_all, preferred_element_type=f32) * score_scale
    )
    dkey_all = jnp.einsum("hts,thd->shd", dscores, q_all, preferred_element_type=f32) * score_scale
    dvalues = jnp.einsum("hts,thd->shd", probs16, dattended, preferred_element_type=f32)
    dquery = jnp.concatenate(
        [dq_all[..., :DN], rotate(dq_all[..., DN:], cos_tab[:, None, :], -sine_tab[:, None, :])], -1
    )
    dquery = dquery.reshape(tok_count, head_count * (DN + DR)).astype(bf16)
    dkeyval = (
        jnp.concatenate([dkey_all[..., :DN], dvalues], -1)
        .reshape(tok_count, head_count * (DN + DV))
        .astype(bf16)
    )
    dlatent_part = matmul_nt(dkeyval, keyval_full)
    dkey_part = jnp.sum(dkey_all[..., DN:], 1)
    dlat_part = jnp.concatenate([dlatent_part, dkey_part], 1).astype(bf16)
    dlat_sum = sum_small(dlat_part)
    dlatent, latnorm_grad = rms_back(latent, lat_scale, lat_weight, dlat_sum[:, :KVR])
    dlatent_all = jnp.concatenate(
        [dlatent, rotate(dlat_sum[:, KVR:], cos_tab, -sine_tab)], -1
    ).astype(bf16)
    gain_grads = jnp.stack(
        [
            jnp.pad(
                latnorm_grad.reshape(owner_count, -1),
                ((0, 0), (0, shard - latnorm.shape[0])),
            ).reshape(-1),
            midnorm_grad,
        ],
        1,
    )
    gain_grads = jnp.pad(gain_grads, ((0, 0), (0, 128 - gain_grads.shape[1])))
    first_grad = first_grads(
        kv_rows,
        normed,
        normed2,
        dmid16,
        dquery,
        jnp.pad(dlatent_all, ((0, 0), (0, experts))),
        jnp.pad(dlogits, ((0, 0), (lat_cols, 0))),
        attended,
        latent_n,
        dkeyval,
        after(gain_grads.astype(bf16), out_sum),
    )
    late = shift(first_grad[:16, :128], 1)
    back = exchange(from_experts(after(out_sum, late), owner_count)).reshape(slot_rows, -1)
    routed_q = matmul_tn(pick, back)
    late_dquery, late_dlat = after((dquery, dlatent_all), late)
    dnormed_q = sum_to_quarter(matmul_nt(late_dquery, query_full))
    dnormed = gather_quarters(dnormed_q.astype(bf16)).astype(f32) + matmul_nt(
        late_dlat, latent_full
    )
    dtokens, prenorm_grad = rms_back(resid_in, pre_scale, pre_weight, dnormed)
    tokens_grad = (dmid + dtokens).astype(bf16)
    prenorm_sum = jnp.sum(exchange(prenorm_grad.reshape(owner_count, shard)), 0)
    exgate_grad, exup_grad, exdown_grad = weight_grads(
        edge, spill, hid_cols, lane, *after((all_rows, dy_rows, ex_dboth, ex_hidden), late)
    )
    layer_q = (quarter_of(mid_resid, 0) + routed_q + shared_q).astype(bf16)
    layer_out = gather_quarters(layer_q)
    first_sum = lax.psum_scatter(first_grad, "ep", scatter_dimension=0, tiled=True).astype(f32)
    second_sum = second_sum.astype(f32)
    return (
        layer_out,
        tokens_grad,
        prenorm_sum,
        first_sum[:, edges[0] : edges[1]],
        first_sum[:, edges[1] : edges[2]],
        first_sum[: latnorm.shape[0], edges[5]],
        first_sum[:, edges[3] : edges[4]]
        .reshape(-1, kv_rows, kv_cols)
        .transpose(1, 0, 2)
        .reshape(keyval_w.shape),
        first_sum[:, edges[4] : edges[5]].T,
        first_sum[:, edges[5] + 1],
        first_sum[:, edges[2] : edges[3]],
        second_sum[:, :sh_cols],
        second_sum[:, sh_cols : 2 * sh_cols],
        second_sum[:, 2 * sh_cols :].T,
        exgate_grad,
        exup_grad,
        exdown_grad,
    )


def solution(mesh):
    in_specs = (
        P("ep", None),
        P("ep", None),
        P("ep", None),
        P("ep", None),
        P("ep"),
        P("ep", "tp"),
        P("ep", None),
        P("ep"),
        P("ep", "tp"),
        P("tp", "ep"),
        P("ep"),
        P("ep", None),
        P("ep", "tp"),
        P("ep", "tp"),
        P("tp", "ep"),
        P("ep", None, "tp"),
        P("ep", None, "tp"),
        P("ep", "tp", None),
        P("ep", None),
    )
    out_specs = (
        P("ep", None),
        P("ep", None),
        P("ep"),
        P("ep", "tp"),
        P("ep", None),
        P("ep"),
        P("ep", "tp"),
        P("tp", "ep"),
        P("ep"),
        P("ep", None),
        P("ep", "tp"),
        P("ep", "tp"),
        P("tp", "ep"),
        P("ep", None, "tp"),
        P("ep", None, "tp"),
        P("ep", "tp", None),
    )
    return jax.shard_map(
        per_device, mesh=mesh, in_specs=in_specs, out_specs=out_specs, check_vma=False
    )
```

```python
import functools

import jax
import jax.numpy as jnp
from jax import lax
from jax.experimental import pallas as pl
from jax.experimental.pallas import tpu as pltpu
from jax.sharding import PartitionSpec as P

D = 2048
DN = 128
DR = 64
DV = 128
KVR = 512
TOPK = 6
EXP_DEV = 2
MAIN = 32

epsilon = 1e-06
route_scale = 2.446
rope_base = 50000.0
masked_fill = -1000000000.0

bf16 = jnp.bfloat16
f32 = jnp.float32


def matmul(left_mat, right_mat):
    return jnp.dot(left_mat, right_mat, preferred_element_type=f32)


def matmul_nt(left_mat, right_mat):
    return lax.dot_general(
        left_mat, right_mat, (((1,), (1,)), ((), ())), preferred_element_type=f32
    )


def matmul_tn(left_mat, right_mat):
    return lax.dot_general(
        left_mat, right_mat, (((0,), (0,)), ((), ())), preferred_element_type=f32
    )


def rms_scale(values):
    return lax.rsqrt(jnp.mean(values * values, -1, keepdims=True) + epsilon)


def rms_back(values, scale_vals, gain_vec, upstream):
    weighted = upstream * gain_vec
    inner_mean = jnp.mean(weighted * values, -1, keepdims=True)
    grad_in = scale_vals * weighted - values * scale_vals * scale_vals * scale_vals * inner_mean
    grad_gain = jnp.sum(upstream * values * scale_vals, 0)
    return (grad_in, grad_gain)


def rope_tables(row_count):
    half_dim = DR // 2
    freq_vec = rope_base ** (-(jnp.arange(half_dim, dtype=f32) * (2.0 / DR)))
    angle_tab = jnp.arange(row_count, dtype=f32)[:, None] * freq_vec[None, :]
    return (jnp.cos(angle_tab), jnp.sin(angle_tab))


def rotate(values, cos_tab, sine_tab):
    half_dim = values.shape[-1] // 2
    first_half = values[..., :half_dim]
    second_half = values[..., half_dim:]
    return jnp.concatenate(
        [
            first_half * cos_tab - second_half * sine_tab,
            second_half * cos_tab + first_half * sine_tab,
        ],
        -1,
    )


def shift(value, step):
    lanes = lax.axis_size("tp")
    return lax.ppermute(value, "tp", [(i, (i + step) % lanes) for i in range(lanes)])


def quarter_of(value, step):
    lanes = lax.axis_size("tp")
    width = value.shape[1] // lanes
    lane = lax.rem(lax.axis_index("tp") + step, lanes)
    return lax.dynamic_slice_in_dim(value, lane * width, width, 1)


def sum_to_quarter(partial):
    low = partial.astype(bf16)
    total = quarter_of(low, 0).astype(f32)
    for step in (1, 3, 2):
        total = total + shift(quarter_of(low, step), step).astype(f32)
    return total


def gather_quarters(piece):
    lanes = lax.axis_size("tp")
    lane = lax.axis_index("tp")
    parts = [piece] + [None] * (lanes - 1)
    for step in (1, 3, 2):
        parts[step] = shift(piece, lanes - step)
    full = jnp.concatenate(parts, 1)
    width = piece.shape[1]
    parts = []
    for step in range(lanes):
        at = lax.rem(lanes - lane + step, lanes) * width
        parts.append(lax.dynamic_slice_in_dim(full, at, width, 1))
    return jnp.concatenate(parts, 1)


def sum_small(partial):
    total = partial.astype(f32)
    for step in (1, 3, 2):
        total = total + shift(partial, step).astype(f32)
    return total


def exchange(value):
    return lax.all_to_all(value, "ep", 0, 0, tiled=True)


def to_experts(value):
    blocks = value.shape[0]
    rest = value.shape[2:]
    return jnp.concatenate(
        [
            value[:, :MAIN].reshape(blocks * MAIN, *rest),
            value[:, MAIN:-MAIN].reshape(-1, *rest),
            value[:, -MAIN:].reshape(blocks * MAIN, *rest),
        ],
        0,
    )


def from_experts(value, blocks):
    rest = value.shape[1:]
    edge = blocks * MAIN
    return jnp.concatenate(
        [
            value[:edge].reshape(blocks, MAIN, *rest),
            value[edge:-edge].reshape(blocks, -1, *rest),
            value[-edge:].reshape(blocks, MAIN, *rest),
        ],
        1,
    )


def after(value, *others):
    return lax.optimization_barrier((value, others))[0]


def plus(one, two):
    return (one.astype(f32) + two.astype(f32)).astype(bf16)


def ring_gather_first(one, two):
    return shift(one, 1), shift(two, 3), shift(two, 1), shift(one, 3)


def ring_gather_second(first):
    return shift(first[0], 1), shift(first[1], 3)


def ring_gather_parts(one, two, first, second):
    one_prev, two_next, two_prev, one_next = first
    return (one, two, one_next, two_next, second[0], second[1], one_prev, two_prev)


def add_three(one, two, three):
    return (one.astype(f32) + two.astype(f32) + three.astype(f32)).astype(bf16)


VMEM_BYTES = 44 * 1024 * 1024
SMALL_COST = pl.CostEstimate(flops=1, bytes_accessed=1, transcendentals=0)


def first_owner_rows(tiles, tile, spill):
    row = lax.broadcasted_iota(jnp.int32, (tile, 1), 0) + (pl.program_id(0) - tiles[0]) * tile
    return lax.rem(row, EXP_DEV * spill) < spill


def per_owner(tiles, tile, spill, run):
    first, mixed = tiles
    step = pl.program_id(0)
    mine = first_owner_rows(tiles, tile, spill)
    is_mixed = (step >= first) & (step < first + mixed)

    @pl.when(is_mixed)
    def _():
        run(None, mine)

    @pl.when(jnp.logical_not(is_mixed))
    def _():
        run(jnp.where(step < first, 0, 1), None)


def hidden_back_kernel(tiles, spill, *refs):
    value, weight, out = refs
    rows = value[...]

    def run(owner, mine):
        if owner is None:
            out[...] = jnp.where(mine, matmul_nt(rows, weight[0]), matmul_nt(rows, weight[1]))
        else:
            out[...] = matmul_nt(rows, weight[owner])

    per_owner(tiles, rows.shape[0], spill, run)


def hidden_kernel(tiles, spill, *refs):
    pieces, (weight, dh_ref, gate_ref, hid, dboth, dgate), refs = refs[:8], refs[8:14], refs[14:]
    drow, rows_out, acc = refs[:8], refs[8], refs[9]
    rows = jnp.concatenate([p[...] for p in pieces], 1)
    rows_out[...] = rows

    def run(owner, mine):
        if owner is None:
            acc[...] = jnp.where(mine, matmul(rows, weight[0]), matmul(rows, weight[1]))
        else:
            acc[...] = matmul(rows, weight[owner])

    per_owner(tiles, rows.shape[0], spill, run)
    wide = hid.shape[1]
    up = acc[:, wide:]
    pre = acc[:, :wide]
    sig = 1.0 / (1.0 + jnp.exp(-pre))
    act = pre * sig
    hidden = (act * up).astype(bf16).astype(f32)
    gate = gate_ref[...]
    dh = dh_ref[...]
    dgate[...] = jnp.sum(hidden * dh, 1, keepdims=True)
    hid[...] = (hidden * gate).astype(bf16)
    dh = dh * gate
    dboth[:, :wide] = (dh * up * (sig * (1.0 + pre * (1.0 - sig)))).astype(bf16)
    dboth[:, wide:] = (dh * act).astype(bf16)

    def back(owner, mine):
        grad = dboth[...]
        cols = drow[0].shape[1]
        none = jnp.zeros_like(grad)
        for j, out in enumerate(drow):
            at = slice(j * cols, (j + 1) * cols)
            if owner is None:
                total = matmul_nt(jnp.where(mine, grad, none), weight[0, at, :])
                total = total + matmul_nt(jnp.where(mine, none, grad), weight[1, at, :])
            else:
                total = matmul_nt(grad, weight[owner, at, :])
            out[...] = total.astype(bf16)

    per_owner(tiles, rows.shape[0], spill, back)


def out_kernel(tiles, spill, value, weight, out):
    def run(owner, mine):
        rows = value[...]
        none = jnp.zeros_like(rows)
        for j in range(out.shape[0]):
            at = slice(j * out.shape[2], (j + 1) * out.shape[2])
            if owner is None:
                total = matmul(jnp.where(mine, rows, none), weight[0, :, at])
                total = total + matmul(jnp.where(mine, none, rows), weight[1, :, at])
            else:
                total = matmul(rows, weight[owner, :, at])
            out[j] = total.astype(bf16)

    per_owner(tiles, value.shape[0], spill, run)


def tile_spec(tile, width):
    return pl.BlockSpec((tile, width), lambda i: (i, 0))


def whole_spec(shape):
    return pl.BlockSpec(shape, lambda i: (0,) * len(shape))


def row_call(body, tile, total, ins, in_specs, outs, flops, scratch=()):
    out_shape = [jax.ShapeDtypeStruct((total, w), t) for w, t in outs]
    moved = sum(a.size * a.dtype.itemsize for a in (*ins, *out_shape))
    return pl.pallas_call(
        body,
        grid=(total // tile,),
        in_specs=in_specs,
        out_specs=[tile_spec(tile, w) for w, _ in outs],
        out_shape=out_shape,
        scratch_shapes=list(scratch),
        cost_estimate=SMALL_COST,
        compiler_params=pltpu.CompilerParams(
            dimension_semantics=("arbitrary",), vmem_limit_bytes=VMEM_BYTES
        ),
    )(*ins)


def first_grad_kernel(
    kv_rows,
    normed,
    normed2,
    dmid,
    dquery,
    dlat,
    dlogits,
    attended,
    latent_n,
    dkeyval,
    gains,
    out,
    kv_grad,
):
    step = pl.program_id(0)

    @pl.when(step == 0)
    def _():
        kv_grad[...] = matmul_tn(latent_n[...], dkeyval[...]).astype(bf16)

    rows, kv_cols = out.shape[0], 256
    at_lat = dquery.shape[1]
    at_kv = at_lat + dlat.shape[1]
    at_out = at_kv + kv_cols
    at_gain = at_out + attended.shape[1]
    mine = normed[...]
    out[:, :at_lat] = matmul_tn(mine, dquery[...]).astype(bf16)
    out[:, at_lat:at_kv] = (
        matmul_tn(mine, dlat[...]) + matmul_tn(normed2[...], dlogits[...])
    ).astype(bf16)
    out[:, at_out:at_gain] = matmul_tn(dmid[...], attended[...]).astype(bf16)
    out[:, at_gain:] = gains[...]
    splits = kv_grad.shape[1] // kv_cols
    count = rows // kv_rows
    for j in range(count):
        if count % splits == 0:
            group = step * (count // splits) + j // splits
            lanes = slice(j % splits * kv_cols, (j % splits + 1) * kv_cols)
        else:
            group = (step * count + j) // splits
            lanes = pl.ds((step * count + j) % splits * kv_cols, kv_cols)
        from_rows = pl.ds(pl.multiple_of(group * kv_rows, kv_rows), kv_rows)
        out[j * kv_rows : (j + 1) * kv_rows, at_kv:at_out] = kv_grad[from_rows, lanes]


def first_grads(kv_rows, normed, normed2, dmid, dquery, dlat, dlogits, attended, latent_n, dkeyval, gains):
    block = 256
    cols = pl.BlockSpec((normed.shape[0], block), lambda i: (0, i))
    width = dquery.shape[1] + dlat.shape[1] + 256 + attended.shape[1] + gains.shape[1]
    whole = (dquery, dlat, dlogits, attended, latent_n, dkeyval)
    return pl.pallas_call(
        functools.partial(first_grad_kernel, kv_rows),
        grid=(D // block,),
        in_specs=[cols, cols, cols]
        + [whole_spec(a.shape) for a in whole]
        + [tile_spec(block, gains.shape[1])],
        out_specs=tile_spec(block, width),
        out_shape=jax.ShapeDtypeStruct((D, width), bf16),
        scratch_shapes=[pltpu.VMEM((KVR, dkeyval.shape[1]), bf16)],
        cost_estimate=SMALL_COST,
        compiler_params=pltpu.CompilerParams(
            dimension_semantics=("arbitrary",), vmem_limit_bytes=VMEM_BYTES
        ),
    )(normed, normed2, dmid, *whole, gains)


def second_grad_kernel(normed2, cotangent, dboth, hidden, out):
    split = dboth.shape[1]
    out[:, :split] = matmul_tn(normed2[...], dboth[...]).astype(bf16)
    out[:, split:] = matmul_tn(cotangent[...], hidden[...]).astype(bf16)


def second_grads(normed2, cotangent, dboth, hidden):
    block = 256
    cols = pl.BlockSpec((normed2.shape[0], block), lambda i: (0, i))
    width = dboth.shape[1] + hidden.shape[1]
    return pl.pallas_call(
        second_grad_kernel,
        grid=(D // block,),
        in_specs=[cols, cols, whole_spec(dboth.shape), whole_spec(hidden.shape)],
        out_specs=tile_spec(block, width),
        out_shape=jax.ShapeDtypeStruct((D, width), bf16),
        cost_estimate=SMALL_COST,
        compiler_params=pltpu.CompilerParams(
            dimension_semantics=("arbitrary",), vmem_limit_bytes=VMEM_BYTES
        ),
    )(normed2, cotangent, dboth, hidden)


def weight_grad_kernel(edge, spill, lane, left, right, *refs):
    outs, kept = refs[:-1], refs[-1]
    span = kept.shape[2]
    owner = pl.program_id(1)

    @pl.when((pl.program_id(0) == 0) & (owner == 0))
    def _():
        row = lax.broadcasted_iota(jnp.int32, (span, 1), 0)
        first = (row < edge) | (lax.rem(jnp.maximum(row - edge, 0), EXP_DEV * spill) < spill)
        second = (row >= span - edge) | (lax.rem(row, EXP_DEV * spill) >= spill)
        for e, (at, keep) in enumerate(((0, first), (edge, second))):
            part = left[at : at + span, :].astype(f32)
            kept[e] = jnp.where(keep, part, 0.0).T.astype(bf16)

    at = pl.ds(pl.multiple_of(owner * edge, edge), span)
    total = matmul(kept[owner], right[at, :])
    wide = total.shape[0] // len(outs)
    for k, out in enumerate(outs):
        out[0] = total[k * wide : k * wide + out.shape[1]]


def weight_grads(edge, spill, hid_cols, count, lane, left, right):
    total, wide = left.shape
    span = total - edge
    block = D // 8
    grid_spec = pltpu.PrefetchScalarGridSpec(
        num_scalar_prefetch=1,
        grid=(8, EXP_DEV),
        in_specs=[
            pl.BlockSpec(left.shape, lambda j, e, lane: (0, 0)),
            pl.BlockSpec((total, block), lambda j, e, lane: (0, j)),
        ],
        out_specs=[
            pl.BlockSpec(
                (1, hid_cols, block), lambda j, e, lane: (e, 0, lax.rem(lane[0] * 2 + j, 8))
            )
        ]
        * count,
        scratch_shapes=[pltpu.VMEM((EXP_DEV, wide, span), bf16)],
    )
    return pl.pallas_call(
        functools.partial(weight_grad_kernel, edge, spill),
        grid_spec=grid_spec,
        out_shape=[jax.ShapeDtypeStruct((EXP_DEV, hid_cols, D), f32)] * count,
        cost_estimate=SMALL_COST,
        compiler_params=pltpu.CompilerParams(
            dimension_semantics=("arbitrary", "arbitrary"), vmem_limit_bytes=VMEM_BYTES
        ),
    )(lane.reshape(1), left, right)


def shared_kernel(normed2, cotangent, weights, dboth, hidden, part, dnormed):
    wide = hidden.shape[1]
    gate_w, up_w, down_w = (weights.at[:, k * wide : (k + 1) * wide] for k in range(3))
    pre = matmul(normed2[...], gate_w[...])
    up = matmul(normed2[...], up_w[...])
    sig = 1.0 / (1.0 + jnp.exp(-pre))
    act = pre * sig
    hidden[...] = (act * up).astype(bf16)
    dh = matmul(cotangent[...], down_w[...])
    dboth[:, :wide] = (dh * up * (sig * (1.0 + pre * (1.0 - sig)))).astype(bf16)
    dboth[:, wide:] = (dh * act).astype(bf16)
    part[...] = matmul_nt(hidden[...], down_w[...]).astype(bf16)
    dnormed[...] = (
        matmul_nt(dboth[:, :wide], gate_w[...]) + matmul_nt(dboth[:, wide:], up_w[...])
    ).astype(bf16)


def shared_experts(normed2, cotangent, weights):
    rows = normed2.shape[0]
    wide = weights.shape[1] // 3
    return pl.pallas_call(
        shared_kernel,
        out_shape=[jax.ShapeDtypeStruct((rows, w), bf16) for w in (2 * wide, wide, D, D)],
        cost_estimate=SMALL_COST,
        compiler_params=pltpu.CompilerParams(vmem_limit_bytes=VMEM_BYTES),
    )(normed2, cotangent, weights)


def per_device(
    tokens,
    expert_ids,
    route_slots,
    doc_ids,
    prenorm,
    query_w,
    latent_w,
    latnorm,
    keyval_w,
    output_w,
    midnorm,
    router_w,
    shgate_w,
    shup_w,
    shdown_w,
    exgate_w,
    exup_w,
    exdown_w,
    cotangent,
):
    owner_count = lax.axis_size("ep")
    experts = owner_count * EXP_DEV
    tok_count = tokens.shape[0]
    capacity = 2 * tok_count * TOPK // experts
    spill = capacity - MAIN
    width = EXP_DEV * capacity
    slot_rows = owner_count * width
    head_count = query_w.shape[1] // (DN + DR)
    score_scale = (DN + DR) ** (-0.5)
    shard = query_w.shape[0]
    q_cols = query_w.shape[1]
    lat_cols = latent_w.shape[1]
    kv_rows = keyval_w.shape[0]
    kv_cols = kv_rows * keyval_w.shape[1] // shard
    out_cols = output_w.shape[0]
    sh_cols = shgate_w.shape[1]

    gains = jnp.stack(
        [prenorm, jnp.pad(latnorm, (0, shard - latnorm.shape[0])), midnorm], 1
    )
    gains = jnp.pad(gains, ((0, 0), (0, 128 - gains.shape[1])))
    first_pack = jnp.concatenate(
        [
            query_w,
            latent_w,
            router_w,
            keyval_w.reshape(kv_rows, -1, kv_cols).transpose(1, 0, 2).reshape(shard, kv_cols),
            output_w.T,
            gains,
        ],
        1,
    )
    first_full = lax.all_gather(first_pack, "ep", axis=0, tiled=True)
    local = expert_ids % EXP_DEV
    inside = jnp.where(
        route_slots < MAIN,
        local * (MAIN + EXP_DEV * spill) + route_slots,
        MAIN + local * spill + (route_slots - MAIN),
    )
    place = (expert_ids // EXP_DEV) * width + inside
    row_iota = lax.broadcasted_iota(jnp.int32, (slot_rows, tok_count), 0)
    matches = [row_iota == place[:, k][None, :] for k in range(TOPK)]
    pick = matches[0]
    for k in range(1, TOPK):
        pick = pick | matches[k]
    pick = pick.astype(bf16)

    token_iota = lax.broadcasted_iota(jnp.int32, (slot_rows, tok_count), 1)
    table = jnp.sum(jnp.where(pick > 0, token_iota + 1, 0), 1).astype(jnp.int32) - 1
    table = exchange(table.reshape(owner_count, width))
    half = D // 8
    lanes = lax.axis_size("tp")
    lane = lax.axis_index("tp")
    quarter = D // lanes
    hid_cols = exgate_w.shape[2]
    hid_wide = -(-hid_cols // 128) * 128

    def from_lane(value, axis):
        parts = []
        for step in range(lanes):
            at = lax.rem(lane + step, lanes) * quarter
            parts.append(lax.dynamic_slice_in_dim(value, at, quarter, axis))
        return jnp.concatenate(parts, axis)

    fill = hid_wide - hid_cols
    gateup_w = jnp.concatenate(
        [
            jnp.pad(from_lane(exgate_w, 1), ((0, 0), (0, 0), (0, fill))),
            jnp.pad(from_lane(exup_w, 1), ((0, 0), (0, 0), (0, fill))),
        ],
        2,
    )
    down_plain = jnp.pad(exdown_w, ((0, 0), (0, fill), (0, 0)))
    edge = owner_count * MAIN
    extra = slot_rows - 2 * edge
    span = edge + extra
    tile = 256 if edge % 256 == 0 else 128
    tiles = (edge // tile, extra // tile)
    big = 2 * (slot_rows + extra) * D * hid_wide
    first_full, table, gateup_w, down_plain = lax.optimization_barrier(
        (first_full, table, gateup_w, down_plain)
    )
    dy_all = lax.all_gather(after(cotangent, first_full), "ep", axis=0, tiled=True)
    edges = [0]
    for cols in (q_cols, lat_cols, experts, kv_cols, out_cols, 128):
        edges.append(edges[-1] + cols)
    query_full = first_full[:, edges[0] : edges[1]]
    latent_full = first_full[:, edges[1] : edges[2]]
    router_full = first_full[:, edges[2] : edges[3]]
    keyval_full = first_full[:, edges[3] : edges[4]].reshape(owner_count, -1, kv_rows, kv_cols)
    keyval_full = keyval_full.transpose(0, 2, 1, 3).reshape(KVR, keyval_w.shape[1])
    output_t = first_full[:, edges[4] : edges[5]]
    pre_gain = first_full[:, edges[5]]
    lat_gain = first_full[:, edges[5] + 1].reshape(owner_count, shard)[:, : latnorm.shape[0]]
    lat_gain = lat_gain.reshape(KVR)
    mid_gain = first_full[:, edges[5] + 2]


    resid_in = tokens.astype(f32)
    pre_scale = rms_scale(resid_in)
    pre_weight = pre_gain.astype(f32)
    normed = (resid_in * pre_scale * pre_weight).astype(bf16)
    query_raw = matmul(normed, query_full).reshape(tok_count, head_count, DN + DR)
    latent_all = matmul(normed, latent_full)
    latent = latent_all[:, :KVR]
    lat_scale = rms_scale(latent)
    lat_weight = lat_gain.astype(f32)
    latent_n = (latent * lat_scale * lat_weight).astype(bf16)
    keyval = matmul(latent_n, keyval_full).astype(bf16).reshape(tok_count, head_count, DN + DV)
    cos_tab, sine_tab = rope_tables(tok_count)
    q_all = jnp.concatenate(
        [
            query_raw[..., :DN],
            rotate(query_raw[..., DN:], cos_tab[:, None, :], sine_tab[:, None, :]),
        ],
        -1,
    ).astype(bf16)
    key_rot = rotate(latent_all[:, KVR:], cos_tab, sine_tab).astype(bf16)
    key_all = jnp.concatenate(
        [keyval[..., :DN], jnp.broadcast_to(key_rot[:, None, :], (tok_count, head_count, DR))], -1
    )
    values = keyval[..., DN:]
    position = jnp.arange(tok_count)
    doc_row = doc_ids[0]
    allowed = ((doc_row[:, None] == doc_row[None, :]) & (position[:, None] >= position[None, :]))[
        None
    ]
    raw_scores = (
        jnp.einsum("thd,shd->hts", q_all, key_all, preferred_element_type=f32) * score_scale
    )
    masked = jnp.where(allowed, raw_scores, masked_fill)
    row_max = jnp.max(masked, -1, keepdims=True)
    exp_scores = jnp.exp(masked - row_max)
    softmax_sum = jnp.sum(exp_scores, -1, keepdims=True)
    probs = exp_scores / softmax_sum
    probs16 = probs.astype(bf16)
    attended = jnp.einsum("hts,shd->thd", probs16, values, preferred_element_type=f32)
    attended = attended.reshape(tok_count, head_count * DV).astype(bf16)
    attn_sum = gather_quarters(sum_to_quarter(matmul_nt(attended, output_t)).astype(bf16))
    mid_resid = resid_in + attn_sum.astype(f32)
    mid_scale = rms_scale(mid_resid)
    mid_weight = mid_gain.astype(f32)
    normed2 = (mid_resid * mid_scale * mid_weight).astype(bf16)

    sent = matmul(pick, quarter_of(normed2, 0)).astype(bf16).reshape(owner_count, width, -1)
    one = exchange(sent[:, :, :half])
    two = exchange(after(sent[:, :, half:], one))
    sh_wide = -(-sh_cols // 128) * 128
    second_pack = jnp.concatenate(
        [
            jnp.pad(w, ((0, 0), (0, sh_wide - sh_cols)))
            for w in (shgate_w, shup_w, shdown_w.T)
        ],
        1,
    )
    second_full = lax.all_gather(after(second_pack, dy_all, one), "ep", axis=0, tiled=True)
    own = (to_experts(one), to_experts(two))
    first = ring_gather_first(*own)
    pick_in = (
        table[:, :, None] == lax.broadcasted_iota(jnp.int32, (owner_count, width, tok_count), 2)
    ).astype(bf16)
    dy_rows = jnp.einsum(
        "ist,itd->isd",
        pick_in,
        after(dy_all, two).reshape(owner_count, tok_count, D),
        preferred_element_type=f32,
    )
    dy_rows = to_experts(dy_rows.astype(bf16))
    logits = matmul(normed2, router_full)
    onehot = (
        expert_ids[:, :, None] == jnp.arange(experts, dtype=jnp.int32)[None, None, :]
    ).astype(f32)
    chosen = jnp.sum(onehot * logits[:, None, :], -1)
    sel_vals = 1.0 / (1.0 + jnp.exp(-chosen))
    sel_total = jnp.sum(sel_vals, -1, keepdims=True)
    gate_vals = route_scale * sel_vals / sel_total
    gate_rows = jnp.zeros((slot_rows, tok_count), f32)
    for k in range(TOPK):
        gate_rows = gate_rows + jnp.where(matches[k], gate_vals[:, k][None, :], 0.0)
    gate_rows = jnp.sum(gate_rows, 1).reshape(owner_count, width)
    gate_rows = to_experts(exchange(after(gate_rows, two)))[:, None]

    going, dy_rows, gate_rows = lax.optimization_barrier((first, dy_rows, gate_rows))
    rows = ring_gather_parts(*own, going, ring_gather_second(going))
    (ex_dh,) = row_call(
        functools.partial(hidden_back_kernel, tiles, spill),
        tile,
        slot_rows,
        (dy_rows, down_plain),
        [tile_spec(tile, D), whole_spec(down_plain.shape)],
        [(hid_wide, f32)],
        big,
    )
    upstream = cotangent.astype(f32)
    sh_dboth, sh_hidden, shared_part, sh_dnormed_part = shared_experts(
        *after((normed2, cotangent), going), second_full
    )
    second_grad = second_grads(normed2, cotangent, sh_dboth, sh_hidden)
    second_sum = lax.psum_scatter(second_grad, "ep", scatter_dimension=0, tiled=True)

    ex_dh, shared_part, sh_dnormed_part, second_grad = lax.optimization_barrier(
        (ex_dh, shared_part, sh_dnormed_part, second_grad)
    )
    shared_q = sum_to_quarter(shared_part)
    sh_dnormed_q = sum_to_quarter(sh_dnormed_part)
    ex_hidden, ex_dboth, dgate_rows, *drow, all_rows = row_call(
        functools.partial(hidden_kernel, tiles, spill),
        tile,
        slot_rows,
        (*rows, gateup_w, ex_dh, gate_rows),
        [tile_spec(tile, half)] * 8
        + [whole_spec(gateup_w.shape), tile_spec(tile, hid_wide), tile_spec(tile, 1)],
        [(hid_wide, bf16), (2 * hid_wide, bf16), (1, f32)] + [(half, bf16)] * 8 + [(D, bf16)],
        4 * big,
        [pltpu.VMEM((tile, 2 * hid_wide), f32)],
    )

    out_rows = pl.pallas_call(
        functools.partial(out_kernel, tiles, spill),
        grid=(slot_rows // tile,),
        in_specs=[tile_spec(tile, hid_wide), whole_spec(down_plain.shape)],
        out_specs=pl.BlockSpec((lanes, tile, quarter), lambda i: (0, i, 0)),
        out_shape=jax.ShapeDtypeStruct((lanes, slot_rows, quarter), bf16),
        cost_estimate=SMALL_COST,
        compiler_params=pltpu.CompilerParams(
            dimension_semantics=("arbitrary",), vmem_limit_bytes=VMEM_BYTES
        ),
    )(ex_hidden, down_plain).reshape(lanes * slot_rows, quarter)
    top = shift(drow[4], 1)
    bottom = shift(drow[5], 3)
    dgate_rows = exchange(from_experts(dgate_rows[:, 0], owner_count)).reshape(-1)
    top, bottom, dgate_rows, out_rows = lax.optimization_barrier(
        (top, bottom, dgate_rows, out_rows)
    )
    from_prev_one = shift(plus(drow[2], top), 1)
    from_next_one = shift(after(drow[6], bottom), 3)
    exgate_grad, exup_grad = weight_grads(
        edge, spill, hid_cols, 2, lane, *after((ex_dboth, all_rows), top, bottom)
    )
    (next_two, prev_two), exgate_grad, exup_grad, _, _ = lax.optimization_barrier(
        (
            (drow[3], plus(drow[7], bottom)),
            exgate_grad,
            exup_grad,
            from_prev_one,
            from_next_one,
        )
    )
    from_prev_two = shift(next_two, 1)
    from_next_two = shift(prev_two, 3)
    drow_one = add_three(drow[0], from_prev_one, from_next_one)
    drow_two = add_three(drow[1], from_prev_two, from_next_two)
    back_one = exchange(from_experts(drow_one, owner_count))
    back_two = exchange(from_experts(drow_two, owner_count))
    routed_grad_q = jnp.concatenate(
        [matmul_tn(pick, b.reshape(slot_rows, -1)) for b in (back_one, back_two)], 1
    )
    out_rows = after(out_rows, drow_two, second_sum, back_one)
    out_sum = lax.psum_scatter(out_rows, "tp", scatter_dimension=0, tiled=True)

    dgate_part = jnp.stack(
        [jnp.sum(jnp.where(matches[k], dgate_rows[:, None], 0.0), 0) for k in range(TOPK)], 1
    )
    dgate_all = sum_small(dgate_part)
    weighted = jnp.sum(dgate_all * gate_vals, -1, keepdims=True) / route_scale
    dsel_vals = route_scale / sel_total * (dgate_all - weighted)
    dchosen = dsel_vals * sel_vals * (1.0 - sel_vals)
    dlogits = jnp.sum(onehot * dchosen[:, :, None], 1).astype(bf16)
    dnormed2 = gather_quarters((routed_grad_q + sh_dnormed_q).astype(bf16)).astype(f32)
    dnormed2 = dnormed2 + matmul_nt(dlogits, router_full)
    dmid_norm, midnorm_grad = rms_back(mid_resid, mid_scale, mid_weight, dnormed2)
    dmid = upstream + dmid_norm
    dmid16 = dmid.astype(bf16)
    dattended = matmul(dmid16, output_t).astype(bf16).reshape(tok_count, head_count, DV)
    dprobs = jnp.einsum("thd,shd->hts", dattended, values, preferred_element_type=f32)
    dscores = (probs * (dprobs - jnp.sum(probs * dprobs, -1, keepdims=True))).astype(bf16)
    dq_all = (
        jnp.einsum("hts,shd->thd", dscores, key_all, preferred_element_type=f32) * score_scale
    )
    dkey_all = jnp.einsum("hts,thd->shd", dscores, q_all, preferred_element_type=f32) * score_scale
    dvalues = jnp.einsum("hts,thd->shd", probs16, dattended, preferred_element_type=f32)
    dquery = jnp.concatenate(
        [dq_all[..., :DN], rotate(dq_all[..., DN:], cos_tab[:, None, :], -sine_tab[:, None, :])], -1
    )
    dquery = dquery.reshape(tok_count, head_count * (DN + DR)).astype(bf16)
    dkeyval = (
        jnp.concatenate([dkey_all[..., :DN], dvalues], -1)
        .reshape(tok_count, head_count * (DN + DV))
        .astype(bf16)
    )
    dlatent_part = matmul_nt(dkeyval, keyval_full)
    dkey_part = jnp.sum(dkey_all[..., DN:], 1)
    dlat_part = jnp.concatenate([dlatent_part, dkey_part], 1).astype(bf16)
    dlat_sum = sum_small(dlat_part)
    dlatent, latnorm_grad = rms_back(latent, lat_scale, lat_weight, dlat_sum[:, :KVR])
    dlatent_all = jnp.concatenate(
        [dlatent, rotate(dlat_sum[:, KVR:], cos_tab, -sine_tab)], -1
    ).astype(bf16)
    gain_grads = jnp.stack(
        [
            jnp.pad(
                latnorm_grad.reshape(owner_count, -1),
                ((0, 0), (0, shard - latnorm.shape[0])),
            ).reshape(-1),
            midnorm_grad,
        ],
        1,
    )
    gain_grads = jnp.pad(gain_grads, ((0, 0), (0, 128 - gain_grads.shape[1])))
    first_grad = first_grads(
        kv_rows,
        normed,
        normed2,
        dmid16,
        dquery,
        jnp.pad(dlatent_all, ((0, 0), (0, experts))),
        jnp.pad(dlogits, ((0, 0), (lat_cols, 0))),
        attended,
        latent_n,
        dkeyval,
        after(gain_grads.astype(bf16), out_sum),
    )
    late = shift(first_grad[:16, :128], 1)
    back = exchange(from_experts(after(out_sum, late), owner_count)).reshape(slot_rows, -1)
    routed_q = matmul_tn(pick, back)
    late_dquery, late_dlat = after((dquery, dlatent_all), late)
    dnormed_q = sum_to_quarter(matmul_nt(late_dquery, query_full))
    dnormed = gather_quarters(dnormed_q.astype(bf16)).astype(f32) + matmul_nt(
        late_dlat, latent_full
    )
    dtokens, prenorm_grad = rms_back(resid_in, pre_scale, pre_weight, dnormed)
    tokens_grad = (dmid + dtokens).astype(bf16)
    prenorm_sum = jnp.sum(exchange(prenorm_grad.reshape(owner_count, shard)), 0)
    (exdown_grad,) = weight_grads(
        edge, spill, hid_cols, 1, jnp.zeros_like(lane), *after((ex_hidden, dy_rows), late)
    )
    layer_q = (quarter_of(mid_resid, 0) + routed_q + shared_q).astype(bf16)
    layer_out = gather_quarters(layer_q)
    first_sum = lax.psum_scatter(first_grad, "ep", scatter_dimension=0, tiled=True).astype(f32)
    second_sum = second_sum.astype(f32)
    return (
        layer_out,
        tokens_grad,
        prenorm_sum,
        first_sum[:, edges[0] : edges[1]],
        first_sum[:, edges[1] : edges[2]],
        first_sum[: latnorm.shape[0], edges[5]],
        first_sum[:, edges[3] : edges[4]]
        .reshape(-1, kv_rows, kv_cols)
        .transpose(1, 0, 2)
        .reshape(keyval_w.shape),
        first_sum[:, edges[4] : edges[5]].T,
        first_sum[:, edges[5] + 1],
        first_sum[:, edges[2] : edges[3]],
        second_sum[:, :sh_cols],
        second_sum[:, sh_wide : sh_wide + sh_cols],
        second_sum[:, 2 * sh_wide : 2 * sh_wide + sh_cols].T,
        exgate_grad.swapaxes(1, 2),
        exup_grad.swapaxes(1, 2),
        exdown_grad,
    )


def solution(mesh):
    in_specs = (
        P("ep", None),
        P("ep", None),
        P("ep", None),
        P("ep", None),
        P("ep"),
        P("ep", "tp"),
        P("ep", None),
        P("ep"),
        P("ep", "tp"),
        P("tp", "ep"),
        P("ep"),
        P("ep", None),
        P("ep", "tp"),
        P("ep", "tp"),
        P("tp", "ep"),
        P("ep", None, "tp"),
        P("ep", None, "tp"),
        P("ep", "tp", None),
        P("ep", None),
    )
    out_specs = (
        P("ep", None),
        P("ep", None),
        P("ep"),
        P("ep", "tp"),
        P("ep", None),
        P("ep"),
        P("ep", "tp"),
        P("tp", "ep"),
        P("ep"),
        P("ep", None),
        P("ep", "tp"),
        P("ep", "tp"),
        P("tp", "ep"),
        P("ep", None, "tp"),
        P("ep", None, "tp"),
        P("ep", "tp", None),
    )
    return jax.shard_map(
        per_device, mesh=mesh, in_specs=in_specs, out_specs=out_specs, check_vma=False
    )
```

```python
import functools

import jax
import jax.numpy as jnp
from jax import lax
from jax.experimental import pallas as pl
from jax.experimental.pallas import tpu as pltpu
from jax.sharding import PartitionSpec as P

D = 2048
DN = 128
DR = 64
DV = 128
KVR = 512
TOPK = 6
EXP_DEV = 2
MAIN = 32

epsilon = 1e-06
route_scale = 2.446
rope_base = 50000.0
masked_fill = -1000000000.0

bf16 = jnp.bfloat16
f32 = jnp.float32


def matmul(left_mat, right_mat):
    return jnp.dot(left_mat, right_mat, preferred_element_type=f32)


def matmul_nt(left_mat, right_mat):
    return lax.dot_general(
        left_mat, right_mat, (((1,), (1,)), ((), ())), preferred_element_type=f32
    )


def matmul_tn(left_mat, right_mat):
    return lax.dot_general(
        left_mat, right_mat, (((0,), (0,)), ((), ())), preferred_element_type=f32
    )


def rms_scale(values):
    return lax.rsqrt(jnp.mean(values * values, -1, keepdims=True) + epsilon)


def rms_back(values, scale_vals, gain_vec, upstream):
    weighted = upstream * gain_vec
    inner_mean = jnp.mean(weighted * values, -1, keepdims=True)
    grad_in = scale_vals * weighted - values * scale_vals * scale_vals * scale_vals * inner_mean
    grad_gain = jnp.sum(upstream * values * scale_vals, 0)
    return (grad_in, grad_gain)


def rope_tables(row_count):
    half_dim = DR // 2
    freq_vec = rope_base ** (-(jnp.arange(half_dim, dtype=f32) * (2.0 / DR)))
    angle_tab = jnp.arange(row_count, dtype=f32)[:, None] * freq_vec[None, :]
    return (jnp.cos(angle_tab), jnp.sin(angle_tab))


def rotate(values, cos_tab, sine_tab):
    half_dim = values.shape[-1] // 2
    first_half = values[..., :half_dim]
    second_half = values[..., half_dim:]
    return jnp.concatenate(
        [
            first_half * cos_tab - second_half * sine_tab,
            second_half * cos_tab + first_half * sine_tab,
        ],
        -1,
    )


def shift(value, step):
    lanes = lax.axis_size("tp")
    return lax.ppermute(value, "tp", [(i, (i + step) % lanes) for i in range(lanes)])


def quarter_of(value, step):
    lanes = lax.axis_size("tp")
    width = value.shape[1] // lanes
    lane = lax.rem(lax.axis_index("tp") + step, lanes)
    return lax.dynamic_slice_in_dim(value, lane * width, width, 1)


def sum_to_quarter(partial):
    low = partial.astype(bf16)
    total = quarter_of(low, 0).astype(f32)
    for step in (1, 3, 2):
        total = total + shift(quarter_of(low, step), step).astype(f32)
    return total


def gather_quarters(piece):
    lanes = lax.axis_size("tp")
    lane = lax.axis_index("tp")
    parts = [piece] + [None] * (lanes - 1)
    for step in (1, 3, 2):
        parts[step] = shift(piece, lanes - step)
    full = jnp.concatenate(parts, 1)
    width = piece.shape[1]
    parts = []
    for step in range(lanes):
        at = lax.rem(lanes - lane + step, lanes) * width
        parts.append(lax.dynamic_slice_in_dim(full, at, width, 1))
    return jnp.concatenate(parts, 1)


def sum_small(partial):
    total = partial.astype(f32)
    for step in (1, 3, 2):
        total = total + shift(partial, step).astype(f32)
    return total


def exchange(value):
    return lax.all_to_all(value, "ep", 0, 0, tiled=True)


def to_experts(value):
    blocks = value.shape[0]
    rest = value.shape[2:]
    return jnp.concatenate(
        [
            value[:, :MAIN].reshape(blocks * MAIN, *rest),
            value[:, MAIN:-MAIN].reshape(-1, *rest),
            value[:, -MAIN:].reshape(blocks * MAIN, *rest),
        ],
        0,
    )


def from_experts(value, blocks):
    rest = value.shape[1:]
    edge = blocks * MAIN
    return jnp.concatenate(
        [
            value[:edge].reshape(blocks, MAIN, *rest),
            value[edge:-edge].reshape(blocks, -1, *rest),
            value[-edge:].reshape(blocks, MAIN, *rest),
        ],
        1,
    )


def after(value, *others):
    return lax.optimization_barrier((value, others))[0]


def plus(one, two):
    return (one.astype(f32) + two.astype(f32)).astype(bf16)


def ring_gather_first(one, two):
    return shift(one, 1), shift(two, 3), shift(two, 1), shift(one, 3)


def ring_gather_second(first):
    return shift(first[0], 1), shift(first[1], 3)


def ring_gather_parts(one, two, first, second):
    one_prev, two_next, two_prev, one_next = first
    return (one, two, one_next, two_next, second[0], second[1], one_prev, two_prev)


def add_three(one, two, three):
    return (one.astype(f32) + two.astype(f32) + three.astype(f32)).astype(bf16)


VMEM_BYTES = 44 * 1024 * 1024
SMALL_COST = pl.CostEstimate(flops=1, bytes_accessed=1, transcendentals=0)


def first_owner_rows(tiles, tile, spill):
    row = lax.broadcasted_iota(jnp.int32, (tile, 1), 0) + (pl.program_id(0) - tiles[0]) * tile
    return lax.rem(row, EXP_DEV * spill) < spill


def per_owner(tiles, tile, spill, run):
    first, mixed = tiles
    step = pl.program_id(0)
    mine = first_owner_rows(tiles, tile, spill)
    is_mixed = (step >= first) & (step < first + mixed)

    @pl.when(is_mixed)
    def _():
        run(None, mine)

    @pl.when(jnp.logical_not(is_mixed))
    def _():
        run(jnp.where(step < first, 0, 1), None)


def hidden_back_kernel(tiles, spill, *refs):
    value, weight, out = refs
    rows = value[...]

    def run(owner, mine):
        if owner is None:
            out[...] = jnp.where(mine, matmul_nt(rows, weight[0]), matmul_nt(rows, weight[1]))
        else:
            out[...] = matmul_nt(rows, weight[owner])

    per_owner(tiles, rows.shape[0], spill, run)


def hidden_kernel(tiles, spill, *refs):
    pieces, (weight, dh_ref, gate_ref, hid, dboth, dgate), refs = refs[:8], refs[8:14], refs[14:]
    drow, rows_out, acc = refs[:8], refs[8], refs[9]
    rows = jnp.concatenate([p[...] for p in pieces], 1)
    rows_out[...] = rows

    def run(owner, mine):
        if owner is None:
            acc[...] = jnp.where(mine, matmul(rows, weight[0]), matmul(rows, weight[1]))
        else:
            acc[...] = matmul(rows, weight[owner])

    per_owner(tiles, rows.shape[0], spill, run)
    wide = hid.shape[1]
    up = acc[:, wide:]
    pre = acc[:, :wide]
    sig = 1.0 / (1.0 + jnp.exp(-pre))
    act = pre * sig
    hidden = (act * up).astype(bf16).astype(f32)
    gate = gate_ref[...]
    dh = dh_ref[...]
    dgate[...] = jnp.sum(hidden * dh, 1, keepdims=True)
    hid[...] = (hidden * gate).astype(bf16)
    dh = dh * gate
    dboth[:, :wide] = (dh * up * (sig * (1.0 + pre * (1.0 - sig)))).astype(bf16)
    dboth[:, wide:] = (dh * act).astype(bf16)

    def back(owner, mine):
        grad = dboth[...]
        cols = drow[0].shape[1]
        none = jnp.zeros_like(grad)
        for j, out in enumerate(drow):
            at = slice(j * cols, (j + 1) * cols)
            if owner is None:
                total = matmul_nt(jnp.where(mine, grad, none), weight[0, at, :])
                total = total + matmul_nt(jnp.where(mine, none, grad), weight[1, at, :])
            else:
                total = matmul_nt(grad, weight[owner, at, :])
            out[...] = total.astype(bf16)

    per_owner(tiles, rows.shape[0], spill, back)


def out_kernel(tiles, spill, value, weight, out):
    def run(owner, mine):
        rows = value[...]
        none = jnp.zeros_like(rows)
        cols = out.shape[1] // 4
        for j in range(4):
            at = slice(j * cols, (j + 1) * cols)
            if owner is None:
                total = matmul(jnp.where(mine, rows, none), weight[0, :, at])
                total = total + matmul(jnp.where(mine, none, rows), weight[1, :, at])
            else:
                total = matmul(rows, weight[owner, :, at])
            out[:, at] = total.astype(bf16)

    per_owner(tiles, value.shape[0], spill, run)


def tile_spec(tile, width):
    return pl.BlockSpec((tile, width), lambda i: (i, 0))


def whole_spec(shape):
    return pl.BlockSpec(shape, lambda i: (0,) * len(shape))


def row_call(body, tile, total, ins, in_specs, outs, flops, scratch=()):
    out_shape = [jax.ShapeDtypeStruct((total, w), t) for w, t in outs]
    moved = sum(a.size * a.dtype.itemsize for a in (*ins, *out_shape))
    return pl.pallas_call(
        body,
        grid=(total // tile,),
        in_specs=in_specs,
        out_specs=[tile_spec(tile, w) for w, _ in outs],
        out_shape=out_shape,
        scratch_shapes=list(scratch),
        cost_estimate=SMALL_COST,
        compiler_params=pltpu.CompilerParams(
            dimension_semantics=("arbitrary",), vmem_limit_bytes=VMEM_BYTES
        ),
    )(*ins)


def first_grad_kernel(
    kv_rows,
    normed,
    normed2,
    dmid,
    dquery,
    dlat,
    dlogits,
    attended,
    latent_n,
    dkeyval,
    gains,
    out,
    kv_grad,
):
    step = pl.program_id(0)

    @pl.when(step == 0)
    def _():
        kv_grad[...] = matmul_tn(latent_n[...], dkeyval[...]).astype(bf16)

    rows, kv_cols = out.shape[0], 256
    at_lat = dquery.shape[1]
    at_kv = at_lat + dlat.shape[1]
    at_out = at_kv + kv_cols
    at_gain = at_out + attended.shape[1]
    mine = normed[...]
    out[:, :at_lat] = matmul_tn(mine, dquery[...]).astype(bf16)
    out[:, at_lat:at_kv] = (
        matmul_tn(mine, dlat[...]) + matmul_tn(normed2[...], dlogits[...])
    ).astype(bf16)
    out[:, at_out:at_gain] = matmul_tn(dmid[...], attended[...]).astype(bf16)
    out[:, at_gain:] = gains[...]
    splits = kv_grad.shape[1] // kv_cols
    count = rows // kv_rows
    for j in range(count):
        if count % splits == 0:
            group = step * (count // splits) + j // splits
            lanes = slice(j % splits * kv_cols, (j % splits + 1) * kv_cols)
        else:
            group = (step * count + j) // splits
            lanes = pl.ds((step * count + j) % splits * kv_cols, kv_cols)
        from_rows = pl.ds(pl.multiple_of(group * kv_rows, kv_rows), kv_rows)
        out[j * kv_rows : (j + 1) * kv_rows, at_kv:at_out] = kv_grad[from_rows, lanes]


def first_grads(kv_rows, normed, normed2, dmid, dquery, dlat, dlogits, attended, latent_n, dkeyval, gains):
    block = 256
    cols = pl.BlockSpec((normed.shape[0], block), lambda i: (0, i))
    width = dquery.shape[1] + dlat.shape[1] + 256 + attended.shape[1] + gains.shape[1]
    whole = (dquery, dlat, dlogits, attended, latent_n, dkeyval)
    return pl.pallas_call(
        functools.partial(first_grad_kernel, kv_rows),
        grid=(D // block,),
        in_specs=[cols, cols, cols]
        + [whole_spec(a.shape) for a in whole]
        + [tile_spec(block, gains.shape[1])],
        out_specs=tile_spec(block, width),
        out_shape=jax.ShapeDtypeStruct((D, width), bf16),
        scratch_shapes=[pltpu.VMEM((KVR, dkeyval.shape[1]), bf16)],
        cost_estimate=SMALL_COST,
        compiler_params=pltpu.CompilerParams(
            dimension_semantics=("arbitrary",), vmem_limit_bytes=VMEM_BYTES
        ),
    )(normed, normed2, dmid, *whole, gains)


def second_grad_kernel(normed2, cotangent, dboth, hidden, out):
    split = dboth.shape[1]
    out[:, :split] = matmul_tn(normed2[...], dboth[...]).astype(bf16)
    out[:, split:] = matmul_tn(cotangent[...], hidden[...]).astype(bf16)


def second_grads(normed2, cotangent, dboth, hidden):
    block = 256
    cols = pl.BlockSpec((normed2.shape[0], block), lambda i: (0, i))
    width = dboth.shape[1] + hidden.shape[1]
    return pl.pallas_call(
        second_grad_kernel,
        grid=(D // block,),
        in_specs=[cols, cols, whole_spec(dboth.shape), whole_spec(hidden.shape)],
        out_specs=tile_spec(block, width),
        out_shape=jax.ShapeDtypeStruct((D, width), bf16),
        cost_estimate=SMALL_COST,
        compiler_params=pltpu.CompilerParams(
            dimension_semantics=("arbitrary",), vmem_limit_bytes=VMEM_BYTES
        ),
    )(normed2, cotangent, dboth, hidden)


def weight_grad_kernel(edge, spill, lane, left, right, *refs):
    outs, kept = refs[:-1], refs[-1]
    span = kept.shape[2]
    owner = pl.program_id(1)

    @pl.when((pl.program_id(0) == 0) & (owner == 0))
    def _():
        row = lax.broadcasted_iota(jnp.int32, (span, 1), 0)
        first = (row < edge) | (lax.rem(jnp.maximum(row - edge, 0), EXP_DEV * spill) < spill)
        second = (row >= span - edge) | (lax.rem(row, EXP_DEV * spill) >= spill)
        for e, (at, keep) in enumerate(((0, first), (edge, second))):
            part = left[at : at + span, :].astype(f32)
            kept[e] = jnp.where(keep, part, 0.0).T.astype(bf16)

    at = pl.ds(pl.multiple_of(owner * edge, edge), span)
    total = matmul(kept[owner], right[at, :])
    wide = total.shape[0] // len(outs)
    for k, out in enumerate(outs):
        out[0] = total[k * wide : k * wide + out.shape[1]]


def weight_grads(edge, spill, hid_cols, count, lane, left, right):
    total, wide = left.shape
    span = total - edge
    block = D // 8
    grid_spec = pltpu.PrefetchScalarGridSpec(
        num_scalar_prefetch=1,
        grid=(8, EXP_DEV),
        in_specs=[
            pl.BlockSpec(left.shape, lambda j, e, lane: (0, 0)),
            pl.BlockSpec((total, block), lambda j, e, lane: (0, j)),
        ],
        out_specs=[
            pl.BlockSpec(
                (1, hid_cols, block), lambda j, e, lane: (e, 0, lax.rem(lane[0] * 2 + j, 8))
            )
        ]
        * count,
        scratch_shapes=[pltpu.VMEM((EXP_DEV, wide, span), bf16)],
    )
    return pl.pallas_call(
        functools.partial(weight_grad_kernel, edge, spill),
        grid_spec=grid_spec,
        out_shape=[jax.ShapeDtypeStruct((EXP_DEV, hid_cols, D), f32)] * count,
        cost_estimate=SMALL_COST,
        compiler_params=pltpu.CompilerParams(
            dimension_semantics=("arbitrary", "arbitrary"), vmem_limit_bytes=VMEM_BYTES
        ),
    )(lane.reshape(1), left, right)


def shared_kernel(normed2, cotangent, weights, _, dboth, hidden, part, dnormed):
    wide = hidden.shape[1]
    gate_w, up_w, down_w = (weights.at[:, k * wide : (k + 1) * wide] for k in range(3))
    pre = matmul(normed2[...], gate_w[...])
    up = matmul(normed2[...], up_w[...])
    sig = 1.0 / (1.0 + jnp.exp(-pre))
    act = pre * sig
    hidden[...] = (act * up).astype(bf16)
    dh = matmul(cotangent[...], down_w[...])
    dboth[:, :wide] = (dh * up * (sig * (1.0 + pre * (1.0 - sig)))).astype(bf16)
    dboth[:, wide:] = (dh * act).astype(bf16)
    part[...] = matmul_nt(hidden[...], down_w[...]).astype(bf16)
    dnormed[...] = (
        matmul_nt(dboth[:, :wide], gate_w[...]) + matmul_nt(dboth[:, wide:], up_w[...])
    ).astype(bf16)


def shared_experts(normed2, cotangent, weights, signal):
    rows = normed2.shape[0]
    wide = weights.shape[1] // 3
    return pl.pallas_call(
        shared_kernel,
        out_shape=[jax.ShapeDtypeStruct((rows, w), bf16) for w in (2 * wide, wide, D, D)],
        cost_estimate=SMALL_COST,
        compiler_params=pltpu.CompilerParams(vmem_limit_bytes=VMEM_BYTES),
    )(normed2, cotangent, weights, signal)


def per_device(
    tokens,
    expert_ids,
    route_slots,
    doc_ids,
    prenorm,
    query_w,
    latent_w,
    latnorm,
    keyval_w,
    output_w,
    midnorm,
    router_w,
    shgate_w,
    shup_w,
    shdown_w,
    exgate_w,
    exup_w,
    exdown_w,
    cotangent,
):
    owner_count = lax.axis_size("ep")
    experts = owner_count * EXP_DEV
    tok_count = tokens.shape[0]
    capacity = 2 * tok_count * TOPK // experts
    spill = capacity - MAIN
    width = EXP_DEV * capacity
    slot_rows = owner_count * width
    head_count = query_w.shape[1] // (DN + DR)
    score_scale = (DN + DR) ** (-0.5)
    shard = query_w.shape[0]
    q_cols = query_w.shape[1]
    lat_cols = latent_w.shape[1]
    kv_rows = keyval_w.shape[0]
    kv_cols = kv_rows * keyval_w.shape[1] // shard
    out_cols = output_w.shape[0]
    sh_cols = shgate_w.shape[1]

    gains = jnp.stack(
        [prenorm, jnp.pad(latnorm, (0, shard - latnorm.shape[0])), midnorm], 1
    )
    gains = jnp.pad(gains, ((0, 0), (0, 128 - gains.shape[1])))
    first_pack = jnp.concatenate(
        [
            query_w,
            latent_w,
            router_w,
            keyval_w.reshape(kv_rows, -1, kv_cols).transpose(1, 0, 2).reshape(shard, kv_cols),
            output_w.T,
            gains,
        ],
        1,
    )
    first_full = lax.all_gather(first_pack, "ep", axis=0, tiled=True)
    local = expert_ids % EXP_DEV
    inside = jnp.where(
        route_slots < MAIN,
        local * (MAIN + EXP_DEV * spill) + route_slots,
        MAIN + local * spill + (route_slots - MAIN),
    )
    place = (expert_ids // EXP_DEV) * width + inside
    row_iota = lax.broadcasted_iota(jnp.int32, (slot_rows, tok_count), 0)
    matches = [row_iota == place[:, k][None, :] for k in range(TOPK)]
    pick = matches[0]
    for k in range(1, TOPK):
        pick = pick | matches[k]
    pick = pick.astype(bf16)

    token_iota = lax.broadcasted_iota(jnp.int32, (slot_rows, tok_count), 1)
    table = jnp.sum(jnp.where(pick > 0, token_iota + 1, 0), 1).astype(jnp.int32) - 1
    table = exchange(table.reshape(owner_count, width))
    half = D // 8
    lanes = lax.axis_size("tp")
    lane = lax.axis_index("tp")
    quarter = D // lanes
    hid_cols = exgate_w.shape[2]
    hid_wide = -(-hid_cols // 128) * 128

    def from_lane(value, axis):
        parts = []
        for step in range(lanes):
            at = lax.rem(lane + step, lanes) * quarter
            parts.append(lax.dynamic_slice_in_dim(value, at, quarter, axis))
        return jnp.concatenate(parts, axis)

    fill = hid_wide - hid_cols
    gateup_w = jnp.concatenate(
        [
            jnp.pad(from_lane(exgate_w, 1), ((0, 0), (0, 0), (0, fill))),
            jnp.pad(from_lane(exup_w, 1), ((0, 0), (0, 0), (0, fill))),
        ],
        2,
    )
    down_plain = jnp.pad(exdown_w, ((0, 0), (0, fill), (0, 0)))
    edge = owner_count * MAIN
    extra = slot_rows - 2 * edge
    span = edge + extra
    tile = 256 if edge % 256 == 0 else 128
    tiles = (edge // tile, extra // tile)
    big = 2 * (slot_rows + extra) * D * hid_wide
    first_full, table, gateup_w, down_plain = lax.optimization_barrier(
        (first_full, table, gateup_w, down_plain)
    )
    dy_all = lax.all_gather(after(cotangent, first_full), "ep", axis=0, tiled=True)
    edges = [0]
    for cols in (q_cols, lat_cols, experts, kv_cols, out_cols, 128):
        edges.append(edges[-1] + cols)
    query_full = first_full[:, edges[0] : edges[1]]
    latent_full = first_full[:, edges[1] : edges[2]]
    router_full = first_full[:, edges[2] : edges[3]]
    keyval_full = first_full[:, edges[3] : edges[4]].reshape(owner_count, -1, kv_rows, kv_cols)
    keyval_full = keyval_full.transpose(0, 2, 1, 3).reshape(KVR, keyval_w.shape[1])
    output_t = first_full[:, edges[4] : edges[5]]
    pre_gain = first_full[:, edges[5]]
    lat_gain = first_full[:, edges[5] + 1].reshape(owner_count, shard)[:, : latnorm.shape[0]]
    lat_gain = lat_gain.reshape(KVR)
    mid_gain = first_full[:, edges[5] + 2]


    resid_in = tokens.astype(f32)
    pre_scale = rms_scale(resid_in)
    pre_weight = pre_gain.astype(f32)
    normed = (resid_in * pre_scale * pre_weight).astype(bf16)
    query_raw = matmul(normed, query_full).reshape(tok_count, head_count, DN + DR)
    latent_all = matmul(normed, latent_full)
    latent = latent_all[:, :KVR]
    lat_scale = rms_scale(latent)
    lat_weight = lat_gain.astype(f32)
    latent_n = (latent * lat_scale * lat_weight).astype(bf16)
    keyval = matmul(latent_n, keyval_full).astype(bf16).reshape(tok_count, head_count, DN + DV)
    cos_tab, sine_tab = rope_tables(tok_count)
    q_all = jnp.concatenate(
        [
            query_raw[..., :DN],
            rotate(query_raw[..., DN:], cos_tab[:, None, :], sine_tab[:, None, :]),
        ],
        -1,
    ).astype(bf16)
    key_rot = rotate(latent_all[:, KVR:], cos_tab, sine_tab).astype(bf16)
    key_all = jnp.concatenate(
        [keyval[..., :DN], jnp.broadcast_to(key_rot[:, None, :], (tok_count, head_count, DR))], -1
    )
    values = keyval[..., DN:]
    position = jnp.arange(tok_count)
    doc_row = doc_ids[0]
    allowed = ((doc_row[:, None] == doc_row[None, :]) & (position[:, None] >= position[None, :]))[
        None
    ]
    raw_scores = (
        jnp.einsum("thd,shd->hts", q_all, key_all, preferred_element_type=f32) * score_scale
    )
    masked = jnp.where(allowed, raw_scores, masked_fill)
    row_max = jnp.max(masked, -1, keepdims=True)
    exp_scores = jnp.exp(masked - row_max)
    softmax_sum = jnp.sum(exp_scores, -1, keepdims=True)
    probs = exp_scores / softmax_sum
    probs16 = probs.astype(bf16)
    attended = jnp.einsum("hts,shd->thd", probs16, values, preferred_element_type=f32)
    attended = attended.reshape(tok_count, head_count * DV).astype(bf16)
    attn_sum = gather_quarters(sum_to_quarter(matmul_nt(attended, output_t)).astype(bf16))
    mid_resid = resid_in + attn_sum.astype(f32)
    mid_scale = rms_scale(mid_resid)
    mid_weight = mid_gain.astype(f32)
    normed2 = (mid_resid * mid_scale * mid_weight).astype(bf16)

    sent = matmul(pick, quarter_of(normed2, 0)).astype(bf16).reshape(owner_count, width, -1)
    one = exchange(sent[:, :, :half])
    two = exchange(after(sent[:, :, half:], one))
    sh_wide = -(-sh_cols // 128) * 128
    second_pack = jnp.concatenate(
        [
            jnp.pad(w, ((0, 0), (0, sh_wide - sh_cols)))
            for w in (shgate_w, shup_w, shdown_w.T)
        ],
        1,
    )
    second_full = lax.all_gather(after(second_pack, dy_all, one), "ep", axis=0, tiled=True)
    own = (to_experts(one), to_experts(two))
    first = ring_gather_first(*own)
    pick_in = (
        table[:, :, None] == lax.broadcasted_iota(jnp.int32, (owner_count, width, tok_count), 2)
    ).astype(bf16)
    dy_rows = jnp.einsum(
        "ist,itd->isd",
        pick_in,
        after(dy_all, two).reshape(owner_count, tok_count, D),
        preferred_element_type=f32,
    )
    dy_rows = to_experts(dy_rows.astype(bf16))
    logits = matmul(normed2, router_full)
    onehot = (
        expert_ids[:, :, None] == jnp.arange(experts, dtype=jnp.int32)[None, None, :]
    ).astype(f32)
    chosen = jnp.sum(onehot * logits[:, None, :], -1)
    sel_vals = 1.0 / (1.0 + jnp.exp(-chosen))
    sel_total = jnp.sum(sel_vals, -1, keepdims=True)
    gate_vals = route_scale * sel_vals / sel_total
    gate_rows = jnp.zeros((slot_rows, tok_count), f32)
    for k in range(TOPK):
        gate_rows = gate_rows + jnp.where(matches[k], gate_vals[:, k][None, :], 0.0)
    gate_rows = jnp.sum(gate_rows, 1).reshape(owner_count, width)
    gate_rows = to_experts(exchange(after(gate_rows, two)))[:, None]

    going, dy_rows, gate_rows = lax.optimization_barrier((first, dy_rows, gate_rows))
    rows = ring_gather_parts(*own, going, ring_gather_second(going))
    (ex_dh,) = row_call(
        functools.partial(hidden_back_kernel, tiles, spill),
        tile,
        slot_rows,
        (dy_rows, down_plain),
        [tile_spec(tile, D), whole_spec(down_plain.shape)],
        [(hid_wide, f32)],
        big,
    )
    upstream = cotangent.astype(f32)
    sh_dboth, sh_hidden, shared_part, sh_dnormed_part = shared_experts(
        normed2, cotangent, second_full, going[0][:16, :128]
    )
    second_grad = second_grads(normed2, cotangent, sh_dboth, sh_hidden)
    second_sum = lax.psum_scatter(second_grad, "ep", scatter_dimension=0, tiled=True)

    ex_dh, shared_part, sh_dnormed_part, second_grad = lax.optimization_barrier(
        (ex_dh, shared_part, sh_dnormed_part, second_grad)
    )
    ex_hidden, ex_dboth, dgate_rows, *drow, all_rows = row_call(
        functools.partial(hidden_kernel, tiles, spill),
        tile,
        slot_rows,
        (*rows, gateup_w, ex_dh, gate_rows),
        [tile_spec(tile, half)] * 8
        + [whole_spec(gateup_w.shape), tile_spec(tile, hid_wide), tile_spec(tile, 1)],
        [(hid_wide, bf16), (2 * hid_wide, bf16), (1, f32)] + [(half, bf16)] * 8 + [(D, bf16)],
        4 * big,
        [pltpu.VMEM((tile, 2 * hid_wide), f32)],
    )

    (out_rows,) = row_call(
        functools.partial(out_kernel, tiles, spill),
        tile,
        slot_rows,
        (ex_hidden, down_plain),
        [tile_spec(tile, hid_wide), whole_spec(down_plain.shape)],
        [(D, bf16)],
        big,
    )
    top = shift(drow[4], 1)
    bottom = shift(drow[5], 3)
    dgate_rows = exchange(from_experts(dgate_rows[:, 0], owner_count)).reshape(-1)
    top, bottom, dgate_rows, out_rows = lax.optimization_barrier(
        (top, bottom, dgate_rows, out_rows)
    )
    from_prev_one = shift(plus(drow[2], top), 1)
    from_next_one = shift(after(drow[6], bottom), 3)
    out_dense = jnp.einsum(
        "ist,isd->itd", pick_in, from_experts(out_rows, owner_count), preferred_element_type=f32
    )
    out_dense = out_dense.astype(bf16).reshape(owner_count * tok_count, D)
    (next_two, prev_two), out_dense, _, _ = lax.optimization_barrier(
        (
            (drow[3], plus(drow[7], bottom)),
            out_dense,
            from_prev_one,
            from_next_one,
        )
    )
    from_prev_two = shift(next_two, 1)
    from_next_two = shift(prev_two, 3)
    drow_one = add_three(drow[0], from_prev_one, from_next_one)
    drow_two = add_three(drow[1], from_prev_two, from_next_two)
    back_one = exchange(from_experts(drow_one, owner_count))
    back_two = exchange(from_experts(drow_two, owner_count))
    routed_grad_q = jnp.concatenate(
        [matmul_tn(pick, b.reshape(slot_rows, -1)) for b in (back_one, back_two)], 1
    )
    out_sum = lax.psum_scatter(
        after(out_dense, second_sum), "ep", scatter_dimension=0, tiled=True
    )

    dgate_part = jnp.stack(
        [jnp.sum(jnp.where(matches[k], dgate_rows[:, None], 0.0), 0) for k in range(TOPK)], 1
    )
    dgate_part, sh_dnormed_part = after((dgate_part, sh_dnormed_part), drow_two)
    sh_dnormed_q = sum_to_quarter(sh_dnormed_part)
    dgate_all = sum_small(dgate_part)
    weighted = jnp.sum(dgate_all * gate_vals, -1, keepdims=True) / route_scale
    dsel_vals = route_scale / sel_total * (dgate_all - weighted)
    dchosen = dsel_vals * sel_vals * (1.0 - sel_vals)
    dlogits = jnp.sum(onehot * dchosen[:, :, None], 1).astype(bf16)
    dnormed2 = gather_quarters((routed_grad_q + sh_dnormed_q).astype(bf16)).astype(f32)
    dnormed2 = dnormed2 + matmul_nt(dlogits, router_full)
    dmid_norm, midnorm_grad = rms_back(mid_resid, mid_scale, mid_weight, dnormed2)
    dmid = upstream + dmid_norm
    dmid16 = dmid.astype(bf16)
    dattended = matmul(dmid16, output_t).astype(bf16).reshape(tok_count, head_count, DV)
    dprobs = jnp.einsum("thd,shd->hts", dattended, values, preferred_element_type=f32)
    dscores = (probs * (dprobs - jnp.sum(probs * dprobs, -1, keepdims=True))).astype(bf16)
    dq_all = (
        jnp.einsum("hts,shd->thd", dscores, key_all, preferred_element_type=f32) * score_scale
    )
    dkey_all = jnp.einsum("hts,thd->shd", dscores, q_all, preferred_element_type=f32) * score_scale
    dvalues = jnp.einsum("hts,thd->shd", probs16, dattended, preferred_element_type=f32)
    dquery = jnp.concatenate(
        [dq_all[..., :DN], rotate(dq_all[..., DN:], cos_tab[:, None, :], -sine_tab[:, None, :])], -1
    )
    dquery = dquery.reshape(tok_count, head_count * (DN + DR)).astype(bf16)
    dkeyval = (
        jnp.concatenate([dkey_all[..., :DN], dvalues], -1)
        .reshape(tok_count, head_count * (DN + DV))
        .astype(bf16)
    )
    dlatent_part = matmul_nt(dkeyval, keyval_full)
    dkey_part = jnp.sum(dkey_all[..., DN:], 1)
    dlat_part = jnp.concatenate([dlatent_part, dkey_part], 1).astype(bf16)
    dlat_sum = sum_small(dlat_part)
    dlatent, latnorm_grad = rms_back(latent, lat_scale, lat_weight, dlat_sum[:, :KVR])
    dlatent_all = jnp.concatenate(
        [dlatent, rotate(dlat_sum[:, KVR:], cos_tab, -sine_tab)], -1
    ).astype(bf16)
    gain_grads = jnp.stack(
        [
            jnp.pad(
                latnorm_grad.reshape(owner_count, -1),
                ((0, 0), (0, shard - latnorm.shape[0])),
            ).reshape(-1),
            midnorm_grad,
        ],
        1,
    )
    gain_grads = jnp.pad(gain_grads, ((0, 0), (0, 128 - gain_grads.shape[1])))
    first_grad = first_grads(
        kv_rows,
        normed,
        normed2,
        dmid16,
        dquery,
        jnp.pad(dlatent_all, ((0, 0), (0, experts))),
        jnp.pad(dlogits, ((0, 0), (lat_cols, 0))),
        attended,
        latent_n,
        dkeyval,
        after(gain_grads.astype(bf16), out_sum),
    )
    late = shift(first_grad[:16, :128], 1)
    out_part = after(out_sum, late).astype(f32) + shared_part.astype(f32)
    out_q = sum_to_quarter(out_part)
    late_dquery, late_dlat = after((dquery, dlatent_all), late)
    dnormed_q = sum_to_quarter(matmul_nt(late_dquery, query_full))
    dnormed = gather_quarters(dnormed_q.astype(bf16)).astype(f32) + matmul_nt(
        late_dlat, latent_full
    )
    dtokens, prenorm_grad = rms_back(resid_in, pre_scale, pre_weight, dnormed)
    tokens_grad = (dmid + dtokens).astype(bf16)
    prenorm_sum = jnp.sum(exchange(prenorm_grad.reshape(owner_count, shard)), 0)
    exgate_grad, exup_grad = weight_grads(
        edge, spill, hid_cols, 2, lane, *after((ex_dboth, all_rows), late)
    )
    (exdown_grad,) = weight_grads(
        edge, spill, hid_cols, 1, jnp.zeros_like(lane), *after((ex_hidden, dy_rows), late)
    )
    layer_q = (quarter_of(mid_resid, 0) + out_q).astype(bf16)
    layer_out = gather_quarters(layer_q)
    first_sum = lax.psum_scatter(first_grad, "ep", scatter_dimension=0, tiled=True).astype(f32)
    second_sum = second_sum.astype(f32)
    return (
        layer_out,
        tokens_grad,
        prenorm_sum,
        first_sum[:, edges[0] : edges[1]],
        first_sum[:, edges[1] : edges[2]],
        first_sum[: latnorm.shape[0], edges[5]],
        first_sum[:, edges[3] : edges[4]]
        .reshape(-1, kv_rows, kv_cols)
        .transpose(1, 0, 2)
        .reshape(keyval_w.shape),
        first_sum[:, edges[4] : edges[5]].T,
        first_sum[:, edges[5] + 1],
        first_sum[:, edges[2] : edges[3]],
        second_sum[:, :sh_cols],
        second_sum[:, sh_wide : sh_wide + sh_cols],
        second_sum[:, 2 * sh_wide : 2 * sh_wide + sh_cols].T,
        exgate_grad.swapaxes(1, 2),
        exup_grad.swapaxes(1, 2),
        exdown_grad,
    )


def solution(mesh):
    in_specs = (
        P("ep", None),
        P("ep", None),
        P("ep", None),
        P("ep", None),
        P("ep"),
        P("ep", "tp"),
        P("ep", None),
        P("ep"),
        P("ep", "tp"),
        P("tp", "ep"),
        P("ep"),
        P("ep", None),
        P("ep", "tp"),
        P("ep", "tp"),
        P("tp", "ep"),
        P("ep", None, "tp"),
        P("ep", None, "tp"),
        P("ep", "tp", None),
        P("ep", None),
    )
    out_specs = (
        P("ep", None),
        P("ep", None),
        P("ep"),
        P("ep", "tp"),
        P("ep", None),
        P("ep"),
        P("ep", "tp"),
        P("tp", "ep"),
        P("ep"),
        P("ep", None),
        P("ep", "tp"),
        P("ep", "tp"),
        P("tp", "ep"),
        P("ep", None, "tp"),
        P("ep", None, "tp"),
        P("ep", "tp", None),
    )
    return jax.shard_map(
        per_device, mesh=mesh, in_specs=in_specs, out_specs=out_specs, check_vma=False
    )
```

```python
import functools

import jax
import jax.numpy as jnp
from jax import lax
from jax.experimental import pallas as pl
from jax.experimental.pallas import tpu as pltpu
from jax.sharding import PartitionSpec as P

D = 2048
DN = 128
DR = 64
DV = 128
KVR = 512
TOPK = 6
EXP_DEV = 2
MAIN = 32

epsilon = 1e-06
route_scale = 2.446
rope_base = 50000.0
masked_fill = -1000000000.0

bf16 = jnp.bfloat16
f32 = jnp.float32


def matmul(left_mat, right_mat):
    return jnp.dot(left_mat, right_mat, preferred_element_type=f32)


def matmul_nt(left_mat, right_mat):
    return lax.dot_general(
        left_mat, right_mat, (((1,), (1,)), ((), ())), preferred_element_type=f32
    )


def matmul_tn(left_mat, right_mat):
    return lax.dot_general(
        left_mat, right_mat, (((0,), (0,)), ((), ())), preferred_element_type=f32
    )


def rms_scale(values):
    return lax.rsqrt(jnp.mean(values * values, -1, keepdims=True) + epsilon)


def rms_back(values, scale_vals, gain_vec, upstream):
    weighted = upstream * gain_vec
    inner_mean = jnp.mean(weighted * values, -1, keepdims=True)
    grad_in = scale_vals * weighted - values * scale_vals * scale_vals * scale_vals * inner_mean
    grad_gain = jnp.sum(upstream * values * scale_vals, 0)
    return (grad_in, grad_gain)


def rope_tables(row_count):
    half_dim = DR // 2
    freq_vec = rope_base ** (-(jnp.arange(half_dim, dtype=f32) * (2.0 / DR)))
    angle_tab = jnp.arange(row_count, dtype=f32)[:, None] * freq_vec[None, :]
    return (jnp.cos(angle_tab), jnp.sin(angle_tab))


def rotate(values, cos_tab, sine_tab):
    half_dim = values.shape[-1] // 2
    first_half = values[..., :half_dim]
    second_half = values[..., half_dim:]
    return jnp.concatenate(
        [
            first_half * cos_tab - second_half * sine_tab,
            second_half * cos_tab + first_half * sine_tab,
        ],
        -1,
    )


def shift(value, step):
    lanes = lax.axis_size("tp")
    return lax.ppermute(value, "tp", [(i, (i + step) % lanes) for i in range(lanes)])


def quarter_of(value, step):
    lanes = lax.axis_size("tp")
    width = value.shape[1] // lanes
    lane = lax.rem(lax.axis_index("tp") + step, lanes)
    return lax.dynamic_slice_in_dim(value, lane * width, width, 1)


def sum_to_quarter(partial):
    low = partial.astype(bf16)
    total = quarter_of(low, 0).astype(f32)
    for step in (1, 3, 2):
        total = total + shift(quarter_of(low, step), step).astype(f32)
    return total


def gather_quarters(piece):
    lanes = lax.axis_size("tp")
    lane = lax.axis_index("tp")
    parts = [piece] + [None] * (lanes - 1)
    for step in (1, 3, 2):
        parts[step] = shift(piece, lanes - step)
    full = jnp.concatenate(parts, 1)
    width = piece.shape[1]
    parts = []
    for step in range(lanes):
        at = lax.rem(lanes - lane + step, lanes) * width
        parts.append(lax.dynamic_slice_in_dim(full, at, width, 1))
    return jnp.concatenate(parts, 1)


def sum_small(partial):
    total = partial.astype(f32)
    for step in (1, 3, 2):
        total = total + shift(partial, step).astype(f32)
    return total


def exchange(value):
    return lax.all_to_all(value, "ep", 0, 0, tiled=True)


def to_experts(value):
    blocks = value.shape[0]
    rest = value.shape[2:]
    return jnp.concatenate(
        [
            value[:, :MAIN].reshape(blocks * MAIN, *rest),
            value[:, MAIN:-MAIN].reshape(-1, *rest),
            value[:, -MAIN:].reshape(blocks * MAIN, *rest),
        ],
        0,
    )


def from_experts(value, blocks):
    rest = value.shape[1:]
    edge = blocks * MAIN
    return jnp.concatenate(
        [
            value[:edge].reshape(blocks, MAIN, *rest),
            value[edge:-edge].reshape(blocks, -1, *rest),
            value[-edge:].reshape(blocks, MAIN, *rest),
        ],
        1,
    )


def after(value, *others):
    return lax.optimization_barrier((value, others))[0]


def plus(one, two):
    return (one.astype(f32) + two.astype(f32)).astype(bf16)


def ring_gather_first(one, two):
    return shift(one, 1), shift(two, 3), shift(two, 1), shift(one, 3)


def ring_gather_second(first):
    return shift(first[0], 1), shift(first[1], 3)


def ring_gather_parts(one, two, first, second):
    one_prev, two_next, two_prev, one_next = first
    return (one, two, one_next, two_next, second[0], second[1], one_prev, two_prev)


def add_three(one, two, three):
    return (one.astype(f32) + two.astype(f32) + three.astype(f32)).astype(bf16)


VMEM_BYTES = 44 * 1024 * 1024
SMALL_COST = pl.CostEstimate(flops=1, bytes_accessed=1, transcendentals=0)


def first_owner_rows(tiles, tile, spill):
    row = lax.broadcasted_iota(jnp.int32, (tile, 1), 0) + (pl.program_id(0) - tiles[0]) * tile
    return lax.rem(row, EXP_DEV * spill) < spill


def per_owner(tiles, tile, spill, run):
    first, mixed = tiles
    step = pl.program_id(0)
    mine = first_owner_rows(tiles, tile, spill)
    is_mixed = (step >= first) & (step < first + mixed)

    @pl.when(is_mixed)
    def _():
        run(None, mine)

    @pl.when(jnp.logical_not(is_mixed))
    def _():
        run(jnp.where(step < first, 0, 1), None)


def hidden_back_kernel(tiles, spill, *refs):
    value, weight, out = refs
    rows = value[...]

    def run(owner, mine):
        if owner is None:
            out[...] = jnp.where(mine, matmul_nt(rows, weight[0]), matmul_nt(rows, weight[1]))
        else:
            out[...] = matmul_nt(rows, weight[owner])

    per_owner(tiles, rows.shape[0], spill, run)


def hidden_kernel(tiles, spill, *refs):
    pieces, (weight, dh_ref, gate_ref, hid, dboth, dgate), refs = refs[:8], refs[8:14], refs[14:]
    drow, rows_out, acc = refs[:8], refs[8], refs[9]
    rows = jnp.concatenate([p[...] for p in pieces], 1)
    rows_out[...] = rows

    def run(owner, mine):
        if owner is None:
            acc[...] = jnp.where(mine, matmul(rows, weight[0]), matmul(rows, weight[1]))
        else:
            acc[...] = matmul(rows, weight[owner])

    per_owner(tiles, rows.shape[0], spill, run)
    wide = hid.shape[1]
    up = acc[:, wide:]
    pre = acc[:, :wide]
    sig = 1.0 / (1.0 + jnp.exp(-pre))
    act = pre * sig
    hidden = (act * up).astype(bf16).astype(f32)
    gate = gate_ref[...]
    dh = dh_ref[...]
    dgate[...] = jnp.sum(hidden * dh, 1, keepdims=True)
    hid[...] = (hidden * gate).astype(bf16)
    dh = dh * gate
    dboth[:, :wide] = (dh * up * (sig * (1.0 + pre * (1.0 - sig)))).astype(bf16)
    dboth[:, wide:] = (dh * act).astype(bf16)

    def back(owner, mine):
        grad = dboth[...]
        cols = drow[0].shape[1]
        none = jnp.zeros_like(grad)
        for j, out in enumerate(drow):
            at = slice(j * cols, (j + 1) * cols)
            if owner is None:
                total = matmul_nt(jnp.where(mine, grad, none), weight[0, at, :])
                total = total + matmul_nt(jnp.where(mine, none, grad), weight[1, at, :])
            else:
                total = matmul_nt(grad, weight[owner, at, :])
            out[...] = total.astype(bf16)

    per_owner(tiles, rows.shape[0], spill, back)


def out_kernel(tiles, spill, value, weight, out):
    def run(owner, mine):
        rows = value[...]
        none = jnp.zeros_like(rows)
        cols = out.shape[1] // 4
        for j in range(4):
            at = slice(j * cols, (j + 1) * cols)
            if owner is None:
                total = matmul(jnp.where(mine, rows, none), weight[0, :, at])
                total = total + matmul(jnp.where(mine, none, rows), weight[1, :, at])
            else:
                total = matmul(rows, weight[owner, :, at])
            out[:, at] = total.astype(bf16)

    per_owner(tiles, value.shape[0], spill, run)


def tile_spec(tile, width):
    return pl.BlockSpec((tile, width), lambda i: (i, 0))


def whole_spec(shape):
    return pl.BlockSpec(shape, lambda i: (0,) * len(shape))


def row_call(body, tile, total, ins, in_specs, outs, flops, scratch=()):
    out_shape = [jax.ShapeDtypeStruct((total, w), t) for w, t in outs]
    moved = sum(a.size * a.dtype.itemsize for a in (*ins, *out_shape))
    return pl.pallas_call(
        body,
        grid=(total // tile,),
        in_specs=in_specs,
        out_specs=[tile_spec(tile, w) for w, _ in outs],
        out_shape=out_shape,
        scratch_shapes=list(scratch),
        cost_estimate=SMALL_COST,
        compiler_params=pltpu.CompilerParams(
            dimension_semantics=("arbitrary",), vmem_limit_bytes=VMEM_BYTES
        ),
    )(*ins)


def first_grad_kernel(
    kv_rows,
    normed,
    normed2,
    dmid,
    dquery,
    dlat,
    dlogits,
    attended,
    latent_n,
    dkeyval,
    gains,
    out,
    kv_grad,
):
    step = pl.program_id(0)

    @pl.when(step == 0)
    def _():
        kv_grad[...] = matmul_tn(latent_n[...], dkeyval[...]).astype(bf16)

    rows, kv_cols = out.shape[0], 256
    at_lat = dquery.shape[1]
    at_kv = at_lat + dlat.shape[1]
    at_out = at_kv + kv_cols
    at_gain = at_out + attended.shape[1]
    mine = normed[...]
    out[:, :at_lat] = matmul_tn(mine, dquery[...]).astype(bf16)
    out[:, at_lat:at_kv] = (
        matmul_tn(mine, dlat[...]) + matmul_tn(normed2[...], dlogits[...])
    ).astype(bf16)
    out[:, at_out:at_gain] = matmul_tn(dmid[...], attended[...]).astype(bf16)
    out[:, at_gain:] = gains[...]
    splits = kv_grad.shape[1] // kv_cols
    count = rows // kv_rows
    for j in range(count):
        if count % splits == 0:
            group = step * (count // splits) + j // splits
            lanes = slice(j % splits * kv_cols, (j % splits + 1) * kv_cols)
        else:
            group = (step * count + j) // splits
            lanes = pl.ds((step * count + j) % splits * kv_cols, kv_cols)
        from_rows = pl.ds(pl.multiple_of(group * kv_rows, kv_rows), kv_rows)
        out[j * kv_rows : (j + 1) * kv_rows, at_kv:at_out] = kv_grad[from_rows, lanes]


def first_grads(kv_rows, normed, normed2, dmid, dquery, dlat, dlogits, attended, latent_n, dkeyval, gains):
    block = 256
    cols = pl.BlockSpec((normed.shape[0], block), lambda i: (0, i))
    width = dquery.shape[1] + dlat.shape[1] + 256 + attended.shape[1] + gains.shape[1]
    whole = (dquery, dlat, dlogits, attended, latent_n, dkeyval)
    return pl.pallas_call(
        functools.partial(first_grad_kernel, kv_rows),
        grid=(D // block,),
        in_specs=[cols, cols, cols]
        + [whole_spec(a.shape) for a in whole]
        + [tile_spec(block, gains.shape[1])],
        out_specs=tile_spec(block, width),
        out_shape=jax.ShapeDtypeStruct((D, width), bf16),
        scratch_shapes=[pltpu.VMEM((KVR, dkeyval.shape[1]), bf16)],
        cost_estimate=SMALL_COST,
        compiler_params=pltpu.CompilerParams(
            dimension_semantics=("arbitrary",), vmem_limit_bytes=VMEM_BYTES
        ),
    )(normed, normed2, dmid, *whole, gains)


def second_grad_kernel(normed2, cotangent, dboth, hidden, out):
    split = dboth.shape[1]
    out[:, :split] = matmul_tn(normed2[...], dboth[...]).astype(bf16)
    out[:, split:] = matmul_tn(cotangent[...], hidden[...]).astype(bf16)


def second_grads(normed2, cotangent, dboth, hidden):
    block = 256
    cols = pl.BlockSpec((normed2.shape[0], block), lambda i: (0, i))
    width = dboth.shape[1] + hidden.shape[1]
    return pl.pallas_call(
        second_grad_kernel,
        grid=(D // block,),
        in_specs=[cols, cols, whole_spec(dboth.shape), whole_spec(hidden.shape)],
        out_specs=tile_spec(block, width),
        out_shape=jax.ShapeDtypeStruct((D, width), bf16),
        cost_estimate=SMALL_COST,
        compiler_params=pltpu.CompilerParams(
            dimension_semantics=("arbitrary",), vmem_limit_bytes=VMEM_BYTES
        ),
    )(normed2, cotangent, dboth, hidden)


def weight_grad_kernel(edge, spill, lane, left, right, *refs):
    outs, kept = refs[:-1], refs[-1]
    span = kept.shape[2]
    owner = pl.program_id(1)

    @pl.when((pl.program_id(0) == 0) & (owner == 0))
    def _():
        row = lax.broadcasted_iota(jnp.int32, (span, 1), 0)
        first = (row < edge) | (lax.rem(jnp.maximum(row - edge, 0), EXP_DEV * spill) < spill)
        second = (row >= span - edge) | (lax.rem(row, EXP_DEV * spill) >= spill)
        for e, (at, keep) in enumerate(((0, first), (edge, second))):
            part = left[at : at + span, :].astype(f32)
            kept[e] = jnp.where(keep, part, 0.0).T.astype(bf16)

    at = pl.ds(pl.multiple_of(owner * edge, edge), span)
    total = matmul(kept[owner], right[at, :])
    wide = total.shape[0] // len(outs)
    for k, out in enumerate(outs):
        out[0] = total[k * wide : k * wide + out.shape[1]]


def weight_grads(edge, spill, hid_cols, count, lane, left, right):
    total, wide = left.shape
    span = total - edge
    block = D // 8
    grid_spec = pltpu.PrefetchScalarGridSpec(
        num_scalar_prefetch=1,
        grid=(8, EXP_DEV),
        in_specs=[
            pl.BlockSpec(left.shape, lambda j, e, lane: (0, 0)),
            pl.BlockSpec((total, block), lambda j, e, lane: (0, j)),
        ],
        out_specs=[
            pl.BlockSpec(
                (1, hid_cols, block), lambda j, e, lane: (e, 0, lax.rem(lane[0] * 2 + j, 8))
            )
        ]
        * count,
        scratch_shapes=[pltpu.VMEM((EXP_DEV, wide, span), bf16)],
    )
    return pl.pallas_call(
        functools.partial(weight_grad_kernel, edge, spill),
        grid_spec=grid_spec,
        out_shape=[jax.ShapeDtypeStruct((EXP_DEV, hid_cols, D), f32)] * count,
        cost_estimate=SMALL_COST,
        compiler_params=pltpu.CompilerParams(
            dimension_semantics=("arbitrary", "arbitrary"), vmem_limit_bytes=VMEM_BYTES
        ),
    )(lane.reshape(1), left, right)


def dense_kernel(blocks, spill, first, mixed, second, tab_first, tab_mixed, tab_second, out):
    tokens = out.shape[0] // blocks
    extra = EXP_DEV * spill * blocks
    lane = lax.broadcasted_iota(jnp.int32, (1, tokens), 1)
    owner = lax.broadcasted_iota(jnp.int32, (extra, 1), 0) // (EXP_DEV * spill)
    for i in range(blocks):
        at = slice(i * MAIN, (i + 1) * MAIN)
        hits = jnp.concatenate(
            [
                tab_first[at, :] == lane,
                (tab_mixed[...] == lane) & (owner == i),
                tab_second[at, :] == lane,
            ],
            0,
        )
        rows = jnp.concatenate([first[at, :], mixed[...], second[at, :]], 0)
        out[i * tokens : (i + 1) * tokens, :] = matmul_tn(
            hits.astype(f32).astype(bf16), rows
        ).astype(bf16)


def dense_rows(spill, owners, tokens, rows, table):
    blocks = 4
    edge = owners * MAIN
    extra = EXP_DEV * spill * blocks
    assert edge % extra == 0 and (edge + owners * EXP_DEV * spill) % (MAIN * blocks) == 0
    start = (edge + owners * EXP_DEV * spill) // (MAIN * blocks)

    def specs(width):
        return [
            pl.BlockSpec((MAIN * blocks, width), lambda g: (g, 0)),
            pl.BlockSpec((extra, width), lambda g: (edge // extra + g, 0)),
            pl.BlockSpec((MAIN * blocks, width), lambda g: (start + g, 0)),
        ]

    return pl.pallas_call(
        functools.partial(dense_kernel, blocks, spill),
        grid=(owners // blocks,),
        in_specs=specs(rows.shape[1]) + specs(1),
        out_specs=pl.BlockSpec((blocks * tokens, rows.shape[1]), lambda g: (g, 0)),
        out_shape=jax.ShapeDtypeStruct((owners * tokens, rows.shape[1]), bf16),
        cost_estimate=SMALL_COST,
        compiler_params=pltpu.CompilerParams(
            dimension_semantics=("arbitrary",), vmem_limit_bytes=VMEM_BYTES
        ),
    )(rows, rows, rows, table, table, table)


def shared_kernel(normed2, cotangent, weights, _, dboth, hidden, part, dnormed):
    wide = hidden.shape[1]
    gate_w, up_w, down_w = (weights.at[:, k * wide : (k + 1) * wide] for k in range(3))
    pre = matmul(normed2[...], gate_w[...])
    up = matmul(normed2[...], up_w[...])
    sig = 1.0 / (1.0 + jnp.exp(-pre))
    act = pre * sig
    hidden[...] = (act * up).astype(bf16)
    dh = matmul(cotangent[...], down_w[...])
    dboth[:, :wide] = (dh * up * (sig * (1.0 + pre * (1.0 - sig)))).astype(bf16)
    dboth[:, wide:] = (dh * act).astype(bf16)
    part[...] = matmul_nt(hidden[...], down_w[...]).astype(bf16)
    dnormed[...] = (
        matmul_nt(dboth[:, :wide], gate_w[...]) + matmul_nt(dboth[:, wide:], up_w[...])
    ).astype(bf16)


def shared_experts(normed2, cotangent, weights, signal):
    rows = normed2.shape[0]
    wide = weights.shape[1] // 3
    return pl.pallas_call(
        shared_kernel,
        out_shape=[jax.ShapeDtypeStruct((rows, w), bf16) for w in (2 * wide, wide, D, D)],
        cost_estimate=SMALL_COST,
        compiler_params=pltpu.CompilerParams(vmem_limit_bytes=VMEM_BYTES),
    )(normed2, cotangent, weights, signal)


def per_device(
    tokens,
    expert_ids,
    route_slots,
    doc_ids,
    prenorm,
    query_w,
    latent_w,
    latnorm,
    keyval_w,
    output_w,
    midnorm,
    router_w,
    shgate_w,
    shup_w,
    shdown_w,
    exgate_w,
    exup_w,
    exdown_w,
    cotangent,
):
    owner_count = lax.axis_size("ep")
    experts = owner_count * EXP_DEV
    tok_count = tokens.shape[0]
    capacity = 2 * tok_count * TOPK // experts
    spill = capacity - MAIN
    width = EXP_DEV * capacity
    slot_rows = owner_count * width
    head_count = query_w.shape[1] // (DN + DR)
    score_scale = (DN + DR) ** (-0.5)
    shard = query_w.shape[0]
    q_cols = query_w.shape[1]
    lat_cols = latent_w.shape[1]
    kv_rows = keyval_w.shape[0]
    kv_cols = kv_rows * keyval_w.shape[1] // shard
    out_cols = output_w.shape[0]
    sh_cols = shgate_w.shape[1]

    gains = jnp.stack(
        [prenorm, jnp.pad(latnorm, (0, shard - latnorm.shape[0])), midnorm], 1
    )
    gains = jnp.pad(gains, ((0, 0), (0, 128 - gains.shape[1])))
    first_pack = jnp.concatenate(
        [
            query_w,
            latent_w,
            router_w,
            keyval_w.reshape(kv_rows, -1, kv_cols).transpose(1, 0, 2).reshape(shard, kv_cols),
            output_w.T,
            gains,
        ],
        1,
    )
    first_full = lax.all_gather(first_pack, "ep", axis=0, tiled=True)
    local = expert_ids % EXP_DEV
    inside = jnp.where(
        route_slots < MAIN,
        local * (MAIN + EXP_DEV * spill) + route_slots,
        MAIN + local * spill + (route_slots - MAIN),
    )
    place = (expert_ids // EXP_DEV) * width + inside
    row_iota = lax.broadcasted_iota(jnp.int32, (slot_rows, tok_count), 0)
    matches = [row_iota == place[:, k][None, :] for k in range(TOPK)]
    pick = matches[0]
    for k in range(1, TOPK):
        pick = pick | matches[k]
    pick = pick.astype(bf16)

    token_iota = lax.broadcasted_iota(jnp.int32, (slot_rows, tok_count), 1)
    table = jnp.sum(jnp.where(pick > 0, token_iota + 1, 0), 1).astype(jnp.int32) - 1
    table = exchange(table.reshape(owner_count, width))
    row_table = to_experts(table)[:, None]
    half = D // 8
    lanes = lax.axis_size("tp")
    lane = lax.axis_index("tp")
    quarter = D // lanes
    hid_cols = exgate_w.shape[2]
    hid_wide = -(-hid_cols // 128) * 128

    def from_lane(value, axis):
        parts = []
        for step in range(lanes):
            at = lax.rem(lane + step, lanes) * quarter
            parts.append(lax.dynamic_slice_in_dim(value, at, quarter, axis))
        return jnp.concatenate(parts, axis)

    fill = hid_wide - hid_cols
    gateup_w = jnp.concatenate(
        [
            jnp.pad(from_lane(exgate_w, 1), ((0, 0), (0, 0), (0, fill))),
            jnp.pad(from_lane(exup_w, 1), ((0, 0), (0, 0), (0, fill))),
        ],
        2,
    )
    down_plain = jnp.pad(exdown_w, ((0, 0), (0, fill), (0, 0)))
    edge = owner_count * MAIN
    extra = slot_rows - 2 * edge
    span = edge + extra
    tile = 256 if edge % 256 == 0 else 128
    tiles = (edge // tile, extra // tile)
    big = 2 * (slot_rows + extra) * D * hid_wide
    first_full, table, row_table, gateup_w, down_plain = lax.optimization_barrier(
        (first_full, table, row_table, gateup_w, down_plain)
    )
    dy_all = lax.all_gather(after(cotangent, first_full), "ep", axis=0, tiled=True)
    edges = [0]
    for cols in (q_cols, lat_cols, experts, kv_cols, out_cols, 128):
        edges.append(edges[-1] + cols)
    query_full = first_full[:, edges[0] : edges[1]]
    latent_full = first_full[:, edges[1] : edges[2]]
    router_full = first_full[:, edges[2] : edges[3]]
    keyval_full = first_full[:, edges[3] : edges[4]].reshape(owner_count, -1, kv_rows, kv_cols)
    keyval_full = keyval_full.transpose(0, 2, 1, 3).reshape(KVR, keyval_w.shape[1])
    output_t = first_full[:, edges[4] : edges[5]]
    pre_gain = first_full[:, edges[5]]
    lat_gain = first_full[:, edges[5] + 1].reshape(owner_count, shard)[:, : latnorm.shape[0]]
    lat_gain = lat_gain.reshape(KVR)
    mid_gain = first_full[:, edges[5] + 2]


    resid_in = tokens.astype(f32)
    pre_scale = rms_scale(resid_in)
    pre_weight = pre_gain.astype(f32)
    normed = (resid_in * pre_scale * pre_weight).astype(bf16)
    query_raw = matmul(normed, query_full).reshape(tok_count, head_count, DN + DR)
    latent_all = matmul(normed, latent_full)
    latent = latent_all[:, :KVR]
    lat_scale = rms_scale(latent)
    lat_weight = lat_gain.astype(f32)
    latent_n = (latent * lat_scale * lat_weight).astype(bf16)
    keyval = matmul(latent_n, keyval_full).astype(bf16).reshape(tok_count, head_count, DN + DV)
    cos_tab, sine_tab = rope_tables(tok_count)
    q_all = jnp.concatenate(
        [
            query_raw[..., :DN],
            rotate(query_raw[..., DN:], cos_tab[:, None, :], sine_tab[:, None, :]),
        ],
        -1,
    ).astype(bf16)
    key_rot = rotate(latent_all[:, KVR:], cos_tab, sine_tab).astype(bf16)
    key_all = jnp.concatenate(
        [keyval[..., :DN], jnp.broadcast_to(key_rot[:, None, :], (tok_count, head_count, DR))], -1
    )
    values = keyval[..., DN:]
    position = jnp.arange(tok_count)
    doc_row = doc_ids[0]
    allowed = ((doc_row[:, None] == doc_row[None, :]) & (position[:, None] >= position[None, :]))[
        None
    ]
    raw_scores = (
        jnp.einsum("thd,shd->hts", q_all, key_all, preferred_element_type=f32) * score_scale
    )
    masked = jnp.where(allowed, raw_scores, masked_fill)
    row_max = jnp.max(masked, -1, keepdims=True)
    exp_scores = jnp.exp(masked - row_max)
    softmax_sum = jnp.sum(exp_scores, -1, keepdims=True)
    probs = exp_scores / softmax_sum
    probs16 = probs.astype(bf16)
    attended = jnp.einsum("hts,shd->thd", probs16, values, preferred_element_type=f32)
    attended = attended.reshape(tok_count, head_count * DV).astype(bf16)
    attn_sum = gather_quarters(sum_to_quarter(matmul_nt(attended, output_t)).astype(bf16))
    mid_resid = resid_in + attn_sum.astype(f32)
    mid_scale = rms_scale(mid_resid)
    mid_weight = mid_gain.astype(f32)
    normed2 = (mid_resid * mid_scale * mid_weight).astype(bf16)

    sent = matmul(pick, quarter_of(normed2, 0)).astype(bf16).reshape(owner_count, width, -1)
    one = exchange(sent[:, :, :half])
    two = exchange(after(sent[:, :, half:], one))
    sh_wide = -(-sh_cols // 128) * 128
    second_pack = jnp.concatenate(
        [
            jnp.pad(w, ((0, 0), (0, sh_wide - sh_cols)))
            for w in (shgate_w, shup_w, shdown_w.T)
        ],
        1,
    )
    second_full = lax.all_gather(after(second_pack, dy_all, one), "ep", axis=0, tiled=True)
    own = (to_experts(one), to_experts(two))
    first = ring_gather_first(*own)
    pick_in = (
        table[:, :, None] == lax.broadcasted_iota(jnp.int32, (owner_count, width, tok_count), 2)
    ).astype(bf16)
    dy_rows = jnp.einsum(
        "ist,itd->isd",
        pick_in,
        after(dy_all, two).reshape(owner_count, tok_count, D),
        preferred_element_type=f32,
    )
    dy_rows = to_experts(dy_rows.astype(bf16))
    logits = matmul(normed2, router_full)
    onehot = (
        expert_ids[:, :, None] == jnp.arange(experts, dtype=jnp.int32)[None, None, :]
    ).astype(f32)
    chosen = jnp.sum(onehot * logits[:, None, :], -1)
    sel_vals = 1.0 / (1.0 + jnp.exp(-chosen))
    sel_total = jnp.sum(sel_vals, -1, keepdims=True)
    gate_vals = route_scale * sel_vals / sel_total
    gate_rows = jnp.zeros((slot_rows, tok_count), f32)
    for k in range(TOPK):
        gate_rows = gate_rows + jnp.where(matches[k], gate_vals[:, k][None, :], 0.0)
    gate_rows = jnp.sum(gate_rows, 1).reshape(owner_count, width)
    gate_rows = to_experts(exchange(after(gate_rows, two)))[:, None]

    going, dy_rows, gate_rows = lax.optimization_barrier((first, dy_rows, gate_rows))
    rows = ring_gather_parts(*own, going, ring_gather_second(going))
    (ex_dh,) = row_call(
        functools.partial(hidden_back_kernel, tiles, spill),
        tile,
        slot_rows,
        (dy_rows, down_plain),
        [tile_spec(tile, D), whole_spec(down_plain.shape)],
        [(hid_wide, f32)],
        big,
    )
    upstream = cotangent.astype(f32)
    sh_dboth, sh_hidden, shared_part, sh_dnormed_part = shared_experts(
        normed2, cotangent, second_full, going[0][:16, :128]
    )
    second_grad = second_grads(normed2, cotangent, sh_dboth, sh_hidden)
    second_sum = lax.psum_scatter(second_grad, "ep", scatter_dimension=0, tiled=True)

    ex_dh, shared_part, sh_dnormed_part, second_grad = lax.optimization_barrier(
        (ex_dh, shared_part, sh_dnormed_part, second_grad)
    )
    ex_hidden, ex_dboth, dgate_rows, *drow, all_rows = row_call(
        functools.partial(hidden_kernel, tiles, spill),
        tile,
        slot_rows,
        (*rows, gateup_w, ex_dh, gate_rows),
        [tile_spec(tile, half)] * 8
        + [whole_spec(gateup_w.shape), tile_spec(tile, hid_wide), tile_spec(tile, 1)],
        [(hid_wide, bf16), (2 * hid_wide, bf16), (1, f32)] + [(half, bf16)] * 8 + [(D, bf16)],
        4 * big,
        [pltpu.VMEM((tile, 2 * hid_wide), f32)],
    )

    (out_rows,) = row_call(
        functools.partial(out_kernel, tiles, spill),
        tile,
        slot_rows,
        (ex_hidden, down_plain),
        [tile_spec(tile, hid_wide), whole_spec(down_plain.shape)],
        [(D, bf16)],
        big,
    )
    top = shift(drow[4], 1)
    bottom = shift(drow[5], 3)
    out_dense = dense_rows(spill, owner_count, tok_count, out_rows, row_table)
    top, bottom, out_dense, dgate_rows = lax.optimization_barrier(
        (top, bottom, out_dense, dgate_rows)
    )
    from_prev_one = shift(plus(drow[2], top), 1)
    from_next_one = shift(after(drow[6], bottom), 3)
    dgate_rows = exchange(from_experts(dgate_rows[:, 0], owner_count)).reshape(-1)
    (next_two, prev_two), dgate_rows, _, _ = lax.optimization_barrier(
        (
            (drow[3], plus(drow[7], bottom)),
            dgate_rows,
            from_prev_one,
            from_next_one,
        )
    )
    from_prev_two = shift(next_two, 1)
    from_next_two = shift(prev_two, 3)
    drow_one = add_three(drow[0], from_prev_one, from_next_one)
    drow_two = add_three(drow[1], from_prev_two, from_next_two)
    back_one = exchange(from_experts(drow_one, owner_count))
    back_two = exchange(from_experts(drow_two, owner_count))
    routed_grad_q = jnp.concatenate(
        [matmul_tn(pick, b.reshape(slot_rows, -1)) for b in (back_one, back_two)], 1
    )
    out_sum = lax.psum_scatter(
        after(out_dense, second_sum), "ep", scatter_dimension=0, tiled=True
    )

    dgate_part = jnp.stack(
        [jnp.sum(jnp.where(matches[k], dgate_rows[:, None], 0.0), 0) for k in range(TOPK)], 1
    )
    dgate_part, sh_dnormed_part = after((dgate_part, sh_dnormed_part), drow_two)
    sh_dnormed_q = sum_to_quarter(sh_dnormed_part)
    dgate_all = sum_small(dgate_part)
    weighted = jnp.sum(dgate_all * gate_vals, -1, keepdims=True) / route_scale
    dsel_vals = route_scale / sel_total * (dgate_all - weighted)
    dchosen = dsel_vals * sel_vals * (1.0 - sel_vals)
    dlogits = jnp.sum(onehot * dchosen[:, :, None], 1).astype(bf16)
    dnormed2 = gather_quarters((routed_grad_q + sh_dnormed_q).astype(bf16)).astype(f32)
    dnormed2 = dnormed2 + matmul_nt(dlogits, router_full)
    dmid_norm, midnorm_grad = rms_back(mid_resid, mid_scale, mid_weight, dnormed2)
    dmid = upstream + dmid_norm
    dmid16 = dmid.astype(bf16)
    dattended = matmul(dmid16, output_t).astype(bf16).reshape(tok_count, head_count, DV)
    dprobs = jnp.einsum("thd,shd->hts", dattended, values, preferred_element_type=f32)
    dscores = (probs * (dprobs - jnp.sum(probs * dprobs, -1, keepdims=True))).astype(bf16)
    dq_all = (
        jnp.einsum("hts,shd->thd", dscores, key_all, preferred_element_type=f32) * score_scale
    )
    dkey_all = jnp.einsum("hts,thd->shd", dscores, q_all, preferred_element_type=f32) * score_scale
    dvalues = jnp.einsum("hts,thd->shd", probs16, dattended, preferred_element_type=f32)
    dquery = jnp.concatenate(
        [dq_all[..., :DN], rotate(dq_all[..., DN:], cos_tab[:, None, :], -sine_tab[:, None, :])], -1
    )
    dquery = dquery.reshape(tok_count, head_count * (DN + DR)).astype(bf16)
    dkeyval = (
        jnp.concatenate([dkey_all[..., :DN], dvalues], -1)
        .reshape(tok_count, head_count * (DN + DV))
        .astype(bf16)
    )
    dlatent_part = matmul_nt(dkeyval, keyval_full)
    dkey_part = jnp.sum(dkey_all[..., DN:], 1)
    dlat_part = jnp.concatenate([dlatent_part, dkey_part], 1).astype(bf16)
    dlat_sum = sum_small(dlat_part)
    dlatent, latnorm_grad = rms_back(latent, lat_scale, lat_weight, dlat_sum[:, :KVR])
    dlatent_all = jnp.concatenate(
        [dlatent, rotate(dlat_sum[:, KVR:], cos_tab, -sine_tab)], -1
    ).astype(bf16)
    gain_grads = jnp.stack(
        [
            jnp.pad(
                latnorm_grad.reshape(owner_count, -1),
                ((0, 0), (0, shard - latnorm.shape[0])),
            ).reshape(-1),
            midnorm_grad,
        ],
        1,
    )
    gain_grads = jnp.pad(gain_grads, ((0, 0), (0, 128 - gain_grads.shape[1])))
    first_grad = first_grads(
        kv_rows,
        normed,
        normed2,
        dmid16,
        dquery,
        jnp.pad(dlatent_all, ((0, 0), (0, experts))),
        jnp.pad(dlogits, ((0, 0), (lat_cols, 0))),
        attended,
        latent_n,
        dkeyval,
        after(gain_grads.astype(bf16), out_sum),
    )
    late = shift(first_grad[:16, :128], 1)
    out_part = after(out_sum, late).astype(f32) + shared_part.astype(f32)
    out_q = sum_to_quarter(out_part)
    late_dquery, late_dlat = after((dquery, dlatent_all), late)
    dnormed_q = sum_to_quarter(matmul_nt(late_dquery, query_full))
    dnormed = gather_quarters(dnormed_q.astype(bf16)).astype(f32) + matmul_nt(
        late_dlat, latent_full
    )
    dtokens, prenorm_grad = rms_back(resid_in, pre_scale, pre_weight, dnormed)
    tokens_grad = (dmid + dtokens).astype(bf16)
    prenorm_sum = jnp.sum(exchange(prenorm_grad.reshape(owner_count, shard)), 0)
    exgate_grad, exup_grad = weight_grads(
        edge, spill, hid_cols, 2, lane, *after((ex_dboth, all_rows), late)
    )
    (exdown_grad,) = weight_grads(
        edge, spill, hid_cols, 1, jnp.zeros_like(lane), *after((ex_hidden, dy_rows), late)
    )
    layer_q = (quarter_of(mid_resid, 0) + out_q).astype(bf16)
    layer_out = gather_quarters(layer_q)
    first_sum = lax.psum_scatter(first_grad, "ep", scatter_dimension=0, tiled=True).astype(f32)
    second_sum = second_sum.astype(f32)
    return (
        layer_out,
        tokens_grad,
        prenorm_sum,
        first_sum[:, edges[0] : edges[1]],
        first_sum[:, edges[1] : edges[2]],
        first_sum[: latnorm.shape[0], edges[5]],
        first_sum[:, edges[3] : edges[4]]
        .reshape(-1, kv_rows, kv_cols)
        .transpose(1, 0, 2)
        .reshape(keyval_w.shape),
        first_sum[:, edges[4] : edges[5]].T,
        first_sum[:, edges[5] + 1],
        first_sum[:, edges[2] : edges[3]],
        second_sum[:, :sh_cols],
        second_sum[:, sh_wide : sh_wide + sh_cols],
        second_sum[:, 2 * sh_wide : 2 * sh_wide + sh_cols].T,
        exgate_grad.swapaxes(1, 2),
        exup_grad.swapaxes(1, 2),
        exdown_grad,
    )


def solution(mesh):
    in_specs = (
        P("ep", None),
        P("ep", None),
        P("ep", None),
        P("ep", None),
        P("ep"),
        P("ep", "tp"),
        P("ep", None),
        P("ep"),
        P("ep", "tp"),
        P("tp", "ep"),
        P("ep"),
        P("ep", None),
        P("ep", "tp"),
        P("ep", "tp"),
        P("tp", "ep"),
        P("ep", None, "tp"),
        P("ep", None, "tp"),
        P("ep", "tp", None),
        P("ep", None),
    )
    out_specs = (
        P("ep", None),
        P("ep", None),
        P("ep"),
        P("ep", "tp"),
        P("ep", None),
        P("ep"),
        P("ep", "tp"),
        P("tp", "ep"),
        P("ep"),
        P("ep", None),
        P("ep", "tp"),
        P("ep", "tp"),
        P("tp", "ep"),
        P("ep", None, "tp"),
        P("ep", None, "tp"),
        P("ep", "tp", None),
    )
    return jax.shard_map(
        per_device, mesh=mesh, in_specs=in_specs, out_specs=out_specs, check_vma=False
    )
```
